32 devices in a mesh: batch: 4 (over z), blk: 4 (over y, x), tensor: 2 (over core).
Axes of the slice: x: 2, y: 2, z: 4, core: 2. Of those that a mesh axis runs over, the one named last changes fastest.
Arguments:
- layer_in: bfloat16 [16384, 896], P(('batch', 'blk', 'tensor')), may hold values from -6 to 6
- cotangent: bfloat16 [16384, 896], P(('batch', 'blk', 'tensor')), may hold values from -6 to 6
- lengths: int32 [4, 1], P('batch'), may hold values from 2048 to 4096, as said below
- attn_gain: float32 [896], replicated, may hold values from 0.5 to 1.5
- w_query: bfloat16 [896, 896], P(None, 'tensor'), may hold values from -0.1875 to 0.1875
- query_bias: bfloat16 [896], P('tensor'), may hold values from -3 to 3
- w_key: bfloat16 [896, 128], P(None, 'tensor'), may hold values from -0.1875 to 0.1875
- key_bias: bfloat16 [128], P('tensor'), may hold values from -3 to 3
- w_value: bfloat16 [896, 128], P(None, 'tensor'), may hold values from -0.1875 to 0.1875
- value_bias: bfloat16 [128], P('tensor'), may hold values from -0.59765625 to 0.59765625
- w_out: bfloat16 [896, 896], P('tensor'), may hold values from -1.5 to 1.5
- mlp_gain: float32 [896], replicated, may hold values from 0.5 to 1.5
- w_gate: bfloat16 [896, 4864], P(None, 'tensor'), may hold values from -0.1875 to 0.1875
- w_up: bfloat16 [896, 4864], P(None, 'tensor'), may hold values from -0.1875 to 0.1875
- w_down: bfloat16 [4864, 896], P('tensor'), may hold values from -0.078125 to 0.078125
Outputs:
- layer_out: bfloat16 [16384, 896], P(('batch', 'blk', 'tensor'))
- input_grad: bfloat16 [16384, 896], P(('batch', 'blk', 'tensor'))
- grad_attn_gain: float32 [896], replicated
- grad_query: float32 [896, 896], P(None, 'tensor')
- grad_query_bias: float32 [896], P('tensor')
- grad_key: float32 [896, 128], P(None, 'tensor')
- grad_key_bias: float32 [128], P('tensor')
- grad_value: float32 [896, 128], P(None, 'tensor')
- grad_value_bias: float32 [128], P('tensor')
- grad_out: float32 [896, 896], P('tensor')
- grad_mlp_gain: float32 [896], replicated
- grad_gate: float32 [896, 4864], P(None, 'tensor')
- grad_up: float32 [896, 4864], P(None, 'tensor')
- grad_down: float32 [4864, 896], P('tensor')
The draws below stay inside these ranges and needn't reach their ends.
Inputs may be any that keep to these rules, and one draw needn't show every extreme that they name: `lengths`: row g gives, for the single bucket of 4096 positions of batch group g, the length of the one sequence that starts at the bucket's first position; the rest of the bucket is padding. In every draw some bucket is full and some holds exactly half of 4096.
All inputs are finite; a program needn't handle non-finite values.
Results may differ from the reference program's by a relative error of at most 0.03.
Values may be sent and summed in bfloat16 or wider, within the bound.
A program may use at most 192 MiB of HBM per device.

```python
from functools import partial
import jax
import jax.numpy as jnp
from jax import lax

D = 896
HEADS = 14
KV_HEADS = 2
HEAD = 64
FF = 4864
TOKENS = 16384
BUCKET = 4096
BUCKETS = 1
N_BATCH = 4


def draw_lengths(key, part):
    first, second = jax.random.split(jax.random.fold_in(key, 11))
    total = N_BATCH * BUCKETS
    values = jax.random.randint(first, (total,), BUCKET // 2, BUCKET + 1, dtype=jnp.int32)
    order = jax.random.permutation(second, total)
    values = values.at[order[0]].set(BUCKET)
    values = values.at[order[1]].set(BUCKET // 2)
    return values.reshape(N_BATCH, BUCKETS)


def block_scale(key, shape, cuts, low, top_value):
    level = 1.0
    for dim, blocks in cuts:
        heights = jax.random.uniform(jax.random.fold_in(jax.random.fold_in(key, 6), dim), (blocks,), jnp.float32, low / len(cuts), top_value / len(cuts))
        level = level * jnp.repeat(jnp.exp(heights), shape[dim] // blocks).reshape((-1,) + (1,) * (len(shape) - 1 - dim))
    return level


def bell_draw(own_key, extent, deviation, most, cuts=(), kind=jnp.bfloat16):
    drawn = deviation * jax.random.normal(own_key, extent, jnp.float32)
    if cuts:
        drawn = drawn * block_scale(own_key, extent, cuts, -0.22, 0.18)
    return jnp.clip(drawn, -most, most).astype(kind)


def setup_inputs(seed: int = 0) -> dict:
    streams_of = jax.random.split(jax.random.key(seed), 16)
    layer_in = bell_draw(streams_of[0], (TOKENS, D), 1.0, 6.0, ((0, 32),))
    cotangent = bell_draw(streams_of[1], (TOKENS, D), 1.0, 6.0, ((0, 32),))
    lengths = draw_lengths(jax.random.fold_in(streams_of[15], 71), 0)
    attn_gain = jnp.clip(1.0 + 0.1 * jax.random.normal(streams_of[3], (D,), jnp.float32), 0.5, 1.5)
    w_query = bell_draw(streams_of[4], (D, HEADS * HEAD), D ** -0.5, 0.1875, ((1, 2),))
    query_bias = bell_draw(streams_of[5], (HEADS * HEAD,), 0.5, 3.0, ((0, 2),))
    w_key = bell_draw(streams_of[6], (D, KV_HEADS * HEAD), D ** -0.5, 0.1875, ((1, 2),))
    key_bias = bell_draw(streams_of[7], (KV_HEADS * HEAD,), 0.5, 3.0, ((0, 2),))
    w_value = bell_draw(streams_of[8], (D, KV_HEADS * HEAD), D ** -0.5, 0.1875, ((1, 2),))
    value_bias = bell_draw(streams_of[9], (KV_HEADS * HEAD,), 0.1, 0.59765625, ((0, 2),))
    w_out = bell_draw(streams_of[10], (HEADS * HEAD, D), (HEADS * HEAD // 64) ** -0.5, 1.5, ((0, 2),))
    mlp_gain = jnp.clip(1.0 + 0.1 * jax.random.normal(streams_of[11], (D,), jnp.float32), 0.5, 1.5)
    w_gate = bell_draw(streams_of[12], (D, FF), D ** -0.5, 0.1875, ((1, 2),))
    w_up = bell_draw(streams_of[13], (D, FF), D ** -0.5, 0.1875, ((1, 2),))
    w_down = bell_draw(streams_of[14], (FF, D), FF ** -0.5, 0.078125, ((0, 2),))
    return dict(layer_in=layer_in, cotangent=cotangent, lengths=lengths, attn_gain=attn_gain, w_query=w_query, query_bias=query_bias, w_key=w_key, key_bias=key_bias, w_value=w_value, value_bias=value_bias, w_out=w_out, mlp_gain=mlp_gain, w_gate=w_gate, w_up=w_up, w_down=w_down)


@jax.custom_vjp
def low(v):
    return lax.optimization_barrier(v.astype(jnp.bfloat16)).astype(jnp.float32)

@jax.custom_vjp
def low_back(v):
    return v

def low_keep(v):
    return (low(v), None)

def low_pass(kept, grad):
    return (grad,)

def back_keep(v):
    return (v, None)

def back_low(kept, grad):
    return (low(grad),)
low.defvjp(low_keep, low_pass)
low_back.defvjp(back_keep, back_low)
rope_base = 1000000.0
norm_eps = 1e-06

def product(left, right):
    return jnp.dot(left, right, precision=lax.Precision.HIGHEST, preferred_element_type=jnp.float32)

def rms_scale(values):
    return lax.rsqrt(lax.optimization_barrier(jnp.mean(values * values, axis=-1, keepdims=True)) + norm_eps)

def rotary_tables(positions, width):
    freq = rope_base ** (-(jnp.arange(width // 2, dtype=jnp.float32) * 2.0) / width)
    phase = positions.astype(jnp.float32)[:, None] * freq[None, :]
    return (jnp.cos(phase)[:, None, :], jnp.sin(phase)[:, None, :])

def rotate(values, cosine, sine):
    half = values.shape[-1] // 2
    first = values[..., :half]
    second = values[..., half:]
    return jnp.concatenate([first * cosine - second * sine, second * cosine + first * sine], axis=-1)

def bucket_attention(item):
    query, keys, values, length = item
    group_size = HEADS // KV_HEADS
    keys = jnp.repeat(keys, group_size, axis=1)
    values = jnp.repeat(values, group_size, axis=1)
    raw = jnp.einsum('qhd,khd->hqk', query, keys, precision=lax.Precision.HIGHEST) * HEAD ** (-0.5)
    scores = low_back(raw)
    index = jnp.arange(BUCKET, dtype=jnp.int32)
    allowed = (index[None, :] <= index[:, None]) & (index[None, :] < length)
    masked = jnp.where(allowed[None], scores, -1e+30)
    top = lax.optimization_barrier(jnp.max(masked, axis=-1, keepdims=True))
    weights = jnp.where(allowed[None], jnp.exp(masked - top), 0.0)
    probs = low(weights / lax.optimization_barrier(jnp.sum(weights, axis=-1, keepdims=True)))
    return jnp.einsum('hqk,khd->qhd', probs, values, precision=lax.Precision.HIGHEST)

def forward(lengths, layer_in, attn_gain, w_query, query_bias, w_key, key_bias, w_value, value_bias, w_out, mlp_gain, w_gate, w_up, w_down):
    positions = jnp.arange(TOKENS, dtype=jnp.int32) % BUCKET
    cosine, sine = rotary_tables(positions, HEAD)
    normed_in = low(layer_in * rms_scale(layer_in) * attn_gain)
    query = low_back(product(normed_in, w_query) + query_bias).reshape(TOKENS, HEADS, HEAD)
    keys = low_back(product(normed_in, w_key) + key_bias).reshape(TOKENS, KV_HEADS, HEAD)
    values = low(low_back(product(normed_in, w_value) + value_bias)).reshape(TOKENS, KV_HEADS, HEAD)
    query_rot = low(rotate(query, cosine, sine))
    key_rot = low(rotate(keys, cosine, sine))
    bucket_count = TOKENS // BUCKET
    context = lax.map(jax.checkpoint(bucket_attention), (query_rot.reshape(bucket_count, BUCKET, HEADS, HEAD), key_rot.reshape(bucket_count, BUCKET, KV_HEADS, HEAD), values.reshape(bucket_count, BUCKET, KV_HEADS, HEAD), lengths.reshape(-1)))
    context = low(low_back(context.reshape(TOKENS, HEADS * HEAD)))
    resid = layer_in + low_back(product(context, w_out))
    mlp_in = low(resid * rms_scale(resid) * mlp_gain)
    gate = low_back(product(mlp_in, w_gate))
    upper = low_back(product(mlp_in, w_up))
    hidden = low(gate / (1.0 + jnp.exp(-gate)) * upper)
    return resid + product(hidden, w_down)

def reference(layer_in, cotangent, lengths, attn_gain, w_query, query_bias, w_key, key_bias, w_value, value_bias, w_out, mlp_gain, w_gate, w_up, w_down):
    params = tuple((item.astype(jnp.float32) for item in (layer_in, attn_gain, w_query, query_bias, w_key, key_bias, w_value, value_bias, w_out, mlp_gain, w_gate, w_up, w_down)))
    result, pullback = jax.vjp(partial(forward, lengths), *params)
    index = jnp.arange(TOKENS, dtype=jnp.int32)
    live = index % BUCKET < lengths.reshape(-1)[index // BUCKET]
    masked_cot = cotangent.astype(jnp.float32) * live[:, None].astype(jnp.float32)
    grads = pullback(masked_cot)
    return (result.astype(jnp.bfloat16), grads[0].astype(jnp.bfloat16), grads[1], grads[2], grads[3], grads[4], grads[5], grads[6], grads[7], grads[8], grads[9], grads[10], grads[11], grads[12])
```

```python
import functools
import math

import jax
import jax.numpy as jnp
from jax import lax
from jax.experimental import pallas as pl
from jax.experimental.pallas import tpu as pltpu
from jax.sharding import PartitionSpec as P

HEAD = 64
SLOT = 128

rope_base = 1000000.0
norm_eps = 1e-06
masked_value = -1e30
bf16 = jnp.bfloat16
f32 = jnp.float32


def dot(left, right, dims, kind=f32):
    return lax.dot_general(left, right, (dims, ((), ())), preferred_element_type=kind)


NN = ((1,), (0,))
NT = ((1,), (1,))
TN = ((0,), (0,))


def contract_rows(left, right, kind=f32):
    return dot(left, right, TN, kind)


def contract_cols(left, right, kind=f32):
    return dot(left, right, NT, kind)


def norm_back(grad, normed, scale, gain):
    weighted = grad * gain
    return scale * (weighted - normed * jnp.mean(weighted * normed, axis=1, keepdims=True))


def partner(value, axis, bit):
    n = lax.axis_size(axis)
    return lax.ppermute(value, axis, [(i, i ^ (1 << bit)) for i in range(n)])


def bits_of(axis):
    return [(axis, bit) for bit in range(int(math.log2(lax.axis_size(axis))))]


def my_bit(axis, bit):
    return (lax.axis_index(axis) >> bit) & 1


def in_order(own, other, axis, bit):
    first = my_bit(axis, bit) == 0
    return jnp.where(
        first, jnp.concatenate([own, other], 0), jnp.concatenate([other, own], 0)
    )


def gather_pair(own, axis, bit):
    return in_order(own, partner(own, axis, bit), axis, bit)


def scatter_pair(value, axis, bit):
    half = value.shape[0] // 2
    mine = my_bit(axis, bit)
    keep = lax.dynamic_slice_in_dim(value, mine * half, half, 0)
    send = lax.dynamic_slice_in_dim(value, (1 - mine) * half, half, 0)
    got = partner(send, axis, bit)
    return (keep.astype(f32) + got.astype(f32)).astype(bf16)


def add_pair(value, axis, bit):
    got = partner(value, axis, bit)
    return (value.astype(f32) + got.astype(f32)).astype(bf16)


def reduce_all(value, steps):
    halved = []
    for axis, bit in steps:
        if value.shape[0] % 16 == 0:
            value = scatter_pair(value, axis, bit)
            halved.append((axis, bit))
        else:
            value = add_pair(value, axis, bit)
    for axis, bit in reversed(halved):
        value = gather_pair(value, axis, bit)
    return value


def reduce_grad(value):
    half = value.shape[0] // 2
    plane, line = bits_of("blk"), bits_of("batch")
    first = reduce_all(value[:half], plane + line)
    second = reduce_all(value[half:], plane[::-1] + line)
    return jnp.concatenate([first, second], 0).astype(f32)


def attn_fwd_kernel(
    heads, rows, info, q_ref, kv_ref, ctx_ref, slots_ref, lse_ref, k1, v1, q1, m_s, acc_s
):
    tq, tk = 256, 512
    blk, length = info[0], info[1]
    total = kv_ref.shape[0]
    lane = lax.broadcasted_iota(jnp.int32, (tk, SLOT), 1)
    row = lax.broadcasted_iota(jnp.int32, (tk, SLOT), 0)

    def prepare(i, _):
        at = pl.ds(i * tk, tk)
        kv = kv_ref[at, :].astype(f32)
        dead = jnp.where(row + i * tk < length, 0.0, masked_value)
        k1[at, :] = jnp.where(lane < HEAD, kv, jnp.where(lane == HEAD, dead, 0.0)).astype(bf16)
        v1[at, :] = jnp.where(lane < HEAD, 1.0, kv).astype(bf16)
        return 0

    lax.fori_loop(0, (blk + 1) * (rows // tk), prepare, 0)
    one = jnp.where(lax.broadcasted_iota(jnp.int32, (tq, SLOT), 1) == HEAD, 1.0, 0.0)

    def tile(at, masked):
        kt = k1[at, :]
        vt = v1[at, :]
        for h in range(heads):
            s = dot(q1[:, h * SLOT : (h + 1) * SLOT], kt, NT)
            if masked is not None:
                s = jnp.where(masked, s, masked_value)
            m_prev = m_s[h]
            m_new = jnp.maximum(m_prev, jnp.max(s, axis=1, keepdims=True))
            alpha = jnp.exp(m_prev - m_new)
            p = jnp.exp(s - jnp.concatenate([m_new] * (tk // SLOT), 1))
            acc_s[h] = acc_s[h] * alpha + dot(p.astype(bf16), vt, NN)
            m_s[h] = m_new

    def query_tile(qt, _):
        at_q = pl.ds(qt * tq, tq)
        for h in range(heads):
            cols = slice(h * SLOT, (h + 1) * SLOT)
            q1[:, cols] = (q_ref[at_q, cols].astype(f32) + one).astype(bf16)
        m_s[...] = jnp.full(m_s.shape, masked_value, f32)
        acc_s[...] = jnp.zeros(acc_s.shape, f32)
        full = blk * (rows // tk) + (qt * tq) // tk

        def full_tile(i, _):
            tile(pl.ds(pl.multiple_of(i * tk, tk), tk), None)
            return 0

        lax.fori_loop(0, full, full_tile, 0)
        shift = (qt * tq) % tk
        ri = lax.broadcasted_iota(jnp.int32, (tq, tk), 0) + shift
        ci = lax.broadcasted_iota(jnp.int32, (tq, tk), 1)
        tile(pl.ds(pl.multiple_of(full * tk, tk), tk), ci <= ri)
        pos = lax.broadcasted_iota(jnp.int32, (1, tq), 1) + blk * rows + qt * tq
        for h in range(heads):
            acc = acc_s[h]
            out = acc / pltpu.roll(acc, HEAD, 1)
            wide = jnp.where(lax.broadcasted_iota(jnp.int32, (tq, SLOT), 1) < HEAD, 0.0, out)
            slots_ref[at_q, h * SLOT : (h + 1) * SLOT] = wide.astype(bf16)
            ctx_ref[at_q, h * HEAD : (h + 1) * HEAD] = wide[:, HEAD:].astype(bf16)
            lse = jnp.transpose(m_s[h] + jnp.log(acc))[0:1, :]
            lse_ref[h : h + 1, pl.ds(pl.multiple_of(qt * tq, tq), tq)] = jnp.where(
                pos < length, lse, -masked_value
            )
        return 0

    lax.fori_loop(0, rows // tq, query_tile, 0)


def attn_fwd(info, q, kv, heads):
    rows = q.shape[0]
    vm = pl.BlockSpec(memory_space=pltpu.VMEM)
    return pl.pallas_call(
        functools.partial(attn_fwd_kernel, heads, rows),
        out_shape=(
            jax.ShapeDtypeStruct((rows, heads * HEAD), bf16),
            jax.ShapeDtypeStruct((rows, heads * SLOT), bf16),
            jax.ShapeDtypeStruct((8, rows), f32),
        ),
        in_specs=[pl.BlockSpec(memory_space=pltpu.SMEM), vm, vm],
        out_specs=(vm, vm, vm),
        scratch_shapes=[
            pltpu.VMEM(kv.shape, bf16),
            pltpu.VMEM(kv.shape, bf16),
            pltpu.VMEM((256, heads * SLOT), bf16),
            pltpu.VMEM((heads, 256, SLOT), f32),
            pltpu.VMEM((heads, 256, SLOT), f32),
        ],
        compiler_params=pltpu.CompilerParams(vmem_limit_bytes=48 * 2**20),
        name="attn_fwd",
    )(info, q, kv)


def turn(x, cosine, sine_low, sine_high):
    return (
        x * cosine + pltpu.roll(x, SLOT - 32, 1) * sine_low + pltpu.roll(x, 32, 1) * sine_high
    )


def attn_bwd_kernel(
    heads, rows, info, q_ref, kv_ref, do_ref, slots_ref, lse_ref, dq_ref, dkv_ref, k0, delta_s, dq_s
):
    tq, tk = 256, 512
    blk = info[0]
    total = kv_ref.shape[0]
    lane = lax.broadcasted_iota(jnp.int32, (tk, SLOT), 1)

    def prepare(i, _):
        at = pl.ds(i * tk, tk)
        k0[at, :] = jnp.where(lane < HEAD, kv_ref[at, :].astype(f32), 0.0).astype(bf16)
        return 0

    lax.fori_loop(0, (blk + 1) * (rows // tk), prepare, 0)

    def deltas(qt, _):
        at = pl.ds(qt * tq, tq)
        for h in range(heads):
            cols = slice(h * SLOT, (h + 1) * SLOT)
            prod = do_ref[at, cols].astype(f32) * slots_ref[at, cols].astype(f32)
            col = jnp.sum(prod, axis=1, keepdims=True)
            wide = jnp.transpose(jnp.broadcast_to(col, (tq, SLOT)))
            delta_s[h : h + 1, pl.ds(pl.multiple_of(qt * tq, tq), tq)] = wide[0:1, :]
        return 0

    lax.fori_loop(0, rows // tq, deltas, 0)
    dq_s[...] = jnp.zeros(dq_s.shape, f32)

    def pair(kt, vt, kvt, qt, masked):
        at = pl.ds(pl.multiple_of(qt * tq, tq), tq)
        grad = None
        for h in range(heads):
            cols = slice(h * SLOT, (h + 1) * SLOT)
            q = q_ref[at, cols]
            do = do_ref[at, cols]
            s = dot(kt, q, NT)
            p = jnp.exp(s - lse_ref[h : h + 1, at])
            if masked is not None:
                p = jnp.where(masked, p, 0.0)
            dp = dot(kvt, do, NT)
            ds = (p * (dp - delta_s[h : h + 1, at])).astype(bf16)
            part = dot(ds, q, NN) + dot(p.astype(bf16), do, NN)
            grad = part if grad is None else grad + part
            dq_s[at, cols] += dot(ds, kt, TN)
        return grad

    def key_tile(i, _):
        at_k = pl.ds(pl.multiple_of(i * tk, tk), tk)
        kt = k0[at_k, :]
        kvt = kv_ref[at_k, :]
        own = blk * (rows // tk)
        first = jnp.maximum(i - own, 0) * (tk // tq)
        ki = lax.broadcasted_iota(jnp.int32, (tk, tq), 0)
        qi = lax.broadcasted_iota(jnp.int32, (tk, tq), 1)

        @pl.when(i < own)
        def _():
            def step(qt, grad):
                return grad + pair(kt, None, kvt, qt, None)

            grad = lax.fori_loop(0, rows // tq, step, jnp.zeros((tk, SLOT), f32))
            dkv_ref[at_k, :] = grad.astype(bf16)

        @pl.when(i >= own)
        def _():
            grad = jnp.zeros((tk, SLOT), f32)
            for j in range(tk // tq):
                grad = grad + pair(kt, None, kvt, first + j, ki <= qi + j * tq)

            def step(qt, grad):
                return grad + pair(kt, None, kvt, qt, None)

            grad = lax.fori_loop(first + tk // tq, rows // tq, step, grad)
            dkv_ref[at_k, :] = grad.astype(bf16)

        return 0

    lax.fori_loop(0, (blk + 1) * (rows // tk), key_tile, 0)

    def clear(i, _):
        dkv_ref[pl.ds(pl.multiple_of(i * tk, tk), tk), :] = jnp.zeros((tk, SLOT), bf16)
        return 0

    lax.fori_loop((blk + 1) * (rows // tk), total // tk, clear, 0)
    dq_ref[...] = dq_s[...]


def attn_bwd(info, q, kv, d_slots, slots, lse, heads):
    rows = q.shape[0]
    vm = pl.BlockSpec(memory_space=pltpu.VMEM)
    return pl.pallas_call(
        functools.partial(attn_bwd_kernel, heads, rows),
        out_shape=(
            jax.ShapeDtypeStruct((rows, heads * SLOT), f32),
            jax.ShapeDtypeStruct(kv.shape, bf16),
        ),
        in_specs=[pl.BlockSpec(memory_space=pltpu.SMEM), vm, vm, vm, vm, vm],
        out_specs=(vm, vm),
        scratch_shapes=[
            pltpu.VMEM(kv.shape, bf16),
            pltpu.VMEM((8, rows), f32),
            pltpu.VMEM((rows, heads * SLOT), f32),
        ],
        compiler_params=pltpu.CompilerParams(vmem_limit_bytes=48 * 2**20),
        name="attn_bwd",
    )(info, q, kv, d_slots, slots, lse)


def spread(weights, heads, first):
    wide = weights.reshape(heads, HEAD, -1)
    zeros = jnp.zeros_like(wide)
    return jnp.concatenate([wide, zeros] if first else [zeros, wide], 1).reshape(heads * SLOT, -1)


def rotary(positions):
    half = HEAD // 2
    freq = rope_base ** (-(jnp.arange(half, dtype=f32) * 2.0) / HEAD)
    phase = positions.astype(f32)[:, None] * freq[None, :]
    cosine, sine = jnp.cos(phase), jnp.sin(phase)
    return cosine, sine


def shards(
    layer_in,
    cotangent,
    lengths,
    attn_gain,
    w_query,
    query_bias,
    w_key,
    key_bias,
    w_value,
    value_bias,
    w_out,
    mlp_gain,
    w_gate,
    w_up,
    w_down,
):
    rows_own, width = layer_in.shape
    rows = rows_own * lax.axis_size("tensor")
    blocks = lax.axis_size("blk")
    heads = w_query.shape[1] // HEAD
    blk = lax.axis_index("blk")
    core = lax.axis_index("tensor")
    bucket = rows * blocks
    length = lengths[0, 0]
    info = jnp.stack([blk.astype(jnp.int32), length])
    start = blk * rows
    own_start = core * rows_own

    x = gather_pair(layer_in, "tensor", 0).astype(f32)
    cot = gather_pair(cotangent, "tensor", 0)
    positions = start + jnp.arange(rows, dtype=jnp.int32)
    live = positions % bucket < length
    cot = jnp.where(live[:, None], cot, 0)

    cosine, sine = rotary(positions)
    zero32 = jnp.zeros_like(sine)
    fill = jnp.ones((rows, HEAD), f32)
    cos_w = jnp.concatenate([cosine, cosine, fill], 1)
    sin_a = jnp.concatenate([sine, zero32, zero32, zero32], 1)
    sin_b = jnp.concatenate([zero32, sine, zero32, zero32], 1)
    slots_n = heads + 1
    w_all = jnp.concatenate(
        [spread(w_query.T, heads, True), w_key.T, w_value.T], 0
    )
    b_all = jnp.concatenate(
        [
            spread(query_bias[:, None], heads, True)[:, 0],
            key_bias,
            value_bias,
        ]
    ).astype(f32)

    def rotate(v, sign):
        v = v.reshape(rows, slots_n, SLOT)
        up = jnp.roll(v, -32, axis=2)
        down = jnp.roll(v, 32, axis=2)
        out = (
            v * cos_w[:, None, :]
            - sign * up * sin_a[:, None, :]
            + sign * down * sin_b[:, None, :]
        )
        return out.reshape(rows, slots_n * SLOT)

    rho1 = lax.rsqrt(jnp.mean(x * x, axis=1, keepdims=True) + norm_eps)
    n1 = x * rho1
    normed_in = (n1 * attn_gain).astype(bf16)
    proj = rotate(contract_cols(normed_in, w_all) + b_all, 1.0)
    q_low = (proj[:, : heads * SLOT].astype(bf16) * HEAD**-0.5).astype(bf16)
    kv = proj[:, heads * SLOT :].astype(bf16)
    for axis, bit in bits_of("blk"):
        kv = gather_pair(kv, axis, bit)
    ctx, ctx_slots, lse = attn_fwd(info, q_low, kv, heads)

    ctx_other = partner(ctx, "tensor", 0)
    w_out_other = partner(w_out, "tensor", 0)
    resid = x + (
        jnp.dot(ctx, w_out, preferred_element_type=f32)
        + jnp.dot(ctx_other, w_out_other, preferred_element_type=f32)
    )
    rho2 = lax.rsqrt(jnp.mean(resid * resid, axis=1, keepdims=True) + norm_eps)
    n2 = resid * rho2
    mlp_in = (n2 * mlp_gain).astype(bf16)
    gate = jnp.dot(mlp_in, w_gate, preferred_element_type=f32)
    upper = jnp.dot(mlp_in, w_up, preferred_element_type=f32)
    sigma = 1.0 / (1.0 + jnp.exp(-gate))
    activ = gate * sigma
    hidden = (activ * upper).astype(bf16)
    grad_down = reduce_grad(contract_rows(hidden, cot, bf16))
    d_hidden = contract_cols(cot, w_down)
    d_gate = (d_hidden * upper * sigma * (1.0 + gate * (1.0 - sigma))).astype(bf16)
    d_up = (d_hidden * activ).astype(bf16)
    grad_gate = reduce_grad(contract_rows(mlp_in, d_gate, bf16))
    grad_up = reduce_grad(contract_rows(mlp_in, d_up, bf16))
    d_mid_part = (contract_cols(d_gate, w_gate) + contract_cols(d_up, w_up)).astype(bf16)
    d_mid = d_mid_part.astype(f32) + partner(d_mid_part, "tensor", 0).astype(f32)
    ffn_out = jnp.dot(hidden, w_down, preferred_element_type=f32).astype(bf16)
    ffn_out = scatter_pair(ffn_out, "tensor", 0).astype(f32)
    own = lambda v: lax.dynamic_slice_in_dim(v, own_start, rows_own, 0)
    layer_out = (own(resid) + ffn_out).astype(bf16)
    mlp_gain_part = jnp.sum(d_mid * n2, axis=0)
    d_resid = cot.astype(f32) + norm_back(d_mid, n2, rho2, mlp_gain)
    d_resid_low = d_resid.astype(bf16)
    grad_out = contract_rows(ctx, d_resid_low, bf16)
    w_out_slots = spread(w_out, heads, False)
    d_slots = contract_cols(d_resid_low, w_out_slots, f32).astype(bf16)
    dq, dkv = attn_bwd(info, q_low, kv, d_slots, ctx_slots, lse, heads)
    for axis, bit in reversed(bits_of("blk")):
        dkv = scatter_pair(dkv, axis, bit)
    keep = (jnp.arange(SLOT) < HEAD).astype(f32)
    dq = jnp.where(keep > 0, dq.reshape(rows, heads, SLOT), 0.0).reshape(rows, heads * SLOT)
    d_proj = rotate(
        jnp.concatenate([dq * HEAD**-0.5, dkv.astype(f32)], 1), -1.0
    ).astype(bf16)
    grad_all = contract_rows(d_proj, normed_in, bf16)
    bias_all = jnp.sum(d_proj.astype(f32), axis=0)
    d_in = contract_cols(d_proj, w_all.T).astype(bf16)
    d_in = scatter_pair(d_in, "tensor", 0).astype(f32)
    n1_own = own(n1)
    attn_gain_part = jnp.sum(d_in * n1_own, axis=0)
    input_grad = (own(d_resid) + norm_back(d_in, n1_own, own(rho1), attn_gain)).astype(bf16)

    qk = heads * SLOT
    grad_q = grad_all[:qk].reshape(heads, SLOT, width)[:, :HEAD].reshape(heads * HEAD, width)
    bias_q = bias_all[:qk].reshape(heads, SLOT)[:, :HEAD].reshape(heads * HEAD)
    nq = heads * HEAD
    small = jnp.concatenate([grad_out, grad_q, grad_all[qk:]], 0)
    small = jnp.pad(small, ((0, (-small.shape[0]) % 256), (0, 0)))
    small = reduce_grad(small)
    vectors = jnp.concatenate([bias_q, bias_all[qk:], attn_gain_part, mlp_gain_part])
    vectors = lax.psum(vectors, ("batch", "blk"))
    nb = bias_all.shape[0] - qk + nq
    attn_gain_sum = lax.psum(vectors[nb : nb + width], "tensor")
    grad_query = small[nq : 2 * nq].T
    grad_key = small[2 * nq : 2 * nq + HEAD].T
    grad_value = small[2 * nq + HEAD : 2 * nq + 2 * HEAD].T
    return (
        layer_out,
        input_grad,
        attn_gain_sum,
        grad_query,
        vectors[:nq],
        grad_key,
        vectors[nq : nq + HEAD],
        grad_value,
        vectors[nq + HEAD : nq + 2 * HEAD],
        small[:nq],
        vectors[nb + width :],
        grad_gate,
        grad_up,
        grad_down,
    )


def solution(mesh):
    rows = P(("batch", "blk", "tensor"), None)
    cols, part, split = P(None, "tensor"), P("tensor"), P("tensor", None)
    return jax.shard_map(
        shards,
        mesh=mesh,
        in_specs=(
            rows, rows, P("batch", None), P(), cols, part, cols, part, cols, part, split, P(),
            cols, cols, split,
        ),
        out_specs=(
            rows, rows, P(), cols, part, cols, part, cols, part, split, P(), cols, cols, split,
        ),
        check_vma=False,
    )
```

```python
import functools
import math

import jax
import jax.numpy as jnp
from jax import lax
from jax.experimental import pallas as pl
from jax.experimental.pallas import tpu as pltpu
from jax.sharding import PartitionSpec as P

HEAD = 64
SLOT = 128

rope_base = 1000000.0
norm_eps = 1e-06
masked_value = -1e30
bf16 = jnp.bfloat16
f32 = jnp.float32


def dot(left, right, dims, kind=f32):
    return lax.dot_general(left, right, (dims, ((), ())), preferred_element_type=kind)


NN = ((1,), (0,))
NT = ((1,), (1,))
TN = ((0,), (0,))


def contract_rows(left, right, kind=f32):
    return dot(left, right, TN, kind)


def contract_cols(left, right, kind=f32):
    return dot(left, right, NT, kind)


def norm_back(grad, normed, scale, gain):
    weighted = grad * gain
    return scale * (weighted - normed * jnp.mean(weighted * normed, axis=1, keepdims=True))


def partner(value, axis, bit):
    n = lax.axis_size(axis)
    return lax.ppermute(value, axis, [(i, i ^ (1 << bit)) for i in range(n)])


def bits_of(axis):
    return [(axis, bit) for bit in range(int(math.log2(lax.axis_size(axis))))]


def my_bit(axis, bit):
    return (lax.axis_index(axis) >> bit) & 1


def in_order(own, other, axis, bit):
    first = my_bit(axis, bit) == 0
    return jnp.where(
        first, jnp.concatenate([own, other], 0), jnp.concatenate([other, own], 0)
    )


def gather_pair(own, axis, bit):
    return in_order(own, partner(own, axis, bit), axis, bit)


def scatter_pair(value, axis, bit):
    half = value.shape[0] // 2
    mine = my_bit(axis, bit)
    keep = lax.dynamic_slice_in_dim(value, mine * half, half, 0)
    send = lax.dynamic_slice_in_dim(value, (1 - mine) * half, half, 0)
    got = partner(send, axis, bit)
    return (keep.astype(f32) + got.astype(f32)).astype(bf16)


def add_pair(value, axis, bit):
    got = partner(value, axis, bit)
    return (value.astype(f32) + got.astype(f32)).astype(bf16)


def reduce_all(value, steps):
    halved = []
    for axis, bit in steps:
        if value.shape[0] % 16 == 0:
            value = scatter_pair(value, axis, bit)
            halved.append((axis, bit))
        else:
            value = add_pair(value, axis, bit)
    for axis, bit in reversed(halved):
        value = gather_pair(value, axis, bit)
    return value


def reduce_grad(value):
    half = value.shape[0] // 2
    plane, line = bits_of("blk"), bits_of("batch")
    first = reduce_all(value[:half], plane + line)
    second = reduce_all(value[half:], plane[::-1] + line)
    return jnp.concatenate([first, second], 0).astype(f32)


def attn_fwd_kernel(
    heads, rows, info, q_ref, kv_ref, ctx_ref, slots_ref, lse_ref, k1, v1, q1, m_s, acc_s
):
    tq, tk = 256, 512
    blk, length = info[0], info[1]
    total = kv_ref.shape[0]
    lane = lax.broadcasted_iota(jnp.int32, (tk, SLOT), 1)
    row = lax.broadcasted_iota(jnp.int32, (tk, SLOT), 0)

    def prepare(i, _):
        at = pl.ds(i * tk, tk)
        kv = kv_ref[at, :].astype(f32)
        dead = jnp.where(row + i * tk < length, 0.0, masked_value)
        k1[at, :] = jnp.where(lane < HEAD, kv, jnp.where(lane == HEAD, dead, 0.0)).astype(bf16)
        v1[at, :] = jnp.where(lane < HEAD, 1.0, kv).astype(bf16)
        return 0

    lax.fori_loop(0, (blk + 1) * (rows // tk), prepare, 0)
    one = jnp.where(lax.broadcasted_iota(jnp.int32, (tq, SLOT), 1) == HEAD, 1.0, 0.0)

    def tile(at, masked):
        kt = k1[at, :]
        vt = v1[at, :]
        for h in range(heads):
            s = dot(q1[:, h * SLOT : (h + 1) * SLOT], kt, NT)
            if masked is not None:
                s = jnp.where(masked, s, masked_value)
            m_prev = m_s[h]
            m_new = jnp.maximum(m_prev, jnp.max(s, axis=1, keepdims=True))
            alpha = jnp.exp(m_prev - m_new)
            p = jnp.exp(s - jnp.concatenate([m_new] * (tk // SLOT), 1))
            acc_s[h] = acc_s[h] * alpha + dot(p.astype(bf16), vt, NN)
            m_s[h] = m_new

    def query_tile(qt, _):
        at_q = pl.ds(qt * tq, tq)
        for h in range(heads):
            cols = slice(h * SLOT, (h + 1) * SLOT)
            q1[:, cols] = (q_ref[at_q, cols].astype(f32) + one).astype(bf16)
        m_s[...] = jnp.full(m_s.shape, masked_value, f32)
        acc_s[...] = jnp.zeros(acc_s.shape, f32)
        full = blk * (rows // tk) + (qt * tq) // tk

        def full_tile(i, _):
            tile(pl.ds(pl.multiple_of(i * tk, tk), tk), None)
            return 0

        lax.fori_loop(0, full, full_tile, 0)
        shift = (qt * tq) % tk
        ri = lax.broadcasted_iota(jnp.int32, (tq, tk), 0) + shift
        ci = lax.broadcasted_iota(jnp.int32, (tq, tk), 1)
        tile(pl.ds(pl.multiple_of(full * tk, tk), tk), ci <= ri)
        pos = lax.broadcasted_iota(jnp.int32, (1, tq), 1) + blk * rows + qt * tq
        for h in range(heads):
            acc = acc_s[h]
            out = acc / pltpu.roll(acc, HEAD, 1)
            wide = jnp.where(lax.broadcasted_iota(jnp.int32, (tq, SLOT), 1) < HEAD, 0.0, out)
            slots_ref[at_q, h * SLOT : (h + 1) * SLOT] = wide.astype(bf16)
            ctx_ref[at_q, h * HEAD : (h + 1) * HEAD] = wide[:, HEAD:].astype(bf16)
            lse = jnp.transpose(m_s[h] + jnp.log(acc))[0:1, :]
            lse_ref[h : h + 1, pl.ds(pl.multiple_of(qt * tq, tq), tq)] = jnp.where(
                pos < length, lse, -masked_value
            )
        return 0

    lax.fori_loop(0, rows // tq, query_tile, 0)


def attn_fwd(info, q, kv, heads):
    rows = q.shape[0]
    vm = pl.BlockSpec(memory_space=pltpu.VMEM)
    return pl.pallas_call(
        functools.partial(attn_fwd_kernel, heads, rows),
        out_shape=(
            jax.ShapeDtypeStruct((rows, heads * HEAD), bf16),
            jax.ShapeDtypeStruct((rows, heads * SLOT), bf16),
            jax.ShapeDtypeStruct((8, rows), f32),
        ),
        in_specs=[pl.BlockSpec(memory_space=pltpu.SMEM), vm, vm],
        out_specs=(vm, vm, vm),
        scratch_shapes=[
            pltpu.VMEM(kv.shape, bf16),
            pltpu.VMEM(kv.shape, bf16),
            pltpu.VMEM((256, heads * SLOT), bf16),
            pltpu.VMEM((heads, 256, SLOT), f32),
            pltpu.VMEM((heads, 256, SLOT), f32),
        ],
        compiler_params=pltpu.CompilerParams(vmem_limit_bytes=48 * 2**20),
        name="attn_fwd",
    )(info, q, kv)


def turn(x, cosine, sine_low, sine_high):
    return (
        x * cosine + pltpu.roll(x, SLOT - 32, 1) * sine_low + pltpu.roll(x, 32, 1) * sine_high
    )


PART = 128


def ffn_kernel(
    x_ref, ctx_ref, ctx_o_ref, wo_ref, wo_o_ref, gain_ref, cot_ref, wg_ref, wu_ref, wd_ref,
    resid_ref, g_ref, dmid_ref, out_ref, mlp, mlp_t, cot_t, trio, dmid_s, out_s,
):
    step = pl.program_id(0)
    rows = x_ref.shape[0]
    tile = 256

    @pl.when(step == 0)
    def _():
        def first(r, _):
            at = pl.ds(pl.multiple_of(r * tile, tile), tile)
            resid = (
                x_ref[at, :].astype(f32)
                + dot(ctx_ref[at, :], wo_ref[...], NN)
                + dot(ctx_o_ref[at, :], wo_o_ref[...], NN)
            )
            resid_ref[at, :] = resid
            rho = lax.rsqrt(jnp.mean(resid * resid, axis=1, keepdims=True) + norm_eps)
            normed = resid * rho * gain_ref[...]
            mlp[at, :] = normed.astype(bf16)
            mlp_t[:, at] = jnp.transpose(normed).astype(bf16)
            cot_t[:, at] = jnp.transpose(cot_ref[at, :].astype(f32)).astype(bf16)
            return 0

        lax.fori_loop(0, rows // tile, first, 0)
        dmid_s[...] = jnp.zeros(dmid_s.shape, f32)
        out_s[...] = jnp.zeros(out_s.shape, f32)

    pair = jnp.concatenate([wg_ref[...], wu_ref[...]], 1)
    down = wd_ref[...]
    for r in range(rows // tile):
        at = slice(r * tile, (r + 1) * tile)
        both = dot(mlp[at, :], pair, NN)
        gate, upper = both[:, :PART], both[:, PART:]
        d_hidden = dot(cot_ref[at, :], down, NT)
        sigma = 1.0 / (1.0 + jnp.exp(-gate))
        activ = gate * sigma
        hidden = (activ * upper).astype(bf16)
        d_gate = (d_hidden * upper * sigma * (1.0 + gate * (1.0 - sigma))).astype(bf16)
        d_up = (d_hidden * activ).astype(bf16)
        d_pair = jnp.concatenate([d_gate, d_up], 1)
        trio[at, :PART] = hidden
        trio[at, PART:] = d_pair
        out_s[at, :] += dot(hidden, down, NN)
        dmid_s[at, :] += dot(d_pair, pair, NT)
    g_ref[0, :, :PART] = dot(cot_t[...], trio[:, :PART], NN).astype(bf16)
    g_ref[0, :, PART:] = dot(mlp_t[...], trio[:, PART:], NN).astype(bf16)

    @pl.when(step == pl.num_programs(0) - 1)
    def _():
        dmid_ref[...] = dmid_s[...].astype(bf16)
        out_ref[...] = out_s[...].astype(bf16)


def feed_forward(x, ctx, ctx_o, w_out, w_out_o, gain, cot, w_gate, w_up, w_down):
    rows, width = x.shape
    hidden = w_gate.shape[1]
    steps = hidden // PART
    whole = lambda a: pl.BlockSpec(a.shape, lambda j: (0,) * a.ndim)
    row_block = pl.BlockSpec((rows, width), lambda j: (0, 0))
    return pl.pallas_call(
        ffn_kernel,
        grid=(steps,),
        out_shape=(
            jax.ShapeDtypeStruct((rows, width), f32),
            jax.ShapeDtypeStruct((steps, width, 3 * PART), bf16),
            jax.ShapeDtypeStruct((rows, width), bf16),
            jax.ShapeDtypeStruct((rows, width), bf16),
        ),
        in_specs=[
            whole(x), whole(ctx), whole(ctx_o), whole(w_out), whole(w_out_o), whole(gain),
            whole(cot),
            pl.BlockSpec((width, PART), lambda j: (0, j)),
            pl.BlockSpec((width, PART), lambda j: (0, j)),
            pl.BlockSpec((PART, width), lambda j: (j, 0)),
        ],
        out_specs=(
            row_block,
            pl.BlockSpec((1, width, 3 * PART), lambda j: (j, 0, 0)),
            row_block,
            row_block,
        ),
        scratch_shapes=[
            pltpu.VMEM((rows, width), bf16),
            pltpu.VMEM((width, rows), bf16),
            pltpu.VMEM((width, rows), bf16),
            pltpu.VMEM((rows, 3 * PART), bf16),
            pltpu.VMEM((rows, width), f32),
            pltpu.VMEM((rows, width), f32),
        ],
        compiler_params=pltpu.CompilerParams(
            vmem_limit_bytes=56 * 2**20, dimension_semantics=("arbitrary",)
        ),
        name="ffn",
    )(x, ctx, ctx_o, w_out, w_out_o, gain, cot, w_gate, w_up, w_down)


RING = 4
CHUNK = 3 * PART


class Stream:
    def __init__(self, first, count, axes):
        self.first, self.count = first, count
        self.reduce, self.sizes = [], []
        size = count
        for axis, bit in axes:
            half = size % 32 == 0
            size = size // 2 if half else size
            self.reduce.append((half, axis, bit))
            self.sizes.append(size)
        self.gather = [(axis, bit) for half, axis, bit in reversed(self.reduce) if half]
        self.stages = len(self.reduce) + len(self.gather) + 1

    def scratch(self):
        copies = len(self.reduce) + len(self.gather)
        return [pltpu.VMEM((RING, self.sizes[0], CHUNK), bf16)] + [
            pltpu.VMEM((RING, size, CHUNK), bf16) for size in self.sizes
        ] + [
            pltpu.SemaphoreType.DMA((copies, RING)),
            pltpu.SemaphoreType.DMA((copies, RING)),
            pltpu.SemaphoreType.DMA((2, RING)),
        ]

    def bind(self, refs, sources, out):
        n = len(self.reduce)
        self.keep, self.got = refs[0], refs[1 : n + 1]
        self.send, self.recv, self.local = refs[n + 1 :]
        self.sources, self.out = sources, out
        self.peer, self.mine, offset = [], [], self.first
        self.offsets = []
        for (half, axis, bit), size in zip(self.reduce, self.sizes):
            at = lax.axis_index(axis)
            one = lax.rem(at // (1 << bit), 2)
            self.peer.append({axis: at + (1 - 2 * one) * (1 << bit)})
            self.mine.append(one)
            offset = offset + one * size if half else offset
            self.offsets.append(offset)
        self.whole = []
        offset, size = self.offsets[-1], self.sizes[-1]
        self.gather_peer = []
        for k in reversed(range(n)):
            half = self.reduce[k][0]
            if half:
                self.whole.append((offset, size))
                self.gather_peer.append(self.peer[k])
                offset, size = offset - self.mine[k] * size, 2 * size

    def copy(self, k, ring, src, dst, peer):
        return pltpu.make_async_remote_copy(
            src_ref=src,
            dst_ref=dst,
            send_sem=self.send.at[k, ring],
            recv_sem=self.recv.at[k, ring],
            device_id=peer,
            device_id_type=pl.DeviceIdType.MESH,
        )

    def start_first(self, ring, source):
        size, one = self.sizes[0], self.mine[0]
        theirs = pl.multiple_of(self.first + (1 - one) * size, 16)
        own = pl.multiple_of(self.first + one * size, 16)
        self.copy(
            0, ring, source.at[pl.ds(theirs, size), :], self.got[0].at[ring], self.peer[0]
        ).start()
        pltpu.make_async_copy(
            source.at[pl.ds(own, size), :], self.keep.at[ring], self.local.at[0, ring]
        ).start()

    def reduce_copy(self, k, ring):
        if k == 0:
            src = self.keep.at[ring]
        elif self.reduce[k][0]:
            size = self.sizes[k]
            theirs = pl.multiple_of((1 - self.mine[k]) * size, 16)
            src = self.got[k - 1].at[ring, pl.ds(theirs, size), :]
        else:
            src = self.got[k - 1].at[ring]
        return self.copy(k, ring, src, self.got[k].at[ring], self.peer[k])

    def gather_copy(self, t, ring, chunk):
        offset, size = self.whole[t]
        rows = pl.ds(pl.multiple_of(offset, 16), size)
        place = self.out.at[chunk, rows, :]
        src = self.got[-1].at[ring] if t == 0 else place
        return self.copy(len(self.reduce) + t, ring, src, place, self.gather_peer[t])

    def own_copy(self, ring, chunk):
        offset, size = self.whole[0]
        rows = pl.ds(pl.multiple_of(offset, 16), size)
        return pltpu.make_async_copy(
            self.got[-1].at[ring], self.out.at[chunk, rows, :], self.local.at[1, ring]
        )

    def stage(self, s, chunk):
        ring = lax.rem(chunk, RING)
        n = len(self.reduce)
        if s == 0:
            base = 0
            for count, place in self.sources:
                @pl.when((chunk >= base) & (chunk < base + count))
                def _(base=base, place=place):
                    self.start_first(ring, place(chunk - base))

                base += count
            return
        if s <= n:
            k = s - 1
            if k == 0:
                pltpu.make_async_copy(
                    self.got[0].at[ring], self.keep.at[ring], self.local.at[0, ring]
                ).wait()
            self.reduce_copy(k, ring).wait()
            size = self.sizes[k]
            if k == 0:
                own = self.keep[ring]
            elif self.reduce[k][0]:
                own = self.got[k - 1][ring, pl.ds(pl.multiple_of(self.mine[k] * size, 16), size), :]
            else:
                own = self.got[k - 1][ring]
            total = own.astype(f32) + self.got[k][ring].astype(f32)
            self.got[k][ring] = total.astype(bf16)
            if s < n:
                self.reduce_copy(s, ring).start()
            else:
                self.own_copy(ring, chunk).start()
                self.gather_copy(0, ring, chunk).start()
            return
        t = s - n - 1
        self.gather_copy(t, ring, chunk).wait()
        if t == 0:
            self.own_copy(ring, chunk).wait()
        if t + 1 < len(self.gather):
            self.gather_copy(t + 1, ring, chunk).start()


def make_streams(width, plane, line):
    unit = width // 7
    return [
        Stream(0, 3 * unit, plane + line),
        Stream(3 * unit, 3 * unit, plane[::-1] + line),
        Stream(6 * unit, unit, line + plane),
    ]


def turn(v, cosine, sine_a, sine_b):
    return v * cosine + pltpu.roll(v, SLOT - 32, 1) * sine_a - pltpu.roll(v, 32, 1) * sine_b


LOADS = (
    "dmid", "resid", "cot", "w_slots", "ctx", "slots", "q", "kv", "lse",
    "cosine", "sine_a", "sine_b", "normed", "w_all", "own_in", "gain1", "gain2", "part",
)


def backward_kernel(heads, streams, n_ffn, n_small, *refs):
    nl = len(LOADS)
    hbm = dict(zip(LOADS, refs[:nl]))
    grads_ref = refs[nl]
    sums_ref, layer_out_ref, input_grad_ref = refs[nl + 1 : nl + 4]
    refs = list(refs[nl + 4 :])
    m = dict(zip(LOADS, refs[:nl]))
    refs = refs[nl:]
    (
        load_sem, dmid_o, part_o, do, dlow, delta, dq, dkv, dkv_o, k0, dproj, small,
        din_send, din_own, din_o, rowsum, vec, pair_send, pair_recv, kv_send, kv_recv, out_sem,
    ) = refs[:22]
    refs = refs[22:]
    rows, width = m["cot"].shape
    half = rows // 2
    blk, nb = lax.axis_index("blk"), lax.axis_size("blk")
    core = lax.axis_index("tensor")
    nz = lax.axis_size("batch")
    other = {"tensor": 1 - core}
    tile = 256

    pos = 0
    for st in streams:
        cnt = len(st.scratch())
        st.bind(
            refs[pos : pos + cnt],
            [(n_ffn, lambda c: grads_ref.at[c]), (n_small, lambda c: small.at[c])],
            sums_ref,
        )
        pos += cnt

    loads = {
        name: pltpu.make_async_copy(hbm[name], m[name], load_sem.at[i])
        for i, name in enumerate(LOADS)
    }
    for copy in loads.values():
        copy.start()

    barrier = pltpu.get_barrier_semaphore()
    peers = [other]
    peers += [{"blk": lax.rem(blk + d, nb)} for d in range(1, nb)]
    batch = lax.axis_index("batch")
    peers += [
        {"batch": batch + (1 - 2 * lax.rem(batch // (1 << b), 2)) * (1 << b)}
        for b in range(int(math.log2(nz)))
    ]
    for peer in peers:
        pl.semaphore_signal(barrier, 1, device_id=peer, device_id_type=pl.DeviceIdType.MESH)
    pl.semaphore_wait(barrier, len(peers))

    def swap(k, src, dst):
        return pltpu.make_async_remote_copy(
            src_ref=src, dst_ref=dst, send_sem=pair_send.at[k], recv_sem=pair_recv.at[k],
            device_id=other, device_id_type=pl.DeviceIdType.MESH,
        )

    def dmid_swap():
        return swap(0, hbm["dmid"], dmid_o)

    theirs = pl.multiple_of((1 - core) * half, 16)
    ours = pl.multiple_of(core * half, 16)

    def part_swap():
        return swap(1, hbm["part"].at[pl.ds(theirs, half), :], part_o)

    def din_swap():
        return swap(2, din_send, din_o)

    dmid_swap().start()
    part_swap().start()

    def put(first, at, value):
        done, n = 0, value.shape[1]
        while done < n:
            c, lane = divmod(first + done, CHUNK)
            take = min(n - done, CHUNK - lane)
            small[c, at, lane : lane + take] = value[:, done : done + take].astype(bf16)
            done += take

    nq = heads * HEAD
    tq, tk = 256, 512

    def before():
        for name in LOADS:
            if name != "part":
                loads[name].wait()
        loads["part"].wait()
        dmid_swap().wait()
        part_swap().wait()
        vec[...] = jnp.zeros(vec.shape, f32)

        def out_rows(r, _):
            at = pl.ds(pl.multiple_of(r * tile, tile), tile)
            mine = pl.ds(pl.multiple_of(ours + r * tile, tile), tile)
            part_o[at, :] = (
                m["resid"][mine, :] + m["part"][mine, :].astype(f32) + part_o[at, :].astype(f32)
            ).astype(bf16)
            return 0

        lax.fori_loop(0, half // tile, out_rows, 0)
        pltpu.make_async_copy(part_o, layer_out_ref, out_sem.at[0]).start()

        def norm(r, _):
            at = pl.ds(pl.multiple_of(r * tile, tile), tile)
            dmid = m["dmid"][at, :].astype(f32) + dmid_o[at, :].astype(f32)
            resid = m["resid"][at, :]
            rho = lax.rsqrt(jnp.mean(resid * resid, axis=1, keepdims=True) + norm_eps)
            n2 = resid * rho
            vec[1:2, :] += jnp.sum(dmid * n2, axis=0, keepdims=True)
            weighted = dmid * m["gain2"][...]
            d_resid = m["cot"][at, :].astype(f32) + rho * (
                weighted - n2 * jnp.mean(weighted * n2, axis=1, keepdims=True)
            )
            m["resid"][at, :] = d_resid
            low = d_resid.astype(bf16)
            dlow[at, :] = low
            d_ctx = dot(low, m["w_slots"][...], NT)
            do[at, :] = d_ctx.astype(bf16)
            for h in range(heads):
                cols = slice(h * SLOT, (h + 1) * SLOT)
                prod = do[at, cols].astype(f32) * m["slots"][at, cols].astype(f32)
                col = jnp.sum(prod, axis=1, keepdims=True)
                wide = jnp.transpose(jnp.broadcast_to(col, (tile, SLOT)))
                delta[h : h + 1, at] = wide[0:1, :]
            return 0

        lax.fori_loop(0, rows // tile, norm, 0)

        def grad_out(k, _):
            at = pl.ds(pl.multiple_of(k * 128, 128), 128)
            put(0, at, dot(dlow[:, at], m["ctx"][...], TN))
            return 0

        lax.fori_loop(0, width // 128, grad_out, 0)
        lane = lax.broadcasted_iota(jnp.int32, (tk, SLOT), 1)

        def keys(i, _):
            at = pl.ds(pl.multiple_of(i * tk, tk), tk)
            k0[at, :] = jnp.where(lane < HEAD, m["kv"][at, :].astype(f32), 0.0).astype(bf16)
            return 0

        lax.fori_loop(0, (blk + 1) * (rows // tk), keys, 0)
        dq[...] = jnp.zeros(dq.shape, f32)

    def pair(kt, kvt, qt, masked):
        at = pl.ds(pl.multiple_of(qt * tq, tq), tq)
        grad = None
        for h in range(heads):
            cols = slice(h * SLOT, (h + 1) * SLOT)
            q = m["q"][at, cols]
            d_ctx = do[at, cols]
            s = dot(kt, q, NT)
            p = jnp.exp(s - m["lse"][h : h + 1, at])
            if masked is not None:
                p = jnp.where(masked, p, 0.0)
            dp = dot(kvt, d_ctx, NT)
            ds = (p * (dp - delta[h : h + 1, at])).astype(bf16)
            part = dot(ds, q, NN) + dot(p.astype(bf16), d_ctx, NN)
            grad = part if grad is None else grad + part
            dq[at, cols] += dot(ds, kt, TN)
        return grad

    def own_block():
        ki = lax.broadcasted_iota(jnp.int32, (tk, tq), 0)
        qi = lax.broadcasted_iota(jnp.int32, (tk, tq), 1)

        def key_tile(i, _):
            at_k = pl.ds(pl.multiple_of(blk * rows + i * tk, tk), tk)
            kt, kvt = k0[at_k, :], m["kv"][at_k, :]
            first = i * (tk // tq)

            def near(j, grad):
                return grad + pair(kt, kvt, first + j, ki <= qi + j * tq)

            def far(qt, grad):
                return grad + pair(kt, kvt, qt, None)

            grad = lax.fori_loop(0, tk // tq, near, jnp.zeros((tk, SLOT), f32))
            grad = lax.fori_loop(first + tk // tq, rows // tq, far, grad)
            dkv[at_k, :] = grad.astype(bf16)
            return 0

        lax.fori_loop(0, rows // tk, key_tile, 0)

    def earlier(i):
        at_k = pl.ds(pl.multiple_of(i * tk, tk), tk)
        kt, kvt = k0[at_k, :], m["kv"][at_k, :]

        def step(qt, grad):
            return grad + pair(kt, kvt, qt, None)

        grad = lax.fori_loop(0, rows // tq, step, jnp.zeros((tk, SLOT), f32))
        dkv[at_k, :] = grad.astype(bf16)

    def kv_copy(d):
        to = lax.rem(blk + d, nb)
        at = pl.ds(pl.multiple_of(to * rows, rows), rows)
        return pltpu.make_async_remote_copy(
            src_ref=dkv.at[at, :], dst_ref=dkv_o.at[d - 1],
            send_sem=kv_send.at[d - 1], recv_sem=kv_recv.at[d - 1],
            device_id={"blk": to}, device_id_type=pl.DeviceIdType.MESH,
        )

    def kv_start():
        for d in range(1, nb):
            @pl.when(lax.rem(blk + d, nb) < blk)
            def _(d=d):
                kv_copy(d).start()

    def project():
        for d in range(1, nb):
            @pl.when(lax.rem(blk + d, nb) < blk)
            def _(d=d):
                kv_copy(d).wait_send()

            @pl.when(lax.rem(blk + nb - d, nb) > blk)
            def _(d=d):
                kv_copy(d).wait_recv()
                for r in range(rows // tile):
                    at = pl.ds(pl.multiple_of(blk * rows + r * tile, tile), tile)
                    total = dkv[at, :].astype(f32) + dkv_o[d - 1, r * tile : (r + 1) * tile].astype(f32)
                    dkv[at, :] = total.astype(bf16)

        rowsum[...] = jnp.zeros(rowsum.shape, f32)
        lane = lax.broadcasted_iota(jnp.int32, (tile, SLOT), 1)

        def unrotate(r, _):
            at = pl.ds(pl.multiple_of(r * tile, tile), tile)
            at_b = pl.ds(pl.multiple_of(blk * rows + r * tile, tile), tile)
            table = m["cosine"][at, :], m["sine_a"][at, :], m["sine_b"][at, :]
            for h in range(heads + 1):
                cols = slice(h * SLOT, (h + 1) * SLOT)
                if h < heads:
                    v = jnp.where(lane < HEAD, turn(dq[at, cols] * HEAD**-0.5, *table), 0.0)
                else:
                    v = turn(dkv[at_b, :].astype(f32), *table)
                low = v.astype(bf16)
                dproj[at, cols] = low
                rowsum[0:1, cols] += jnp.sum(low.astype(f32), axis=0, keepdims=True)
            return 0

        lax.fori_loop(0, rows // tile, unrotate, 0)

        def d_in(to, first):
            def step(r, _):
                src = pl.ds(pl.multiple_of(first + r * tile, tile), tile)
                at = pl.ds(pl.multiple_of(r * tile, tile), tile)
                to[at, :] = dot(dproj[src, :], m["w_all"][...], NN).astype(bf16)
                return 0

            lax.fori_loop(0, half // tile, step, 0)

        d_in(din_send, theirs)
        din_swap().start()
        d_in(din_own, ours)

        def grads(k, _):
            at = pl.ds(pl.multiple_of(k * 128, 128), 128)
            g = dot(m["normed"][:, at], dproj[...], TN)
            for h in range(heads):
                put(nq + h * HEAD, at, g[:, h * SLOT : h * SLOT + HEAD])
            put(2 * nq, at, g[:, heads * SLOT :])
            return 0

        lax.fori_loop(0, width // 128, grads, 0)

    def finish():
        din_swap().wait()

        def step(r, _):
            at = pl.ds(pl.multiple_of(r * tile, tile), tile)
            mine = pl.ds(pl.multiple_of(ours + r * tile, tile), tile)
            d_in = din_own[at, :].astype(f32) + din_o[at, :].astype(f32)
            x = m["own_in"][at, :].astype(f32)
            rho = lax.rsqrt(jnp.mean(x * x, axis=1, keepdims=True) + norm_eps)
            n1 = x * rho
            vec[0:1, :] += jnp.sum(d_in * n1, axis=0, keepdims=True)
            weighted = d_in * m["gain1"][...]
            grad = m["resid"][mine, :] + rho * (
                weighted - n1 * jnp.mean(weighted * n1, axis=1, keepdims=True)
            )
            din_own[at, :] = grad.astype(bf16)
            return 0

        lax.fori_loop(0, half // tile, step, 0)
        pltpu.make_async_copy(din_own, input_grad_ref, out_sem.at[1]).start()
        for h in range(heads):
            vec[2:3, h * HEAD : (h + 1) * HEAD] = rowsum[0:1, h * SLOT : h * SLOT + HEAD]
        vec[2:3, nq : nq + SLOT] = rowsum[0:1, heads * SLOT :]
        put(2 * nq + SLOT, slice(None), jnp.transpose(vec[...]))

    n_attn = 2 + (nb - 1) * (rows // tk)

    def compute(i):
        pl.when(i == 0)(before)
        pl.when(i == 1)(own_block)

        @pl.when((i >= 2) & (i - 2 < blk * (rows // tk)))
        def _():
            earlier(i - 2)

        pl.when(i == n_attn)(kv_start)
        pl.when(i == n_attn + 1)(project)
        pl.when(i == n_attn + 2)(finish)

    n = n_ffn + n_small
    depth = max(st.stages for st in streams)

    def slot(i, _):
        for st in streams:
            for s in reversed(range(st.stages)):
                @pl.when((i - s >= 0) & (i - s < n))
                def _(st=st, s=s):
                    st.stage(s, i - s)

        compute(i)
        return 0

    lax.fori_loop(0, n + depth - 1, slot, 0)
    pltpu.make_async_copy(part_o, layer_out_ref, out_sem.at[0]).wait()
    pltpu.make_async_copy(din_own, input_grad_ref, out_sem.at[1]).wait()


def backward(values, grads, heads, plane, line, nb):
    rows, width = values["cot"].shape
    half = rows // 2
    keys = values["kv"].shape[0]
    n_ffn = grads.shape[0]
    n_small = -(-(2 * heads * HEAD + 2 * SLOT) // CHUNK)
    assert n_ffn >= 5 + (nb - 1) * 2
    streams = make_streams(width, plane, line)
    hbm = pl.BlockSpec(memory_space=pl.ANY)
    dma = pltpu.SemaphoreType.DMA
    scratch = [pltpu.VMEM(values[name].shape, values[name].dtype) for name in LOADS]
    scratch += [
        dma((len(LOADS),)),
        pltpu.VMEM((rows, width), bf16),
        pltpu.VMEM((half, width), bf16),
        pltpu.VMEM((rows, heads * SLOT), bf16),
        pltpu.VMEM((rows, width), bf16),
        pltpu.VMEM((8, rows), f32),
        pltpu.VMEM((rows, heads * SLOT), f32),
        pltpu.VMEM((keys, SLOT), bf16),
        pltpu.VMEM((nb - 1, rows, SLOT), bf16),
        pltpu.VMEM((keys, SLOT), bf16),
        pltpu.VMEM((rows, (heads + 1) * SLOT), bf16),
        pltpu.VMEM((n_small, width, CHUNK), bf16),
        pltpu.VMEM((half, width), bf16),
        pltpu.VMEM((half, width), bf16),
        pltpu.VMEM((half, width), bf16),
        pltpu.VMEM((8, (heads + 1) * SLOT), f32),
        pltpu.VMEM((SLOT, width), f32),
        dma((3,)),
        dma((3,)),
        dma((nb - 1,)),
        dma((nb - 1,)),
        dma((2,)),
    ]
    for st in streams:
        scratch += st.scratch()
    return pl.pallas_call(
        functools.partial(backward_kernel, heads, streams, n_ffn, n_small),
        out_shape=(
            jax.ShapeDtypeStruct((n_ffn + n_small, width, CHUNK), bf16),
            jax.ShapeDtypeStruct((half, width), bf16),
            jax.ShapeDtypeStruct((half, width), bf16),
        ),
        in_specs=[hbm] * (len(LOADS) + 1),
        out_specs=(hbm, hbm, hbm),
        scratch_shapes=scratch,
        compiler_params=pltpu.CompilerParams(
            collective_id=0, has_side_effects=True, vmem_limit_bytes=60 * 2**20
        ),
        name="backward",
    )(*[values[name] for name in LOADS], grads)


def spread(weights, heads, first):
    wide = weights.reshape(heads, HEAD, -1)
    zeros = jnp.zeros_like(wide)
    return jnp.concatenate([wide, zeros] if first else [zeros, wide], 1).reshape(heads * SLOT, -1)


def rotary(positions):
    half = HEAD // 2
    freq = rope_base ** (-(jnp.arange(half, dtype=f32) * 2.0) / HEAD)
    phase = positions.astype(f32)[:, None] * freq[None, :]
    cosine, sine = jnp.cos(phase), jnp.sin(phase)
    return cosine, sine


def shards(
    layer_in,
    cotangent,
    lengths,
    attn_gain,
    w_query,
    query_bias,
    w_key,
    key_bias,
    w_value,
    value_bias,
    w_out,
    mlp_gain,
    w_gate,
    w_up,
    w_down,
):
    rows_own, width = layer_in.shape
    rows = rows_own * lax.axis_size("tensor")
    blocks = lax.axis_size("blk")
    heads = w_query.shape[1] // HEAD
    blk = lax.axis_index("blk")
    core = lax.axis_index("tensor")
    bucket = rows * blocks
    length = lengths[0, 0]
    info = jnp.stack([blk.astype(jnp.int32), length])
    start = blk * rows
    own_start = core * rows_own

    x_low = gather_pair(layer_in, "tensor", 0)
    x = x_low.astype(f32)
    cot = gather_pair(cotangent, "tensor", 0)
    positions = start + jnp.arange(rows, dtype=jnp.int32)
    live = positions % bucket < length
    cot = jnp.where(live[:, None], cot, 0)

    cosine, sine = rotary(positions)
    zero32 = jnp.zeros_like(sine)
    fill = jnp.ones((rows, HEAD), f32)
    cos_w = jnp.concatenate([cosine, cosine, fill], 1)
    sin_a = jnp.concatenate([sine, zero32, zero32, zero32], 1)
    sin_b = jnp.concatenate([zero32, sine, zero32, zero32], 1)
    slots_n = heads + 1
    w_all = jnp.concatenate(
        [spread(w_query.T, heads, True), w_key.T, w_value.T], 0
    )
    b_all = jnp.concatenate(
        [
            spread(query_bias[:, None], heads, True)[:, 0],
            key_bias,
            value_bias,
        ]
    ).astype(f32)

    def rotate(v, sign):
        v = v.reshape(rows, slots_n, SLOT)
        up = jnp.roll(v, -32, axis=2)
        down = jnp.roll(v, 32, axis=2)
        out = (
            v * cos_w[:, None, :]
            - sign * up * sin_a[:, None, :]
            + sign * down * sin_b[:, None, :]
        )
        return out.reshape(rows, slots_n * SLOT)

    rho1 = lax.rsqrt(jnp.mean(x * x, axis=1, keepdims=True) + norm_eps)
    n1 = x * rho1
    normed_in = (n1 * attn_gain).astype(bf16)
    proj = rotate(contract_cols(normed_in, w_all) + b_all, 1.0)
    q_low = (proj[:, : heads * SLOT].astype(bf16) * HEAD**-0.5).astype(bf16)
    kv = proj[:, heads * SLOT :].astype(bf16)
    for axis, bit in bits_of("blk"):
        kv = gather_pair(kv, axis, bit)
    ctx, ctx_slots, lse = attn_fwd(info, q_low, kv, heads)

    ctx_other = partner(ctx, "tensor", 0)
    w_out_other = partner(w_out, "tensor", 0)
    resid, grads, dmid, part = feed_forward(
        x_low, ctx, ctx_other, w_out, w_out_other, mlp_gain[None, :], cot, w_gate, w_up, w_down
    )
    values = dict(
        dmid=dmid,
        resid=resid,
        cot=cot,
        w_slots=spread(w_out, heads, False),
        ctx=ctx,
        slots=ctx_slots,
        q=q_low,
        kv=kv,
        lse=lse,
        cosine=cos_w,
        sine_a=sin_a,
        sine_b=sin_b,
        normed=normed_in,
        w_all=w_all,
        own_in=layer_in,
        gain1=attn_gain[None, :],
        gain2=mlp_gain[None, :],
        part=part,
    )
    sums, layer_out, input_grad = backward(
        values, grads, heads, bits_of("blk"), bits_of("batch"), blocks
    )
    n_ffn = grads.shape[0]
    ffn = sums[:n_ffn].astype(f32)
    grad_down = ffn[:, :, :PART].transpose(0, 2, 1).reshape(n_ffn * PART, width)
    grad_gate = ffn[:, :, PART : 2 * PART].transpose(1, 0, 2).reshape(width, n_ffn * PART)
    grad_up = ffn[:, :, 2 * PART :].transpose(1, 0, 2).reshape(width, n_ffn * PART)
    small = sums[n_ffn:].transpose(1, 0, 2).reshape(width, -1).astype(f32)
    nq = heads * HEAD
    vec = small[:, 2 * nq + SLOT : 2 * nq + SLOT + 3].T
    gain = vec[0] + partner(vec[0], "tensor", 0)
    return (
        layer_out,
        input_grad,
        gain,
        small[:, nq : 2 * nq],
        vec[2, :nq],
        small[:, 2 * nq : 2 * nq + HEAD],
        vec[2, nq : nq + HEAD],
        small[:, 2 * nq + HEAD : 2 * nq + 2 * HEAD],
        vec[2, nq + HEAD : nq + 2 * HEAD],
        small[:, :nq].T,
        vec[1],
        grad_gate,
        grad_up,
        grad_down,
    )


def solution(mesh):
    rows = P(("batch", "blk", "tensor"), None)
    cols, part, split = P(None, "tensor"), P("tensor"), P("tensor", None)
    return jax.shard_map(
        shards,
        mesh=mesh,
        in_specs=(
            rows, rows, P("batch", None), P(), cols, part, cols, part, cols, part, split, P(),
            cols, cols, split,
        ),
        out_specs=(
            rows, rows, P(), cols, part, cols, part, cols, part, split, P(), cols, cols, split,
        ),
        check_vma=False,
    )
```

```python
import functools
import math

import jax
import jax.numpy as jnp
import numpy as np
from jax import lax
from jax.experimental import pallas as pl
from jax.experimental.pallas import tpu as pltpu
from jax.sharding import PartitionSpec as P

HEAD = 64
SLOT = 128

rope_base = 1000000.0
norm_eps = 1e-06
masked_value = -1e30
bf16 = jnp.bfloat16
f32 = jnp.float32


def dot(left, right, dims, kind=f32):
    return lax.dot_general(left, right, (dims, ((), ())), preferred_element_type=kind)


NN = ((1,), (0,))
NT = ((1,), (1,))
TN = ((0,), (0,))


def bits_of(mesh_axis):
    return [(mesh_axis, bit) for bit in range(int(math.log2(lax.axis_size(mesh_axis))))]


def rotary_table(count):
    half = HEAD // 2
    freq = np.float32(rope_base) ** (-(np.arange(half, dtype=np.float32) * np.float32(2.0)) / np.float32(HEAD))
    phase = np.arange(count, dtype=np.float32)[:, None] * freq[None, :].astype(np.float32)
    phase = phase.astype(np.float64)
    return np.concatenate([np.cos(phase), np.sin(phase)], 1).astype(np.float32)


def spread_table(table):
    n = table.shape[0]
    wide = jnp.concatenate([table, jnp.zeros_like(table)], 1)
    lane = lax.broadcasted_iota(jnp.int32, (n, SLOT), 1)
    cosine = jnp.where(lane < 32, wide, jnp.where(lane < HEAD, pltpu.roll(wide, 32, 1), 1.0))
    sine_a = jnp.where(lane < 32, pltpu.roll(wide, SLOT - 32, 1), 0.0)
    sine_b = jnp.where((lane >= 32) & (lane < HEAD), wide, 0.0)
    return cosine, sine_a, sine_b


def turn(v, table, sign):
    cosine, sine_a, sine_b = table
    return v * cosine + sign * (
        pltpu.roll(v, 32, 1) * sine_b - pltpu.roll(v, SLOT - 32, 1) * sine_a
    )


def meet(peers):
    barrier = pltpu.get_barrier_semaphore()
    for peer in peers:
        pl.semaphore_signal(barrier, 1, device_id=peer, device_id_type=pl.DeviceIdType.MESH)
    pl.semaphore_wait(barrier, len(peers))


def remote(src, dst, send, recv, peer):
    return pltpu.make_async_remote_copy(
        src_ref=src, dst_ref=dst, send_sem=send, recv_sem=recv,
        device_id=peer, device_id_type=pl.DeviceIdType.MESH,
    )


ONES = 72
FRONT_IN = ("own_in", "own_cot", "wq", "wk", "wv", "bq", "bk", "bv", "gain", "table")
FRONT_OUT = ("x", "cot", "normed", "q", "kv", "ctx", "ctx_o", "slots", "lse")


def front_kernel(heads, length_ref, *refs):
    ni, no = len(FRONT_IN), len(FRONT_OUT)
    hbm = dict(zip(FRONT_IN, refs[:ni]))
    out = dict(zip(FRONT_OUT, refs[ni : ni + no]))
    m = dict(zip(FRONT_OUT, refs[ni + no : ni + 2 * no]))
    (
        wq, wk, wv, bq, bk, bv, gain, table, q1, k1, vt1, m_s, acc_s,
        load_sem, out_sem, pair_send, pair_recv, kv_send, kv_recv,
    ) = refs[ni + 2 * no :]
    w = dict(zip(FRONT_IN[2:], (wq, wk, wv, bq, bk, bv, gain, table)))
    rows, width = m["x"].shape
    half = rows // 2
    blk, nb = lax.axis_index("blk"), lax.axis_size("blk")
    core = lax.axis_index("tensor")
    other = {"tensor": 1 - core}
    ours = pl.multiple_of(core * half, 16)
    theirs = pl.multiple_of((1 - core) * half, 16)
    start = blk * rows
    length = length_ref[0, 0]
    tile, tk = 256, 512

    loads = [
        pltpu.make_async_copy(hbm["own_in"], m["x"].at[pl.ds(ours, half), :], load_sem.at[0]),
        pltpu.make_async_copy(hbm["own_cot"], m["cot"].at[pl.ds(ours, half), :], load_sem.at[1]),
    ] + [
        pltpu.make_async_copy(hbm[name], w[name], load_sem.at[2 + i])
        for i, name in enumerate(FRONT_IN[2:])
    ]
    for copy in loads:
        copy.start()
    meet([other] + [{"blk": lax.rem(blk + d, nb)} for d in range(1, nb)])

    def swap(k, src, dst):
        return remote(src, dst, pair_send.at[k], pair_recv.at[k], other)

    def x_swap():
        return swap(0, hbm["own_in"], m["x"].at[pl.ds(ours, half), :])

    def cot_swap():
        return swap(1, hbm["own_cot"], m["cot"].at[pl.ds(ours, half), :])

    def ctx_swap():
        return swap(2, m["ctx"], m["ctx_o"])

    def save(name):
        i = FRONT_OUT.index(name)
        return pltpu.make_async_copy(m[name], out[name], out_sem.at[i])

    x_swap().start()
    cot_swap().start()
    loads[0].wait()
    for copy in loads[2:]:
        copy.wait()
    lane = lax.broadcasted_iota(jnp.int32, (tile, SLOT), 1)

    def rows_in(first):
        def step(r, _):
            at = pl.ds(pl.multiple_of(first + r * tile, tile), tile)
            x = m["x"][at, :].astype(f32)
            rho = lax.rsqrt(jnp.mean(x * x, axis=1, keepdims=True) + norm_eps)
            normed = (x * rho * gain[...]).astype(bf16)
            m["normed"][at, :] = normed
            factors = spread_table(table[at, :])
            proj = dot(normed, wq[...], NN) + bq[...].astype(f32)
            zero = jnp.zeros((tile, HEAD), f32)
            for h in range(heads):
                cols = slice(h * SLOT, (h + 1) * SLOT)
                v = jnp.concatenate([proj[:, h * HEAD : (h + 1) * HEAD], zero], 1)
                v = turn(v, factors, 1.0).astype(bf16).astype(f32) * HEAD**-0.5
                m["q"][at, cols] = v.astype(bf16)
                q1[at, cols] = jnp.where(lane == HEAD, 1.0, v).astype(bf16)
            kv = jnp.concatenate(
                [
                    dot(normed, wk[...], NN) + bk[...].astype(f32),
                    dot(normed, wv[...], NN) + bv[...].astype(f32),
                ],
                1,
            )
            at_b = pl.ds(pl.multiple_of(start + first + r * tile, tile), tile)
            m["kv"][at_b, :] = turn(kv, factors, 1.0).astype(bf16)
            return 0

        lax.fori_loop(0, half // tile, step, 0)

    rows_in(ours)
    x_swap().wait()
    rows_in(theirs)

    def kv_copy(d):
        at = pl.ds(pl.multiple_of(blk * rows, rows), rows)
        return remote(
            m["kv"].at[at, :], m["kv"].at[at, :], kv_send.at[d - 1], kv_recv.at[d - 1],
            {"blk": lax.rem(blk + d, nb)},
        )

    for d in range(1, nb):
        @pl.when(blk + d < nb)
        def _(d=d):
            kv_copy(d).start()

    save("x").start()
    save("normed").start()
    save("q").start()
    wide_lane = lax.broadcasted_iota(jnp.int32, (tk, SLOT), 1)
    wide_row = lax.broadcasted_iota(jnp.int32, (tk, SLOT), 0)

    def prepare(first):
        at = pl.ds(pl.multiple_of(first, tk), tk)
        kv = m["kv"][at, :].astype(f32)
        dead = jnp.where(wide_row + first < length, 0.0, masked_value)
        k1[at, :] = jnp.where(
            wide_lane < HEAD, kv, jnp.where(wide_lane == HEAD, dead, 0.0)
        ).astype(bf16)
        vt1[0:HEAD, at] = jnp.transpose(kv)[HEAD:, :].astype(bf16)
        vt1[HEAD:, at] = jnp.ones((ONES - HEAD, tk), bf16)
        return at

    def attend(first, q0, diagonal):
        at = prepare(first)
        kt, vt = k1[at, :], vt1[:, at]
        n = rows - q0
        qs = slice(q0, rows)

        def score(h):
            s = dot(kt, q1[qs, h * SLOT : (h + 1) * SLOT], NT)
            if diagonal:
                ki = lax.broadcasted_iota(jnp.int32, (tk, n), 0)
                qi = lax.broadcasted_iota(jnp.int32, (tk, n), 1)
                s = jnp.where(ki <= qi, s, masked_value)
            return s

        def add(h, p, alpha):
            acc_s[h, :, qs] = acc_s[h, :, qs] * alpha + dot(vt, p, NN)

        ahead, behind = score(0), None
        for h in range(heads):
            s = ahead
            if h + 1 < heads:
                ahead = score(h + 1)
            m_prev = m_s[h : h + 1, qs]
            m_new = jnp.maximum(m_prev, jnp.max(s, axis=0, keepdims=True))
            alpha = jnp.exp(m_prev - m_new)
            p = jnp.exp(s - m_new).astype(bf16)
            m_s[h : h + 1, qs] = m_new
            if behind is not None:
                add(*behind)
            behind = (h, p, alpha)
        add(*behind)

    m_s[...] = jnp.full(m_s.shape, masked_value, f32)
    acc_s[...] = jnp.zeros(acc_s.shape, f32)
    for e in range(rows // tk):
        attend(start + e * tk, e * tk, True)

    def block(d, _):
        src = blk - d
        at = pl.ds(pl.multiple_of(src * rows, rows), rows)
        remote(
            m["kv"].at[at, :], m["kv"].at[at, :], kv_send.at[d - 1], kv_recv.at[d - 1],
            {"blk": src},
        ).wait_recv()

        def key_tile(i, _):
            attend(src * rows + i * tk, 0, False)
            return 0

        lax.fori_loop(0, rows // tk, key_tile, 0)
        return 0

    lax.fori_loop(1, blk + 1, block, 0)
    pos = lax.broadcasted_iota(jnp.int32, (1, rows), 1) + start
    zero = jnp.zeros((HEAD, rows), f32)
    for h in range(heads):
        acc = acc_s[h]
        total = acc[HEAD : HEAD + 1, :]
        ctx = jnp.transpose(jnp.concatenate([zero, acc[:HEAD] / total], 0))
        m["slots"][:, h * SLOT : (h + 1) * SLOT] = ctx.astype(bf16)
        m["ctx"][:, h * HEAD : (h + 1) * HEAD] = ctx[:, HEAD:].astype(bf16)
        m["lse"][h : h + 1, :] = jnp.where(
            pos < length, m_s[h : h + 1, :] + jnp.log(total), -masked_value
        )
    m["lse"][heads:, :] = jnp.zeros((8 - heads, rows), f32)
    ctx_swap().start()
    save("ctx").start()
    save("slots").start()
    save("lse").start()

    def kv_save(b):
        at = pl.ds(pl.multiple_of(b * rows, rows), rows)
        return pltpu.make_async_copy(
            m["kv"].at[at, :], out["kv"].at[at, :], out_sem.at[FRONT_OUT.index("kv")]
        )

    def keep_kv(b, _):
        kv_save(b).start()
        kv_save(b).wait()
        return 0

    loads[1].wait()
    cot_swap().wait()

    def mask(r, _):
        at = pl.ds(pl.multiple_of(r * tile, tile), tile)
        row = lax.broadcasted_iota(jnp.int32, (tile, width), 0) + start + r * tile
        m["cot"][at, :] = jnp.where(row < length, m["cot"][at, :].astype(f32), 0.0).astype(bf16)
        return 0

    lax.fori_loop(0, rows // tile, mask, 0)
    save("cot").start()
    lax.fori_loop(0, blk + 1, keep_kv, 0)
    for d in range(1, nb):
        @pl.when(blk + d < nb)
        def _(d=d):
            kv_copy(d).wait_send()

    ctx_swap().wait()
    save("ctx_o").start()
    for name in FRONT_OUT:
        if name != "kv":
            save(name).wait()


def front(length, values, heads, nb):
    half, width = values["own_in"].shape
    rows = 2 * half
    keys = rows * nb
    shape = jax.ShapeDtypeStruct
    outs = dict(
        x=shape((rows, width), bf16),
        cot=shape((rows, width), bf16),
        normed=shape((rows, width), bf16),
        q=shape((rows, heads * SLOT), bf16),
        kv=shape((keys, SLOT), bf16),
        ctx=shape((rows, heads * HEAD), bf16),
        ctx_o=shape((rows, heads * HEAD), bf16),
        slots=shape((rows, heads * SLOT), bf16),
        lse=shape((8, rows), f32),
    )
    hbm = pl.BlockSpec(memory_space=pl.ANY)
    dma = pltpu.SemaphoreType.DMA
    vm = lambda a: pltpu.VMEM(a.shape, a.dtype)
    results = pl.pallas_call(
        functools.partial(front_kernel, heads),
        out_shape=[outs[name] for name in FRONT_OUT],
        in_specs=[pl.BlockSpec(memory_space=pltpu.SMEM)] + [hbm] * len(FRONT_IN),
        out_specs=[hbm] * len(FRONT_OUT),
        scratch_shapes=[vm(outs[name]) for name in FRONT_OUT]
        + [vm(values[name]) for name in FRONT_IN[2:]]
        + [
            pltpu.VMEM((rows, heads * SLOT), bf16),
            pltpu.VMEM((keys, SLOT), bf16),
            pltpu.VMEM((ONES, keys), bf16),
            pltpu.VMEM((8, rows), f32),
            pltpu.VMEM((heads, ONES, rows), f32),
            dma((len(FRONT_IN),)),
            dma((len(FRONT_OUT),)),
            dma((3,)),
            dma((3,)),
            dma((nb - 1,)),
            dma((nb - 1,)),
        ],
        compiler_params=pltpu.CompilerParams(
            collective_id=1, has_side_effects=True, vmem_limit_bytes=58 * 2**20
        ),
        name="front",
    )(length, *[values[name] for name in FRONT_IN])
    return dict(zip(FRONT_OUT, results))


PART = 128


def ffn_kernel(
    x_ref, ctx_ref, ctx_o_ref, wo_ref, wo_o_ref, gain_ref, cot_ref, wg_ref, wu_ref, wd_ref,
    resid_ref, g_ref, dmid_ref, out_ref, mlp, mlp_t, cot_t, trio, dmid_s, out_s,
):
    step = pl.program_id(0)
    rows = x_ref.shape[0]
    tile = 256

    @pl.when(step == 0)
    def _():
        def first(r, _):
            at = pl.ds(pl.multiple_of(r * tile, tile), tile)
            resid = (
                x_ref[at, :].astype(f32)
                + dot(ctx_ref[at, :], wo_ref[...], NN)
                + dot(ctx_o_ref[at, :], wo_o_ref[...], NN)
            )
            resid_ref[at, :] = resid
            rho = lax.rsqrt(jnp.mean(resid * resid, axis=1, keepdims=True) + norm_eps)
            normed = resid * rho * gain_ref[...]
            mlp[at, :] = normed.astype(bf16)
            mlp_t[:, at] = jnp.transpose(normed).astype(bf16)
            cot_t[:, at] = jnp.transpose(cot_ref[at, :].astype(f32)).astype(bf16)
            return 0

        lax.fori_loop(0, rows // tile, first, 0)
        dmid_s[...] = jnp.zeros(dmid_s.shape, f32)
        out_s[...] = jnp.zeros(out_s.shape, f32)

    pair = jnp.concatenate([wg_ref[...], wu_ref[...]], 1)
    down = wd_ref[...]
    for r in range(rows // tile):
        at = slice(r * tile, (r + 1) * tile)
        both = dot(mlp[at, :], pair, NN)
        gate, upper = both[:, :PART], both[:, PART:]
        d_hidden = dot(cot_ref[at, :], down, NT)
        sigma = 1.0 / (1.0 + jnp.exp(-gate))
        activ = gate * sigma
        hidden = (activ * upper).astype(bf16)
        d_gate = (d_hidden * upper * sigma * (1.0 + gate * (1.0 - sigma))).astype(bf16)
        d_up = (d_hidden * activ).astype(bf16)
        d_pair = jnp.concatenate([d_gate, d_up], 1)
        trio[at, :PART] = hidden
        trio[at, PART:] = d_pair
        out_s[at, :] += dot(hidden, down, NN)
        dmid_s[at, :] += dot(d_pair, pair, NT)
    g_ref[0, :, :PART] = dot(cot_t[...], trio[:, :PART], NN).astype(bf16)
    g_ref[0, :, PART:] = dot(mlp_t[...], trio[:, PART:], NN).astype(bf16)

    @pl.when(step == pl.num_programs(0) - 1)
    def _():
        dmid_ref[...] = dmid_s[...].astype(bf16)
        out_ref[...] = out_s[...].astype(bf16)


def feed_forward(x, ctx, ctx_o, w_out, w_out_o, gain, cot, w_gate, w_up, w_down):
    rows, width = x.shape
    hidden = w_gate.shape[1]
    steps = hidden // PART
    whole = lambda a: pl.BlockSpec(a.shape, lambda j: (0,) * a.ndim)
    row_block = pl.BlockSpec((rows, width), lambda j: (0, 0))
    return pl.pallas_call(
        ffn_kernel,
        grid=(steps,),
        out_shape=(
            jax.ShapeDtypeStruct((rows, width), f32),
            jax.ShapeDtypeStruct((steps, width, 3 * PART), bf16),
            jax.ShapeDtypeStruct((rows, width), bf16),
            jax.ShapeDtypeStruct((rows, width), bf16),
        ),
        in_specs=[
            whole(x), whole(ctx), whole(ctx_o), whole(w_out), whole(w_out_o), whole(gain),
            whole(cot),
            pl.BlockSpec((width, PART), lambda j: (0, j)),
            pl.BlockSpec((width, PART), lambda j: (0, j)),
            pl.BlockSpec((PART, width), lambda j: (j, 0)),
        ],
        out_specs=(
            row_block,
            pl.BlockSpec((1, width, 3 * PART), lambda j: (j, 0, 0)),
            row_block,
            row_block,
        ),
        scratch_shapes=[
            pltpu.VMEM((rows, width), bf16),
            pltpu.VMEM((width, rows), bf16),
            pltpu.VMEM((width, rows), bf16),
            pltpu.VMEM((rows, 3 * PART), bf16),
            pltpu.VMEM((rows, width), f32),
            pltpu.VMEM((rows, width), f32),
        ],
        compiler_params=pltpu.CompilerParams(
            vmem_limit_bytes=56 * 2**20, dimension_semantics=("arbitrary",)
        ),
        name="ffn",
    )(x, ctx, ctx_o, w_out, w_out_o, gain, cot, w_gate, w_up, w_down)


RING = 4
CHUNK = 3 * PART


class Stream:
    def __init__(self, first, count, axes):
        self.first, self.count = first, count
        self.reduce, self.sizes = [], []
        size = count
        for axis, bit in axes:
            half = size % 32 == 0
            size = size // 2 if half else size
            self.reduce.append((half, axis, bit))
            self.sizes.append(size)
        self.gather = [(axis, bit) for half, axis, bit in reversed(self.reduce) if half]
        self.stages = len(self.reduce) + len(self.gather) + 1

    def scratch(self):
        copies = len(self.reduce) + len(self.gather)
        return [pltpu.VMEM((RING, self.sizes[0], CHUNK), bf16)] + [
            pltpu.VMEM((RING, size, CHUNK), bf16) for size in self.sizes
        ] + [
            pltpu.SemaphoreType.DMA((copies, RING)),
            pltpu.SemaphoreType.DMA((copies, RING)),
            pltpu.SemaphoreType.DMA((2, RING)),
        ]

    def bind(self, refs, sources, out):
        n = len(self.reduce)
        self.keep, self.got = refs[0], refs[1 : n + 1]
        self.send, self.recv, self.local = refs[n + 1 :]
        self.sources, self.out = sources, out
        self.peer, self.mine, offset = [], [], self.first
        self.offsets = []
        for (half, axis, bit), size in zip(self.reduce, self.sizes):
            at = lax.axis_index(axis)
            one = lax.rem(at // (1 << bit), 2)
            self.peer.append({axis: at + (1 - 2 * one) * (1 << bit)})
            self.mine.append(one)
            offset = offset + one * size if half else offset
            self.offsets.append(offset)
        self.whole = []
        offset, size = self.offsets[-1], self.sizes[-1]
        self.gather_peer = []
        for k in reversed(range(n)):
            half = self.reduce[k][0]
            if half:
                self.whole.append((offset, size))
                self.gather_peer.append(self.peer[k])
                offset, size = offset - self.mine[k] * size, 2 * size

    def copy(self, k, ring, src, dst, peer):
        return pltpu.make_async_remote_copy(
            src_ref=src,
            dst_ref=dst,
            send_sem=self.send.at[k, ring],
            recv_sem=self.recv.at[k, ring],
            device_id=peer,
            device_id_type=pl.DeviceIdType.MESH,
        )

    def start_first(self, ring, source):
        size, one = self.sizes[0], self.mine[0]
        theirs = pl.multiple_of(self.first + (1 - one) * size, 16)
        own = pl.multiple_of(self.first + one * size, 16)
        self.copy(
            0, ring, source.at[pl.ds(theirs, size), :], self.got[0].at[ring], self.peer[0]
        ).start()
        pltpu.make_async_copy(
            source.at[pl.ds(own, size), :], self.keep.at[ring], self.local.at[0, ring]
        ).start()

    def reduce_copy(self, k, ring):
        if k == 0:
            src = self.keep.at[ring]
        elif self.reduce[k][0]:
            size = self.sizes[k]
            theirs = pl.multiple_of((1 - self.mine[k]) * size, 16)
            src = self.got[k - 1].at[ring, pl.ds(theirs, size), :]
        else:
            src = self.got[k - 1].at[ring]
        return self.copy(k, ring, src, self.got[k].at[ring], self.peer[k])

    def gather_copy(self, t, ring, chunk):
        offset, size = self.whole[t]
        rows = pl.ds(pl.multiple_of(offset, 16), size)
        place = self.out.at[chunk, rows, :]
        src = self.got[-1].at[ring] if t == 0 else place
        return self.copy(len(self.reduce) + t, ring, src, place, self.gather_peer[t])

    def own_copy(self, ring, chunk):
        offset, size = self.whole[0]
        rows = pl.ds(pl.multiple_of(offset, 16), size)
        return pltpu.make_async_copy(
            self.got[-1].at[ring], self.out.at[chunk, rows, :], self.local.at[1, ring]
        )

    def stage(self, s, chunk):
        ring = lax.rem(chunk, RING)
        n = len(self.reduce)
        if s == 0:
            base = 0
            for count, place in self.sources:
                @pl.when((chunk >= base) & (chunk < base + count))
                def _(base=base, place=place):
                    self.start_first(ring, place(chunk - base))

                base += count
            return
        if s <= n:
            k = s - 1
            if k == 0:
                pltpu.make_async_copy(
                    self.got[0].at[ring], self.keep.at[ring], self.local.at[0, ring]
                ).wait()
            self.reduce_copy(k, ring).wait()
            size = self.sizes[k]
            if k == 0:
                own = self.keep[ring]
            elif self.reduce[k][0]:
                own = self.got[k - 1][ring, pl.ds(pl.multiple_of(self.mine[k] * size, 16), size), :]
            else:
                own = self.got[k - 1][ring]
            total = own.astype(f32) + self.got[k][ring].astype(f32)
            self.got[k][ring] = total.astype(bf16)
            if s < n:
                self.reduce_copy(s, ring).start()
            else:
                self.own_copy(ring, chunk).start()
                self.gather_copy(0, ring, chunk).start()
            return
        t = s - n - 1
        self.gather_copy(t, ring, chunk).wait()
        if t == 0:
            self.own_copy(ring, chunk).wait()
        if t + 1 < len(self.gather):
            self.gather_copy(t + 1, ring, chunk).start()


def make_streams(width, plane, line):
    unit = width // 7
    return [
        Stream(0, 3 * unit, plane + line),
        Stream(3 * unit, 3 * unit, plane[::-1] + line),
        Stream(6 * unit, unit, line + plane),
    ]


LOADS = (
    "dmid", "resid", "cot", "w_out", "ctx", "slots", "q", "kv", "lse",
    "table", "normed", "wq", "wk", "wv", "own_in", "gain1", "gain2", "part",
)


def backward_kernel(heads, streams, n_ffn, n_small, *refs):
    nl = len(LOADS)
    hbm = dict(zip(LOADS, refs[:nl]))
    grads_ref = refs[nl]
    sums_ref, layer_out_ref, input_grad_ref = refs[nl + 1 : nl + 4]
    refs = list(refs[nl + 4 :])
    m = dict(zip(LOADS, refs[:nl]))
    refs = refs[nl:]
    (
        load_sem, dmid_o, part_o, do, dlow, delta, dq, dkv, dkv_o, k0, dproj, small,
        din_send, din_own, din_o, rowsum, vec, pair_send, pair_recv, kv_send, kv_recv, out_sem,
        w_slots, gain_own, gain_o,
    ) = refs[:25]
    refs = refs[25:]
    rows, width = m["cot"].shape
    half = rows // 2
    blk, nb = lax.axis_index("blk"), lax.axis_size("blk")
    core = lax.axis_index("tensor")
    nz = lax.axis_size("batch")
    other = {"tensor": 1 - core}
    tile = 256

    pos = 0
    for st in streams:
        cnt = len(st.scratch())
        st.bind(
            refs[pos : pos + cnt],
            [(n_ffn, lambda c: grads_ref.at[c]), (n_small, lambda c: small.at[c])],
            sums_ref,
        )
        pos += cnt

    loads = {
        name: pltpu.make_async_copy(hbm[name], m[name], load_sem.at[i])
        for i, name in enumerate(LOADS)
    }
    for copy in loads.values():
        copy.start()

    batch = lax.axis_index("batch")
    meet(
        [other]
        + [{"blk": lax.rem(blk + d, nb)} for d in range(1, nb)]
        + [
            {"batch": batch + (1 - 2 * lax.rem(batch // (1 << b), 2)) * (1 << b)}
            for b in range(int(math.log2(nz)))
        ]
    )

    def swap(k, src, dst):
        return remote(src, dst, pair_send.at[k], pair_recv.at[k], other)

    def dmid_swap():
        return swap(0, hbm["dmid"], dmid_o)

    theirs = pl.multiple_of((1 - core) * half, 16)
    ours = pl.multiple_of(core * half, 16)

    def part_swap():
        return swap(1, hbm["part"].at[pl.ds(theirs, half), :], part_o)

    def din_swap():
        return swap(2, din_send, din_o)

    def gain_swap():
        return swap(3, gain_own, gain_o)

    dmid_swap().start()
    part_swap().start()

    def put(first, at, value):
        done, n = 0, value.shape[1]
        while done < n:
            c, lane = divmod(first + done, CHUNK)
            take = min(n - done, CHUNK - lane)
            small[c, at, lane : lane + take] = value[:, done : done + take].astype(bf16)
            done += take

    nq = heads * HEAD
    tq, tk = 256, 512

    def before():
        for name in LOADS:
            if name != "part":
                loads[name].wait()
        loads["part"].wait()
        dmid_swap().wait()
        part_swap().wait()
        vec[...] = jnp.zeros(vec.shape, f32)
        w_slots[...] = jnp.zeros(w_slots.shape, bf16)
        for h in range(heads):
            w_slots[h * SLOT + HEAD : (h + 1) * SLOT, :] = m["w_out"][h * HEAD : (h + 1) * HEAD, :]

        def out_rows(r, _):
            at = pl.ds(pl.multiple_of(r * tile, tile), tile)
            mine = pl.ds(pl.multiple_of(ours + r * tile, tile), tile)
            part_o[at, :] = (
                m["resid"][mine, :] + m["part"][mine, :].astype(f32) + part_o[at, :].astype(f32)
            ).astype(bf16)
            return 0

        lax.fori_loop(0, half // tile, out_rows, 0)
        pltpu.make_async_copy(part_o, layer_out_ref, out_sem.at[0]).start()

        def norm(r, _):
            at = pl.ds(pl.multiple_of(r * tile, tile), tile)
            dmid = m["dmid"][at, :].astype(f32) + dmid_o[at, :].astype(f32)
            resid = m["resid"][at, :]
            rho = lax.rsqrt(jnp.mean(resid * resid, axis=1, keepdims=True) + norm_eps)
            n2 = resid * rho
            vec[1:2, :] += jnp.sum(dmid * n2, axis=0, keepdims=True)
            weighted = dmid * m["gain2"][...]
            d_resid = m["cot"][at, :].astype(f32) + rho * (
                weighted - n2 * jnp.mean(weighted * n2, axis=1, keepdims=True)
            )
            m["resid"][at, :] = d_resid
            low = d_resid.astype(bf16)
            dlow[at, :] = low
            d_ctx = dot(low, w_slots[...], NT)
            do[at, :] = d_ctx.astype(bf16)
            for h in range(heads):
                cols = slice(h * SLOT, (h + 1) * SLOT)
                prod = do[at, cols].astype(f32) * m["slots"][at, cols].astype(f32)
                col = jnp.sum(prod, axis=1, keepdims=True)
                wide = jnp.transpose(jnp.broadcast_to(col, (tile, SLOT)))
                delta[h : h + 1, at] = wide[0:1, :]
            return 0

        lax.fori_loop(0, rows // tile, norm, 0)

        def grad_out(k, _):
            at = pl.ds(pl.multiple_of(k * 128, 128), 128)
            put(0, at, dot(dlow[:, at], m["ctx"][...], TN))
            return 0

        lax.fori_loop(0, width // 128, grad_out, 0)
        lane = lax.broadcasted_iota(jnp.int32, (tk, SLOT), 1)

        def keys(i, _):
            at = pl.ds(pl.multiple_of(i * tk, tk), tk)
            k0[at, :] = jnp.where(lane < HEAD, m["kv"][at, :].astype(f32), 0.0).astype(bf16)
            return 0

        lax.fori_loop(0, (blk + 1) * (rows // tk), keys, 0)
        dq[...] = jnp.zeros(dq.shape, f32)

    def pair(kt, kvt, qt, masked):
        at = pl.ds(pl.multiple_of(qt * tq, tq), tq)

        def score(h):
            cols = slice(h * SLOT, (h + 1) * SLOT)
            return dot(kt, m["q"][at, cols], NT), dot(kvt, do[at, cols], NT)

        def add(h, p, ds):
            cols = slice(h * SLOT, (h + 1) * SLOT)
            dq[at, cols] += dot(ds, kt, TN)
            return dot(ds, m["q"][at, cols], NN) + dot(p, do[at, cols], NN)

        grad, ahead, behind = None, score(0), None
        for h in range(heads):
            s, dp = ahead
            if h + 1 < heads:
                ahead = score(h + 1)
            p = jnp.exp(s - m["lse"][h : h + 1, at])
            if masked is not None:
                p = jnp.where(masked, p, 0.0)
            ds = (p * (dp - delta[h : h + 1, at])).astype(bf16)
            if behind is not None:
                part = add(*behind)
                grad = part if grad is None else grad + part
            behind = (h, p.astype(bf16), ds)
        return grad + add(*behind)

    def own_block():
        ki = lax.broadcasted_iota(jnp.int32, (tk, tq), 0)
        qi = lax.broadcasted_iota(jnp.int32, (tk, tq), 1)

        def key_tile(i, _):
            at_k = pl.ds(pl.multiple_of(blk * rows + i * tk, tk), tk)
            kt, kvt = k0[at_k, :], m["kv"][at_k, :]
            first = i * (tk // tq)

            def near(j, grad):
                return grad + pair(kt, kvt, first + j, ki <= qi + j * tq)

            def far(qt, grad):
                return grad + pair(kt, kvt, qt, None)

            grad = lax.fori_loop(0, tk // tq, near, jnp.zeros((tk, SLOT), f32))
            grad = lax.fori_loop(first + tk // tq, rows // tq, far, grad)
            dkv[at_k, :] = grad.astype(bf16)
            return 0

        lax.fori_loop(0, rows // tk, key_tile, 0)

    def earlier(i):
        at_k = pl.ds(pl.multiple_of(i * tk, tk), tk)
        kt, kvt = k0[at_k, :], m["kv"][at_k, :]

        def step(qt, grad):
            return grad + pair(kt, kvt, qt, None)

        grad = lax.fori_loop(0, rows // tq, step, jnp.zeros((tk, SLOT), f32))
        dkv[at_k, :] = grad.astype(bf16)

    def kv_copy(d):
        to = lax.rem(blk + d, nb)
        at = pl.ds(pl.multiple_of(to * rows, rows), rows)
        return remote(
            dkv.at[at, :], dkv_o.at[d - 1], kv_send.at[d - 1], kv_recv.at[d - 1], {"blk": to}
        )

    def kv_start():
        for d in range(1, nb):
            @pl.when(lax.rem(blk + d, nb) < blk)
            def _(d=d):
                kv_copy(d).start()

    def project():
        for d in range(1, nb):
            @pl.when(lax.rem(blk + d, nb) < blk)
            def _(d=d):
                kv_copy(d).wait_send()

            @pl.when(lax.rem(blk + nb - d, nb) > blk)
            def _(d=d):
                kv_copy(d).wait_recv()
                for r in range(rows // tile):
                    at = pl.ds(pl.multiple_of(blk * rows + r * tile, tile), tile)
                    total = dkv[at, :].astype(f32) + dkv_o[d - 1, r * tile : (r + 1) * tile].astype(f32)
                    dkv[at, :] = total.astype(bf16)

        rowsum[...] = jnp.zeros(rowsum.shape, f32)

        def unrotate(r, _):
            at = pl.ds(pl.multiple_of(r * tile, tile), tile)
            at_b = pl.ds(pl.multiple_of(blk * rows + r * tile, tile), tile)
            table = spread_table(m["table"][at, :])
            for h in range(heads):
                v = turn(dq[at, h * SLOT : (h + 1) * SLOT] * HEAD**-0.5, table, -1.0)
                dproj[at, h * HEAD : (h + 1) * HEAD] = v[:, :HEAD].astype(bf16)
            dproj[at, nq:] = turn(dkv[at_b, :].astype(f32), table, -1.0).astype(bf16)
            rowsum[0:1, :] += jnp.sum(dproj[at, :].astype(f32), axis=0, keepdims=True)
            return 0

        lax.fori_loop(0, rows // tile, unrotate, 0)

        def d_in(to, first):
            def step(r, _):
                src = pl.ds(pl.multiple_of(first + r * tile, tile), tile)
                at = pl.ds(pl.multiple_of(r * tile, tile), tile)
                to[at, :] = (
                    dot(dproj[src, :nq], m["wq"][...], NT)
                    + dot(dproj[src, nq : nq + HEAD], m["wk"][...], NT)
                    + dot(dproj[src, nq + HEAD :], m["wv"][...], NT)
                ).astype(bf16)
                return 0

            lax.fori_loop(0, half // tile, step, 0)

        d_in(din_send, theirs)
        din_swap().start()
        d_in(din_own, ours)

        def grads(k, _):
            at = pl.ds(pl.multiple_of(k * 128, 128), 128)
            put(nq, at, dot(m["normed"][:, at], dproj[...], TN))
            return 0

        lax.fori_loop(0, width // 128, grads, 0)

    def finish():
        din_swap().wait()

        def step(r, _):
            at = pl.ds(pl.multiple_of(r * tile, tile), tile)
            mine = pl.ds(pl.multiple_of(ours + r * tile, tile), tile)
            d_in = din_own[at, :].astype(f32) + din_o[at, :].astype(f32)
            x = m["own_in"][at, :].astype(f32)
            rho = lax.rsqrt(jnp.mean(x * x, axis=1, keepdims=True) + norm_eps)
            n1 = x * rho
            vec[0:1, :] += jnp.sum(d_in * n1, axis=0, keepdims=True)
            weighted = d_in * m["gain1"][...]
            grad = m["resid"][mine, :] + rho * (
                weighted - n1 * jnp.mean(weighted * n1, axis=1, keepdims=True)
            )
            din_own[at, :] = grad.astype(bf16)
            return 0

        lax.fori_loop(0, half // tile, step, 0)
        pltpu.make_async_copy(din_own, input_grad_ref, out_sem.at[1]).start()
        gain_own[...] = vec[0:8, :]
        gain_swap().start()
        vec[2:3, : nq + SLOT] = rowsum[0:1, :]
        gain_swap().wait()
        vec[0:1, :] = gain_own[0:1, :] + gain_o[0:1, :]
        put(2 * nq + SLOT, slice(None), jnp.transpose(vec[...]))

    n_attn = 2 + (nb - 1) * (rows // tk)

    def compute(i):
        pl.when(i == 0)(before)
        pl.when(i == 1)(own_block)

        @pl.when((i >= 2) & (i - 2 < blk * (rows // tk)))
        def _():
            earlier(i - 2)

        pl.when(i == n_attn)(kv_start)
        pl.when(i == n_attn + 1)(project)
        pl.when(i == n_attn + 2)(finish)

    n = n_ffn + n_small
    depth = max(st.stages for st in streams)

    def slot(i, _):
        for st in streams:
            for s in reversed(range(st.stages)):
                @pl.when((i - s >= 0) & (i - s < n))
                def _(st=st, s=s):
                    st.stage(s, i - s)

        compute(i)
        return 0

    lax.fori_loop(0, n + depth - 1, slot, 0)
    pltpu.make_async_copy(part_o, layer_out_ref, out_sem.at[0]).wait()
    pltpu.make_async_copy(din_own, input_grad_ref, out_sem.at[1]).wait()


def backward(values, grads, heads, plane, line, nb):
    rows, width = values["cot"].shape
    half = rows // 2
    keys = values["kv"].shape[0]
    n_ffn = grads.shape[0]
    n_small = -(-(2 * heads * HEAD + 2 * SLOT) // CHUNK)
    assert n_ffn >= 5 + (nb - 1) * 2
    streams = make_streams(width, plane, line)
    hbm = pl.BlockSpec(memory_space=pl.ANY)
    dma = pltpu.SemaphoreType.DMA
    scratch = [pltpu.VMEM(values[name].shape, values[name].dtype) for name in LOADS]
    scratch += [
        dma((len(LOADS),)),
        pltpu.VMEM((rows, width), bf16),
        pltpu.VMEM((half, width), bf16),
        pltpu.VMEM((rows, heads * SLOT), bf16),
        pltpu.VMEM((rows, width), bf16),
        pltpu.VMEM((8, rows), f32),
        pltpu.VMEM((rows, heads * SLOT), f32),
        pltpu.VMEM((keys, SLOT), bf16),
        pltpu.VMEM((nb - 1, rows, SLOT), bf16),
        pltpu.VMEM((keys, SLOT), bf16),
        pltpu.VMEM((rows, heads * HEAD + SLOT), bf16),
        pltpu.VMEM((n_small, width, CHUNK), bf16),
        pltpu.VMEM((half, width), bf16),
        pltpu.VMEM((half, width), bf16),
        pltpu.VMEM((half, width), bf16),
        pltpu.VMEM((8, heads * HEAD + SLOT), f32),
        pltpu.VMEM((SLOT, width), f32),
        dma((4,)),
        dma((4,)),
        dma((nb - 1,)),
        dma((nb - 1,)),
        dma((2,)),
        pltpu.VMEM((heads * SLOT, width), bf16),
        pltpu.VMEM((8, width), f32),
        pltpu.VMEM((8, width), f32),
    ]
    for st in streams:
        scratch += st.scratch()
    return pl.pallas_call(
        functools.partial(backward_kernel, heads, streams, n_ffn, n_small),
        out_shape=(
            jax.ShapeDtypeStruct((n_ffn + n_small, width, CHUNK), bf16),
            jax.ShapeDtypeStruct((half, width), bf16),
            jax.ShapeDtypeStruct((half, width), bf16),
        ),
        in_specs=[hbm] * (len(LOADS) + 1),
        out_specs=(hbm, hbm, hbm),
        scratch_shapes=scratch,
        compiler_params=pltpu.CompilerParams(
            collective_id=0, has_side_effects=True, vmem_limit_bytes=60 * 2**20
        ),
        name="backward",
    )(*[values[name] for name in LOADS], grads)


def unpack_kernel(heads, n_small, chunk_ref, *refs):
    small, (down, gate, up, g_out, g_q, g_k, g_v, vec) = refs[:n_small], refs[n_small:]
    step = pl.program_id(0)
    value = chunk_ref[0]
    down[...] = jnp.transpose(value[:, :PART].astype(f32))
    gate[...] = value[:, PART : 2 * PART].astype(f32)
    up[...] = value[:, 2 * PART :].astype(f32)

    def take(first, count):
        done = 0
        while done < count:
            c, lane = divmod(first + done, CHUNK)
            n = min(count - done, SLOT - lane % SLOT)
            yield done, n, small[c][0, :, lane : lane + n].astype(f32)
            done += n

    @pl.when(step == 0)
    def _():
        nq = heads * HEAD
        for done, n, piece in take(0, nq):
            g_out[done : done + n, :] = jnp.transpose(piece)
        for done, n, piece in take(nq, nq):
            g_q[:, done : done + n] = piece
        for done, n, piece in take(2 * nq, HEAD):
            g_k[...] = piece
        for done, n, piece in take(2 * nq + HEAD, HEAD):
            g_v[...] = piece
        for done, n, piece in take(2 * nq + 2 * HEAD, SLOT):
            vec[...] = jnp.transpose(piece)[0:8, :]


def unpack(sums, n_ffn, heads):
    n, width, _ = sums.shape
    n_small = n - n_ffn
    shape = lambda *dims: jax.ShapeDtypeStruct(dims, f32)
    nq = heads * HEAD
    whole = [(nq, width), (width, nq), (width, HEAD), (width, HEAD), (8, width)]
    return pl.pallas_call(
        functools.partial(unpack_kernel, heads, n_small),
        grid=(n_ffn,),
        out_shape=[
            shape(n_ffn * PART, width), shape(width, n_ffn * PART), shape(width, n_ffn * PART)
        ] + [shape(*dims) for dims in whole],
        in_specs=[pl.BlockSpec((1, width, CHUNK), lambda j: (j, 0, 0))]
        + [
            pl.BlockSpec((1, width, CHUNK), lambda j, c=c: (n_ffn + c, 0, 0))
            for c in range(n_small)
        ],
        out_specs=[
            pl.BlockSpec((PART, width), lambda j: (j, 0)),
            pl.BlockSpec((width, PART), lambda j: (0, j)),
            pl.BlockSpec((width, PART), lambda j: (0, j)),
        ] + [pl.BlockSpec(dims, lambda j: (0, 0)) for dims in whole],
        compiler_params=pltpu.CompilerParams(
            vmem_limit_bytes=48 * 2**20, dimension_semantics=("arbitrary",)
        ),
        name="unpack",
    )(*[sums] * (1 + n_small))


def shards(
    layer_in, cotangent, lengths, attn_gain, w_query, query_bias, w_key, key_bias, w_value,
    value_bias, w_out, mlp_gain, w_gate, w_up, w_down,
):
    half, width = layer_in.shape
    rows = half * lax.axis_size("tensor")
    nb = lax.axis_size("blk")
    heads = w_query.shape[1] // HEAD
    tables = jnp.asarray(rotary_table(rows * nb)).reshape(nb, rows, HEAD)
    table = lax.dynamic_index_in_dim(tables, lax.axis_index("blk"), 0, keepdims=False)
    inputs = dict(
        own_in=layer_in, own_cot=cotangent, wq=w_query, wk=w_key, wv=w_value,
        bq=query_bias[None, :], bk=key_bias[None, :], bv=value_bias[None, :],
        gain=attn_gain[None, :], table=table,
    )
    w_out_o = lax.ppermute(w_out, "tensor", [(0, 1), (1, 0)])
    mid = front(lengths, inputs, heads, nb)
    resid, grads, dmid, part = feed_forward(
        mid["x"], mid["ctx"], mid["ctx_o"], w_out, w_out_o, mlp_gain[None, :], mid["cot"],
        w_gate, w_up, w_down,
    )
    values = dict(
        dmid=dmid, resid=resid, w_out=w_out, table=table, wq=w_query, wk=w_key, wv=w_value,
        own_in=layer_in, gain1=attn_gain[None, :], gain2=mlp_gain[None, :], part=part,
    )
    for name in ("cot", "ctx", "slots", "q", "kv", "lse", "normed"):
        values[name] = mid[name]
    sums, layer_out, input_grad = backward(
        values, grads, heads, bits_of("blk"), bits_of("batch"), nb
    )
    g_down, g_gate, g_up, g_out, g_query, g_key, g_value, vec = unpack(
        sums, grads.shape[0], heads
    )
    nq = heads * HEAD
    return (
        layer_out, input_grad, vec[0], g_query, vec[2, :nq], g_key, vec[2, nq : nq + HEAD],
        g_value, vec[2, nq + HEAD : nq + 2 * HEAD], g_out, vec[1], g_gate, g_up, g_down,
    )


def solution(mesh):
    rows = P(("batch", "blk", "tensor"), None)
    cols, part, split = P(None, "tensor"), P("tensor"), P("tensor", None)
    return jax.shard_map(
        shards,
        mesh=mesh,
        in_specs=(
            rows, rows, P("batch", None), P(), cols, part, cols, part, cols, part, split, P(),
            cols, cols, split,
        ),
        out_specs=(
            rows, rows, P(), cols, part, cols, part, cols, part, split, P(), cols, cols, split,
        ),
        check_vma=False,
    )
```

```python
import functools
import math

import jax
import jax.numpy as jnp
import numpy as np
from jax import lax
from jax.experimental import pallas as pl
from jax.experimental.pallas import tpu as pltpu
from jax.sharding import PartitionSpec as P

HEAD = 64
SLOT = 128

rope_base = 1000000.0
norm_eps = 1e-06
masked_value = -1e30
bf16 = jnp.bfloat16
f32 = jnp.float32


def dot(left, right, dims, kind=f32):
    return lax.dot_general(left, right, (dims, ((), ())), preferred_element_type=kind)


NN = ((1,), (0,))
NT = ((1,), (1,))
TN = ((0,), (0,))


def bits_of(mesh_axis):
    return [(mesh_axis, bit) for bit in range(int(math.log2(lax.axis_size(mesh_axis))))]


def rotary_table(count):
    half = HEAD // 2
    freq = np.float32(rope_base) ** (-(np.arange(half, dtype=np.float32) * np.float32(2.0)) / np.float32(HEAD))
    phase = np.arange(count, dtype=np.float32)[:, None] * freq[None, :].astype(np.float32)
    phase = phase.astype(np.float64)
    return np.concatenate([np.cos(phase), np.sin(phase)], 1).astype(np.float32)


def spread_table(table):
    n = table.shape[0]
    wide = jnp.concatenate([table, jnp.zeros_like(table)], 1)
    lane = lax.broadcasted_iota(jnp.int32, (n, SLOT), 1)
    cosine = jnp.where(lane < 32, wide, jnp.where(lane < HEAD, pltpu.roll(wide, 32, 1), 1.0))
    sine_a = jnp.where(lane < 32, pltpu.roll(wide, SLOT - 32, 1), 0.0)
    sine_b = jnp.where((lane >= 32) & (lane < HEAD), wide, 0.0)
    return cosine, sine_a, sine_b


def turn(v, table, sign):
    cosine, sine_a, sine_b = table
    return v * cosine + sign * (
        pltpu.roll(v, 32, 1) * sine_b - pltpu.roll(v, SLOT - 32, 1) * sine_a
    )


def meet(peers):
    barrier = pltpu.get_barrier_semaphore()
    for peer in peers:
        pl.semaphore_signal(barrier, 1, device_id=peer, device_id_type=pl.DeviceIdType.MESH)
    pl.semaphore_wait(barrier, len(peers))


def remote(src, dst, send, recv, peer):
    return pltpu.make_async_remote_copy(
        src_ref=src, dst_ref=dst, send_sem=send, recv_sem=recv,
        device_id=peer, device_id_type=pl.DeviceIdType.MESH,
    )


ONES = 72
FRONT_IN = ("own_in", "own_cot", "wq", "wk", "wv", "w_out", "gain1", "bias", "table")
FRONT_OUT = ("cot", "normed", "q", "kv", "ctx", "lse", "resid")


def row_of(ref, count):
    parts = [ref[i : i + 1, :] for i in range(-(-count // 128))]
    return jnp.concatenate(parts, 1)[:, :count]


def weight_copies(hbm, dst, sems, first, blk):
    rows = dst["table"].shape[0]
    nq = hbm["wq"].shape[0]
    nk = hbm["wk"].shape[0]
    parts = [
        (hbm["wq"], dst["w_qkv"].at[0:nq, :]),
        (hbm["wk"], dst["w_qkv"].at[nq : nq + nk, :]),
        (hbm["wv"], dst["w_qkv"].at[nq + nk : nq + 2 * nk, :]),
        (hbm["table"].at[pl.ds(pl.multiple_of(blk * rows, rows), rows), :], dst["table"]),
    ]
    return [
        pltpu.make_async_copy(src, to, sems.at[first + i]) for i, (src, to) in enumerate(parts)
    ]


def front_kernel(heads, length_ref, *refs):
    ni, no = len(FRONT_IN), len(FRONT_OUT)
    hbm = dict(zip(FRONT_IN, refs[:ni]))
    out = dict(zip(FRONT_OUT, refs[ni : ni + no]))
    m = dict(zip(FRONT_OUT, refs[ni + no : ni + 2 * no]))
    (
        x, ctx_o, w_qkv, w_out, w_out_o, gain, bias, gain_rows, bias_rows, table, q1, k1, vt1, m_s, acc_s,
        load_sem, out_sem, pair_send, pair_recv, kv_send, kv_recv,
    ) = refs[ni + 2 * no :]
    rows, width = m["cot"].shape
    half = rows // 2
    blk, nb = lax.axis_index("blk"), lax.axis_size("blk")
    core = lax.axis_index("tensor")
    other = {"tensor": 1 - core}
    ours = pl.multiple_of(core * half, 16)
    theirs = pl.multiple_of((1 - core) * half, 16)
    start = blk * rows
    length = length_ref[0, 0]
    tile, tk = 256, 512

    loads = [
        pltpu.make_async_copy(hbm["own_in"], x.at[pl.ds(ours, half), :], load_sem.at[0]),
        pltpu.make_async_copy(hbm["own_cot"], m["cot"].at[pl.ds(ours, half), :], load_sem.at[1]),
        pltpu.make_async_copy(hbm["w_out"], w_out, load_sem.at[2]),
        pltpu.make_async_copy(hbm["gain1"], gain_rows, load_sem.at[3]),
        pltpu.make_async_copy(hbm["bias"], bias_rows, load_sem.at[4]),
    ] + weight_copies(hbm, dict(w_qkv=w_qkv, table=table), load_sem, 5, blk)
    for copy in loads:
        copy.start()
    meet([other] + [{"blk": lax.rem(blk + d, nb)} for d in range(1, nb)])

    def swap(k, src, dst):
        return remote(src, dst, pair_send.at[k], pair_recv.at[k], other)

    def x_swap():
        return swap(0, hbm["own_in"], x.at[pl.ds(ours, half), :])

    def cot_swap():
        return swap(1, hbm["own_cot"], m["cot"].at[pl.ds(ours, half), :])

    def ctx_swap():
        return swap(2, m["ctx"], ctx_o)

    def out_swap():
        return swap(3, hbm["w_out"], w_out_o)

    def save(name):
        i = FRONT_OUT.index(name)
        return pltpu.make_async_copy(m[name], out[name], out_sem.at[i])

    x_swap().start()
    cot_swap().start()
    out_swap().start()
    loads[0].wait()
    for copy in loads[2:]:
        copy.wait()
    nq = heads * HEAD
    gain[...] = row_of(gain_rows, width)
    bias[...] = row_of(bias_rows, nq + SLOT)
    lane = lax.broadcasted_iota(jnp.int32, (tile, SLOT), 1)

    def rows_in(first):
        def step(r, _):
            at = pl.ds(pl.multiple_of(first + r * tile, tile), tile)
            own = x[at, :].astype(f32)
            rho = lax.rsqrt(jnp.mean(own * own, axis=1, keepdims=True) + norm_eps)
            normed = (own * rho * gain[...]).astype(bf16)
            m["normed"][at, :] = normed
            factors = spread_table(table[at, :])
            proj = dot(normed, w_qkv[...], NT) + bias[...]
            zero = jnp.zeros((tile, HEAD), f32)
            for h in range(heads):
                cols = slice(h * SLOT, (h + 1) * SLOT)
                v = jnp.concatenate([proj[:, h * HEAD : (h + 1) * HEAD], zero], 1)
                v = turn(v, factors, 1.0).astype(bf16).astype(f32) * HEAD**-0.5
                m["q"][at, cols] = v.astype(bf16)
                q1[at, cols] = jnp.where(lane == HEAD, 1.0, v).astype(bf16)
            at_b = pl.ds(pl.multiple_of(start + first + r * tile, tile), tile)
            m["kv"][at_b, :] = turn(proj[:, nq:], factors, 1.0).astype(bf16)
            return 0

        lax.fori_loop(0, half // tile, step, 0)

    rows_in(ours)
    x_swap().wait()
    rows_in(theirs)

    def kv_copy(d):
        at = pl.ds(pl.multiple_of(blk * rows, rows), rows)
        return remote(
            m["kv"].at[at, :], m["kv"].at[at, :], kv_send.at[d - 1], kv_recv.at[d - 1],
            {"blk": lax.rem(blk + d, nb)},
        )

    for d in range(1, nb):
        @pl.when(blk + d < nb)
        def _(d=d):
            kv_copy(d).start()

    save("normed").start()
    save("q").start()
    wide_lane = lax.broadcasted_iota(jnp.int32, (tk, SLOT), 1)
    wide_row = lax.broadcasted_iota(jnp.int32, (tk, SLOT), 0)

    def prepare(first):
        at = pl.ds(pl.multiple_of(first, tk), tk)
        kv = m["kv"][at, :].astype(f32)
        dead = jnp.where(wide_row + first < length, 0.0, masked_value)
        k1[at, :] = jnp.where(
            wide_lane < HEAD, kv, jnp.where(wide_lane == HEAD, dead, 0.0)
        ).astype(bf16)
        vt1[0:HEAD, at] = jnp.transpose(kv)[HEAD:, :].astype(bf16)
        vt1[HEAD:, at] = jnp.ones((ONES - HEAD, tk), bf16)
        return at

    def attend(first, q0, diagonal):
        at = prepare(first)
        kt, vt = k1[at, :], vt1[:, at]
        n = rows - q0
        qs = slice(q0, rows)

        def score(h):
            s = dot(kt, q1[qs, h * SLOT : (h + 1) * SLOT], NT)
            if diagonal:
                ki = lax.broadcasted_iota(jnp.int32, (tk, n), 0)
                qi = lax.broadcasted_iota(jnp.int32, (tk, n), 1)
                s = jnp.where(ki <= qi, s, masked_value)
            return s

        def add(h, p, alpha):
            acc_s[h, :, qs] = acc_s[h, :, qs] * alpha + dot(vt, p, NN)

        ahead, behind = score(0), None
        for h in range(heads):
            s = ahead
            if h + 1 < heads:
                ahead = score(h + 1)
            m_prev = m_s[h : h + 1, qs]
            m_new = jnp.maximum(m_prev, jnp.max(s, axis=0, keepdims=True))
            alpha = jnp.exp(m_prev - m_new)
            p = jnp.exp(s - m_new).astype(bf16)
            m_s[h : h + 1, qs] = m_new
            if behind is not None:
                add(*behind)
            behind = (h, p, alpha)
        add(*behind)

    m_s[...] = jnp.full(m_s.shape, masked_value, f32)
    acc_s[...] = jnp.zeros(acc_s.shape, f32)
    for e in range(rows // tk):
        attend(start + e * tk, e * tk, True)

    def block(d, _):
        src = blk - d
        at = pl.ds(pl.multiple_of(src * rows, rows), rows)
        remote(
            m["kv"].at[at, :], m["kv"].at[at, :], kv_send.at[d - 1], kv_recv.at[d - 1],
            {"blk": src},
        ).wait_recv()

        def key_tile(i, _):
            attend(src * rows + i * tk, 0, False)
            return 0

        lax.fori_loop(0, rows // tk, key_tile, 0)
        return 0

    lax.fori_loop(1, blk + 1, block, 0)
    pos = lax.broadcasted_iota(jnp.int32, (1, rows), 1) + start
    zero = jnp.zeros((HEAD, rows), f32)
    for h in range(heads):
        acc = acc_s[h]
        total = acc[HEAD : HEAD + 1, :]
        ctx = jnp.transpose(jnp.concatenate([acc[:HEAD] / total, zero], 0))
        m["ctx"][:, h * HEAD : (h + 1) * HEAD] = ctx[:, :HEAD].astype(bf16)
        m["lse"][h : h + 1, :] = jnp.where(
            pos < length, m_s[h : h + 1, :] + jnp.log(total), -masked_value
        )
    m["lse"][heads:, :] = jnp.zeros((8 - heads, rows), f32)
    ctx_swap().start()
    save("ctx").start()
    save("lse").start()

    def kv_save(b):
        at = pl.ds(pl.multiple_of(b * rows, rows), rows)
        return pltpu.make_async_copy(
            m["kv"].at[at, :], out["kv"].at[at, :], out_sem.at[FRONT_OUT.index("kv")]
        )

    def keep_kv(b, _):
        kv_save(b).start()
        kv_save(b).wait()
        return 0

    loads[1].wait()
    cot_swap().wait()

    def mask(r, _):
        at = pl.ds(pl.multiple_of(r * tile, tile), tile)
        row = lax.broadcasted_iota(jnp.int32, (tile, width), 0) + start + r * tile
        m["cot"][at, :] = jnp.where(row < length, m["cot"][at, :].astype(f32), 0.0).astype(bf16)
        return 0

    lax.fori_loop(0, rows // tile, mask, 0)
    save("cot").start()
    lax.fori_loop(0, blk + 1, keep_kv, 0)
    for d in range(1, nb):
        @pl.when(blk + d < nb)
        def _(d=d):
            kv_copy(d).wait_send()

    out_swap().wait()
    ctx_swap().wait()

    def out_rows(r, _):
        at = pl.ds(pl.multiple_of(r * tile, tile), tile)
        m["resid"][at, :] = (
            x[at, :].astype(f32)
            + dot(m["ctx"][at, :], w_out[...], NN)
            + dot(ctx_o[at, :], w_out_o[...], NN)
        )
        return 0

    lax.fori_loop(0, rows // tile, out_rows, 0)
    save("resid").start()
    for name in FRONT_OUT:
        if name != "kv":
            save(name).wait()


def front(length, values, heads, nb):
    half, width = values["own_in"].shape
    rows = 2 * half
    keys = rows * nb
    shape = jax.ShapeDtypeStruct
    outs = dict(
        cot=shape((rows, width), bf16),
        normed=shape((rows, width), bf16),
        q=shape((rows, heads * SLOT), bf16),
        kv=shape((keys, SLOT), bf16),
        ctx=shape((rows, heads * HEAD), bf16),
        lse=shape((8, rows), f32),
        resid=shape((rows, width), f32),
    )
    hbm = pl.BlockSpec(memory_space=pl.ANY)
    dma = pltpu.SemaphoreType.DMA
    vm = lambda a: pltpu.VMEM(a.shape, a.dtype)
    results = pl.pallas_call(
        functools.partial(front_kernel, heads),
        out_shape=[outs[name] for name in FRONT_OUT],
        in_specs=[pl.BlockSpec(memory_space=pltpu.SMEM)] + [hbm] * len(FRONT_IN),
        out_specs=[hbm] * len(FRONT_OUT),
        scratch_shapes=[vm(outs[name]) for name in FRONT_OUT]
        + [
            pltpu.VMEM((rows, width), bf16),
            pltpu.VMEM((rows, heads * HEAD), bf16),
            pltpu.VMEM((heads * HEAD + SLOT, width), bf16),
            vm(values["w_out"]),
            vm(values["w_out"]),
            pltpu.VMEM((1, width), f32),
            pltpu.VMEM((1, heads * HEAD + SLOT), f32),
            vm(values["gain1"]),
            vm(values["bias"]),
            pltpu.VMEM((rows, HEAD), f32),
            pltpu.VMEM((rows, heads * SLOT), bf16),
            pltpu.VMEM((keys, SLOT), bf16),
            pltpu.VMEM((ONES, keys), bf16),
            pltpu.VMEM((8, rows), f32),
            pltpu.VMEM((heads, ONES, rows), f32),
            dma((9,)),
            dma((len(FRONT_OUT),)),
            dma((4,)),
            dma((4,)),
            dma((nb - 1,)),
            dma((nb - 1,)),
        ],
        compiler_params=pltpu.CompilerParams(
            collective_id=1, has_side_effects=True, vmem_limit_bytes=58 * 2**20
        ),
        name="front",
    )(length, *[values[name] for name in FRONT_IN])
    return dict(zip(FRONT_OUT, results))


PART = 128
RING = 4
CHUNK = 3 * PART


class Stream:
    def __init__(self, first, count, axes):
        self.first, self.count = first, count
        self.reduce, self.sizes = [], []
        size = count
        for axis, bit in axes:
            if bit == "line":
                kinds = [("up", axis, 0), ("middle", axis, None), ("down", axis, 0)]
            elif size % 32 == 0 and size >= 64:
                kinds = [("half", axis, bit)]
                size //= 2
            else:
                kinds = [("full", axis, bit)]
            self.reduce += kinds
            self.sizes += [size] * len(kinds)
        self.gather = [(axis, bit) for kind, axis, bit in reversed(self.reduce) if kind == "half"]
        self.stages = len(self.reduce) + len(self.gather) + 1

    def scratch(self):
        copies = len(self.reduce) + len(self.gather)
        return [pltpu.VMEM((RING, self.sizes[0], CHUNK), bf16)] + [
            pltpu.VMEM((RING, size, CHUNK), bf16) for size in self.sizes
        ] + [
            pltpu.SemaphoreType.DMA((copies, RING)),
            pltpu.SemaphoreType.DMA((copies, RING)),
            pltpu.SemaphoreType.DMA((2, RING)),
        ]

    def bind(self, refs, sources, out):
        n = len(self.reduce)
        self.keep, self.got = refs[0], refs[1 : n + 1]
        self.send, self.recv, self.local = refs[n + 1 :]
        self.sources, self.out = sources, out
        self.peer, self.mine, offset = [], [], self.first
        self.sends, self.gets = [], []
        self.offsets = []
        for (kind, axis, bit), size in zip(self.reduce, self.sizes):
            at = lax.axis_index(axis)
            if kind == "middle":
                self.peer.append({axis: 3 - at})
            else:
                one = lax.rem(at // (1 << bit), 2)
                self.peer.append({axis: at + (1 - 2 * one) * (1 << bit)})
            middle = (at + 1) // 2 == 1
            self.middle = middle
            sends = {"up": jnp.logical_not(middle), "middle": middle, "down": middle}
            gets = {"up": middle, "middle": middle, "down": jnp.logical_not(middle)}
            self.sends.append(sends.get(kind))
            self.gets.append(gets.get(kind))
            self.mine.append(one if kind == "half" else 0)
            offset = offset + one * size if kind == "half" else offset
            self.offsets.append(offset)
        self.whole = []
        offset, size = self.offsets[-1], self.sizes[-1]
        self.gather_peer = []
        for k in reversed(range(n)):
            if self.reduce[k][0] == "half":
                self.whole.append((offset, size))
                self.gather_peer.append(self.peer[k])
                offset, size = offset - self.mine[k] * size, 2 * size

    def copy(self, k, ring, src, dst, peer):
        return pltpu.make_async_remote_copy(
            src_ref=src,
            dst_ref=dst,
            send_sem=self.send.at[k, ring],
            recv_sem=self.recv.at[k, ring],
            device_id=peer,
            device_id_type=pl.DeviceIdType.MESH,
        )

    def start_first(self, ring, source):
        size, one = self.sizes[0], self.mine[0]
        theirs = pl.multiple_of(self.first + (1 - one) * size, 16)
        own = pl.multiple_of(self.first + one * size, 16)
        self.copy(
            0, ring, source.at[pl.ds(theirs, size), :], self.got[0].at[ring], self.peer[0]
        ).start()
        pltpu.make_async_copy(
            source.at[pl.ds(own, size), :], self.keep.at[ring], self.local.at[0, ring]
        ).start()

    def reduce_copy(self, k, ring):
        if k == 0:
            src = self.keep.at[ring]
        elif self.reduce[k][0] == "half":
            size = self.sizes[k]
            theirs = pl.multiple_of((1 - self.mine[k]) * size, 16)
            src = self.got[k - 1].at[ring, pl.ds(theirs, size), :]
        else:
            src = self.got[k - 1].at[ring]
        return self.copy(k, ring, src, self.got[k].at[ring], self.peer[k])

    def gather_copy(self, t, ring, chunk):
        offset, size = self.whole[t]
        rows = pl.ds(pl.multiple_of(offset, 16), size)
        place = self.out.at[chunk, rows, :]
        src = self.got[-1].at[ring] if t == 0 else place
        return self.copy(len(self.reduce) + t, ring, src, place, self.gather_peer[t])

    def own_copy(self, ring, chunk):
        offset, size = self.whole[0]
        rows = pl.ds(pl.multiple_of(offset, 16), size)
        return pltpu.make_async_copy(
            self.got[-1].at[ring], self.out.at[chunk, rows, :], self.local.at[1, ring]
        )

    def stage(self, s, turn, chunk):
        ring = lax.rem(turn, RING)
        n = len(self.reduce)
        if s == 0:
            base = 0
            for count, place in self.sources:
                @pl.when((chunk >= base) & (chunk < base + count))
                def _(base=base, place=place):
                    self.start_first(ring, place(chunk - base))

                base += count
            return
        if s <= n:
            k = s - 1
            if k == 0:
                pltpu.make_async_copy(
                    self.got[0].at[ring], self.keep.at[ring], self.local.at[0, ring]
                ).wait()
            kind, size = self.reduce[k][0], self.sizes[k]
            copy = self.reduce_copy(k, ring)
            if kind in ("half", "full"):
                copy.wait()
                if k == 0:
                    own = self.keep[ring]
                elif kind == "half":
                    rows = pl.ds(pl.multiple_of(self.mine[k] * size, 16), size)
                    own = self.got[k - 1][ring, rows, :]
                else:
                    own = self.got[k - 1][ring]
                total = own.astype(f32) + self.got[k][ring].astype(f32)
                self.got[k][ring] = total.astype(bf16)
            else:
                pl.when(self.sends[k])(copy.wait_send)
                pl.when(self.gets[k])(copy.wait_recv)

                @pl.when(self.middle)
                def _():
                    if kind == "down":
                        self.got[k][ring] = self.got[k - 1][ring]
                    else:
                        total = self.got[k - 1][ring].astype(f32) + self.got[k][ring].astype(f32)
                        self.got[k][ring] = total.astype(bf16)

            if s < n:
                follow = self.reduce_copy(s, ring)
                if self.sends[s] is None:
                    follow.start()
                else:
                    pl.when(self.sends[s])(follow.start)
            else:
                self.own_copy(ring, chunk).start()
                self.gather_copy(0, ring, chunk).start()
            return
        t = s - n - 1
        self.gather_copy(t, ring, chunk).wait()
        if t == 0:
            self.own_copy(ring, chunk).wait()
        if t + 1 < len(self.gather):
            self.gather_copy(t + 1, ring, chunk).start()


def make_streams(width, plane, line):
    unit = width // 14
    short = [(line[0][0], "line")] if len(line) == 2 else line
    return [
        Stream(0, 5 * unit, plane + short),
        Stream(5 * unit, 5 * unit, plane[::-1] + short),
        Stream(10 * unit, 4 * unit, line + plane),
    ]


LOADS = ("resid", "cot", "gain1", "gain2", "w_out", "ctx", "q", "kv", "lse", "normed", "own_in")
FIRST = ("resid", "cot", "gain1", "gain2")
STREAMED = ("wq", "wk", "wv", "table", "w_gate", "w_up", "w_down")


def backward_kernel(heads, streams, n_ffn, n_small, *refs):
    nl, ns = len(LOADS), len(STREAMED)
    hbm = dict(zip(LOADS + STREAMED, refs[: nl + ns]))
    sums_ref, layer_out_ref, input_grad_ref, grads_ref = refs[nl + ns : nl + ns + 4]
    refs = list(refs[nl + ns + 4 :])
    m = dict(zip(LOADS, refs[:nl]))
    refs = refs[nl:]
    (
        load_sem, w_qkv, table_s, up_t, cot_t, wide, trio, acc, out_s, wg, wu, wd, made,
        w_sem, made_sem, dmid_o, part_o, dlow, delta, dkv, dkv_o, k0, small,
        din_o, rowsum, pair_send, pair_recv, kv_send, kv_recv, out_sem,
        gain_own, gain_o, dq_t, k_t, gain1, gain2,
    ) = refs[:36]
    refs = refs[36:]
    mlp = do = wide
    dmid_s = acc
    dproj = trio
    vec = acc.at[0:SLOT, :]
    din_own = dmid_o.at[0 : dmid_o.shape[0] // 2, :]
    to_send = wd
    rows, width = m["cot"].shape
    half = rows // 2
    blk, nb = lax.axis_index("blk"), lax.axis_size("blk")
    core = lax.axis_index("tensor")
    nz = lax.axis_size("batch")
    other = {"tensor": 1 - core}
    tile = 256
    nq = heads * HEAD
    qkv = nq + SLOT

    pos = 0
    for st in streams:
        cnt = len(st.scratch())
        st.bind(
            refs[pos : pos + cnt],
            [(n_ffn, lambda c: grads_ref.at[c]), (n_small, lambda c: small.at[c])],
            sums_ref,
        )
        pos += cnt

    loads = {
        name: pltpu.make_async_copy(hbm[name], m[name], load_sem.at[i])
        for i, name in enumerate(LOADS)
    }
    late = weight_copies(hbm, dict(w_qkv=w_qkv, table=table_s), load_sem, nl, blk)

    n_pairs = -(-n_ffn // 2)
    odd = n_ffn % 2 == 1
    wide2 = 2 * PART

    def weights(p, count):
        slot = lax.rem(p, 2)
        cols = pl.ds(pl.multiple_of(p * wide2, wide2), count)
        return [
            pltpu.make_async_copy(
                hbm["w_gate"].at[:, cols], wg.at[slot, :, 0:count], w_sem.at[0, slot]
            ),
            pltpu.make_async_copy(
                hbm["w_up"].at[:, cols], wu.at[slot, :, 0:count], w_sem.at[1, slot]
            ),
            pltpu.make_async_copy(
                hbm["w_down"].at[cols, :],
                wd.at[pl.ds(pl.multiple_of(slot * wide2, wide2), count), :],
                w_sem.at[2, slot],
            ),
        ]

    def for_weights(p, act):
        last = n_pairs - 1 if odd else n_pairs

        @pl.when(p < last)
        def _():
            for copy in weights(p, wide2):
                act(copy)

        if odd:
            @pl.when(p == last)
            def _():
                for copy in weights(p, PART):
                    act(copy)

    for name in FIRST:
        loads[name].start()
    for_weights(0, lambda copy: copy.start())
    for_weights(1, lambda copy: copy.start())
    for name in LOADS:
        if name not in FIRST:
            loads[name].start()
    for copy in late:
        copy.start()

    batch = lax.axis_index("batch")
    meet(
        [other]
        + [{"blk": lax.rem(blk + d, nb)} for d in range(1, nb)]
        + [
            {"batch": batch + (1 - 2 * lax.rem(batch // (1 << b), 2)) * (1 << b)}
            for b in range(int(math.log2(nz)))
        ]
        + ([{"batch": 3 - batch}] if nz == 4 else [])
    )

    def swap(k, src, dst):
        return remote(src, dst, pair_send.at[k], pair_recv.at[k], other)

    def dmid_swap():
        return swap(0, dlow, dmid_o)

    theirs = pl.multiple_of((1 - core) * half, 16)
    ours = pl.multiple_of(core * half, 16)

    def part_swap():
        return swap(1, to_send, part_o)

    def din_swap():
        return swap(2, to_send, din_o)

    def gain_swap():
        return swap(3, gain_own, gain_o)

    def put(first, at, value):
        done, n = 0, value.shape[1]
        while done < n:
            c, lane = divmod(first + done, CHUNK)
            take = min(n - done, CHUNK - lane)
            small[c, at, lane : lane + take] = value[:, done : done + take].astype(bf16)
            done += take

    tq, tk = 256, 512

    def begin():
        for name in FIRST:
            loads[name].wait()
        gain1[...] = row_of(m["gain1"], width)
        gain2[...] = row_of(m["gain2"], width)

        def step(r, _):
            at = pl.ds(pl.multiple_of(r * tile, tile), tile)
            resid = m["resid"][at, :]
            rho = lax.rsqrt(jnp.mean(resid * resid, axis=1, keepdims=True) + norm_eps)
            normed = resid * rho * gain2[...]
            mlp[at, :] = normed.astype(bf16)
            up_t[:, at] = jnp.transpose(normed).astype(bf16)
            cot_t[:, at] = jnp.transpose(m["cot"][at, :].astype(f32)).astype(bf16)
            return 0

        lax.fori_loop(0, rows // tile, step, 0)
        dmid_s[...] = jnp.zeros(dmid_s.shape, f32)
        out_s[...] = jnp.zeros(out_s.shape, f32)

    def made_copy(p):
        slot = lax.rem(p, 2)
        return pltpu.make_async_copy(
            made.at[slot], grads_ref.at[pl.ds(p * 2, 2)], made_sem.at[slot]
        )

    def feed_forward(p):
        slot = lax.rem(p, 2)

        @pl.when(p >= 2)
        def _():
            made_copy(p - 1).wait()

        for_weights(p, lambda copy: copy.wait())
        if odd:
            @pl.when(p == n_pairs - 1)
            def _():
                wg[slot, :, PART:] = jnp.zeros((width, PART), bf16)
                wu[slot, :, PART:] = jnp.zeros((width, PART), bf16)
                rest = pl.ds(pl.multiple_of(slot * wide2 + PART, PART), PART)
                wd[rest, :] = jnp.zeros((PART, width), bf16)

        w_g, w_u = wg[slot], wu[slot]
        w_d = wd[pl.ds(pl.multiple_of(slot * wide2, wide2), wide2), :]
        for r in range(rows // tile):
            at = slice(r * tile, (r + 1) * tile)
            gate = dot(mlp[at, :], w_g, NN)
            upper = dot(mlp[at, :], w_u, NN)
            d_hidden = dot(m["cot"][at, :], w_d, NT)
            sigma = 1.0 / (1.0 + jnp.exp(-gate))
            activ = gate * sigma
            hidden = (activ * upper).astype(bf16)
            d_gate = (d_hidden * upper * sigma * (1.0 + gate * (1.0 - sigma))).astype(bf16)
            d_up = (d_hidden * activ).astype(bf16)
            for c in range(2):
                cols = slice(c * PART, (c + 1) * PART)
                trio[at, c * CHUNK : c * CHUNK + PART] = hidden[:, cols]
                trio[at, c * CHUNK + PART : c * CHUNK + 2 * PART] = d_gate[:, cols]
                trio[at, c * CHUNK + 2 * PART : (c + 1) * CHUNK] = d_up[:, cols]
            out_s[at, :] += dot(hidden, w_d, NN)
            dmid_s[at, :] += dot(d_gate, w_g, NT) + dot(d_up, w_u, NT)
        for c in range(2):
            first = c * CHUNK
            made[slot, c, :, :PART] = dot(
                cot_t[...], trio[:, first : first + PART], NN
            ).astype(bf16)
            made[slot, c, :, PART:] = dot(
                up_t[...], trio[:, first + PART : first + CHUNK], NN
            ).astype(bf16)
        made_copy(p).start()
        for_weights(p + 2, lambda copy: copy.start())

        @pl.when(p == 0)
        def _():
            made_copy(p).wait()

    def hand_over():
        made_copy(n_pairs - 1).wait()

        def step(r, _):
            at = pl.ds(pl.multiple_of(r * tile, tile), tile)
            dlow[at, :] = dmid_s[at, :].astype(bf16)
            return 0

        lax.fori_loop(0, rows // tile, step, 0)
        dmid_swap().start()

        def step_part(r, _):
            at = pl.ds(pl.multiple_of(r * tile, tile), tile)
            src = pl.ds(pl.multiple_of(theirs + r * tile, tile), tile)
            to_send[at, :] = out_s[src, :].astype(bf16)
            return 0

        lax.fori_loop(0, half // tile, step_part, 0)
        part_swap().start()

    def before():
        for name in LOADS:
            if name not in FIRST:
                loads[name].wait()
        for copy in late:
            copy.wait()
        dmid_swap().wait()
        part_swap().wait()
        vec[...] = jnp.zeros(vec.shape, f32)

        def out_rows(r, _):
            at = pl.ds(pl.multiple_of(r * tile, tile), tile)
            mine = pl.ds(pl.multiple_of(ours + r * tile, tile), tile)
            part_o[at, :] = (
                m["resid"][mine, :] + out_s[mine, :] + part_o[at, :].astype(f32)
            ).astype(bf16)
            return 0

        lax.fori_loop(0, half // tile, out_rows, 0)
        pltpu.make_async_copy(part_o, layer_out_ref, out_sem.at[0]).start()

        head = lax.broadcasted_iota(jnp.int32, (8, nq), 0)
        column = lax.broadcasted_iota(jnp.int32, (8, nq), 1)
        inside = (column >= head * HEAD) & (column < (head + 1) * HEAD)
        of_head = jnp.where(inside, 1.0, 0.0).astype(bf16)

        def norm(r, _):
            at = pl.ds(pl.multiple_of(r * tile, tile), tile)
            dmid = dlow[at, :].astype(f32) + dmid_o[at, :].astype(f32)
            resid = m["resid"][at, :]
            rho = lax.rsqrt(jnp.mean(resid * resid, axis=1, keepdims=True) + norm_eps)
            n2 = resid * rho
            vec[1:2, :] += jnp.sum(dmid * n2, axis=0, keepdims=True)
            weighted = dmid * gain2[...]
            d_resid = m["cot"][at, :].astype(f32) + rho * (
                weighted - n2 * jnp.mean(weighted * n2, axis=1, keepdims=True)
            )
            m["resid"][at, :] = d_resid
            low = d_resid.astype(bf16)
            dlow[at, :] = low
            d_ctx = dot(low, m["w_out"][...], NT).astype(bf16).astype(f32)
            zero = jnp.zeros((tile, HEAD), f32)
            for h in range(heads):
                own = d_ctx[:, h * HEAD : (h + 1) * HEAD]
                do[at, h * SLOT : (h + 1) * SLOT] = jnp.concatenate([zero, own], 1).astype(bf16)
            rest = d_ctx * m["ctx"][at, :].astype(f32)
            total = jnp.zeros((8, tile), f32)
            for _ in range(3):
                term = rest.astype(bf16)
                total = total + dot(of_head, term, NT)
                rest = rest - term.astype(f32)
            delta[:, at] = total
            return 0

        lax.fori_loop(0, rows // tile, norm, 0)
        lane = lax.broadcasted_iota(jnp.int32, (tk, SLOT), 1)

        def keys(i, _):
            at = pl.ds(pl.multiple_of(i * tk, tk), tk)
            kv = m["kv"][at, :].astype(f32)
            k0[at, :] = jnp.where(lane < HEAD, kv, 0.0).astype(bf16)
            k_t[:, at] = jnp.transpose(kv)[:HEAD, :].astype(bf16)
            return 0

        lax.fori_loop(0, (blk + 1) * (rows // tk), keys, 0)
        dq_t[...] = jnp.zeros(dq_t.shape, f32)

    def grad_out():
        def step(k, _):
            at = pl.ds(pl.multiple_of(k * 128, 128), 128)
            put(0, at, dot(dlow[:, at], m["ctx"][...], TN))
            return 0

        lax.fori_loop(0, width // 128, step, 0)

    def pair(kt, kvt, kt_t, qt, masked):
        at = pl.ds(pl.multiple_of(qt * tq, tq), tq)

        def score(h):
            cols = slice(h * SLOT, (h + 1) * SLOT)
            return dot(kt, m["q"][at, cols], NT), dot(kvt, do[at, cols], NT)

        def add(h, p, ds):
            cols = slice(h * SLOT, (h + 1) * SLOT)
            dq_t[h, :, at] += dot(kt_t, ds, NN)
            return dot(ds, m["q"][at, cols], NN) + dot(p, do[at, cols], NN)

        grad, ahead, behind = None, score(0), None
        for h in range(heads):
            s, dp = ahead
            if h + 1 < heads:
                ahead = score(h + 1)
            p = jnp.exp(s - m["lse"][h : h + 1, at])
            if masked is not None:
                p = jnp.where(masked, p, 0.0)
            ds = (p * (dp - delta[h : h + 1, at])).astype(bf16)
            if behind is not None:
                part = add(*behind)
                grad = part if grad is None else grad + part
            behind = (h, p.astype(bf16), ds)
        return grad + add(*behind)

    def own_tile(e):
        ki = lax.broadcasted_iota(jnp.int32, (tk, tq), 0)
        qi = lax.broadcasted_iota(jnp.int32, (tk, tq), 1)
        at_k = pl.ds(pl.multiple_of(blk * rows + e * tk, tk), tk)
        kt, kvt, kt_t = k0[at_k, :], m["kv"][at_k, :], k_t[:, at_k]
        first = e * (tk // tq)

        def near(j, grad):
            return grad + pair(kt, kvt, kt_t, first + j, ki <= qi + j * tq)

        def far(qt, grad):
            return grad + pair(kt, kvt, kt_t, qt, None)

        grad = lax.fori_loop(0, tk // tq, near, jnp.zeros((tk, SLOT), f32))
        grad = lax.fori_loop(first + tk // tq, rows // tq, far, grad)
        dkv[at_k, :] = grad.astype(bf16)

    def earlier(i):
        at_k = pl.ds(pl.multiple_of(i * tk, tk), tk)
        kt, kvt, kt_t = k0[at_k, :], m["kv"][at_k, :], k_t[:, at_k]

        def step(qt, grad):
            return grad + pair(kt, kvt, kt_t, qt, None)

        grad = lax.fori_loop(0, rows // tq, step, jnp.zeros((tk, SLOT), f32))
        dkv[at_k, :] = grad.astype(bf16)

    def kv_copy(d):
        to = lax.rem(blk + d, nb)
        at = pl.ds(pl.multiple_of(to * rows, rows), rows)
        return remote(
            dkv.at[at, :], dkv_o.at[d - 1], kv_send.at[d - 1], kv_recv.at[d - 1], {"blk": to}
        )

    def kv_start():
        for d in range(1, nb):
            @pl.when(lax.rem(blk + d, nb) < blk)
            def _(d=d):
                kv_copy(d).start()

    def project_queries():
        def step(r, _):
            at = pl.ds(pl.multiple_of(r * tile, tile), tile)
            table = spread_table(table_s[at, :])
            zero = jnp.zeros((HEAD, tile), f32)
            for h in range(heads):
                v = jnp.transpose(jnp.concatenate([dq_t[h, :, at], zero], 0))
                v = turn(v * HEAD**-0.5, table, -1.0)
                dproj[at, h * HEAD : (h + 1) * HEAD] = v[:, :HEAD].astype(bf16)
            return 0

        lax.fori_loop(0, rows // tile, step, 0)

    def project():
        for d in range(1, nb):
            @pl.when(lax.rem(blk + d, nb) < blk)
            def _(d=d):
                kv_copy(d).wait_send()

            @pl.when(lax.rem(blk + nb - d, nb) > blk)
            def _(d=d):
                kv_copy(d).wait_recv()
                for r in range(rows // tile):
                    at = pl.ds(pl.multiple_of(blk * rows + r * tile, tile), tile)
                    total = dkv[at, :].astype(f32) + dkv_o[d - 1, r * tile : (r + 1) * tile].astype(f32)
                    dkv[at, :] = total.astype(bf16)

        rowsum[...] = jnp.zeros(rowsum.shape, f32)

        def unrotate(r, _):
            at = pl.ds(pl.multiple_of(r * tile, tile), tile)
            at_b = pl.ds(pl.multiple_of(blk * rows + r * tile, tile), tile)
            table = spread_table(table_s[at, :])
            dproj[at, nq:qkv] = turn(dkv[at_b, :].astype(f32), table, -1.0).astype(bf16)
            rowsum[0:1, :] += jnp.sum(dproj[at, :qkv].astype(f32), axis=0, keepdims=True)
            return 0

        lax.fori_loop(0, rows // tile, unrotate, 0)

        def d_in(to, first):
            def step(r, _):
                src = pl.ds(pl.multiple_of(first + r * tile, tile), tile)
                at = pl.ds(pl.multiple_of(r * tile, tile), tile)
                to[at, :] = dot(dproj[src, :qkv], w_qkv[...], NN).astype(bf16)
                return 0

            lax.fori_loop(0, half // tile, step, 0)

        d_in(to_send, theirs)
        din_swap().start()
        d_in(din_own, ours)

        def grads(k, _):
            at = pl.ds(pl.multiple_of(k * 128, 128), 128)
            put(nq, at, dot(m["normed"][:, at], dproj[:, :qkv], TN))
            return 0

        lax.fori_loop(0, width // 128, grads, 0)

    def finish():
        din_swap().wait()

        def step(r, _):
            at = pl.ds(pl.multiple_of(r * tile, tile), tile)
            mine = pl.ds(pl.multiple_of(ours + r * tile, tile), tile)
            d_in = din_own[at, :].astype(f32) + din_o[at, :].astype(f32)
            x = m["own_in"][at, :].astype(f32)
            rho = lax.rsqrt(jnp.mean(x * x, axis=1, keepdims=True) + norm_eps)
            n1 = x * rho
            vec[0:1, :] += jnp.sum(d_in * n1, axis=0, keepdims=True)
            weighted = d_in * gain1[...]
            grad = m["resid"][mine, :] + rho * (
                weighted - n1 * jnp.mean(weighted * n1, axis=1, keepdims=True)
            )
            din_own[at, :] = grad.astype(bf16)
            return 0

        lax.fori_loop(0, half // tile, step, 0)
        pltpu.make_async_copy(din_own, input_grad_ref, out_sem.at[1]).start()
        gain_own[...] = vec[0:8, :]
        gain_swap().start()
        vec[2:3, : nq + SLOT] = rowsum[0:1, :]
        gain_swap().wait()
        vec[0:1, :] = gain_own[0:1, :] + gain_o[0:1, :]
        put(2 * nq + SLOT, slice(None), jnp.transpose(vec[...]))

    plan = slots_of(n_ffn, rows // tk, nb)

    def compute(i):
        pl.when(i == 0)(begin)
        few = plan["singles"]
        count = jnp.where(i < few, 1, jnp.where(i < plan["before"], 2, 0))
        first = jnp.where(i < few, i, 2 * i - few)
        count = jnp.minimum(count, jnp.maximum(n_pairs - first, 0))

        def step(c, _):
            feed_forward(first + c)
            return 0

        lax.fori_loop(0, count, step, 0)
        pl.when(i == plan["before"] - 1)(hand_over)
        pl.when(i == plan["before"])(before)

        @pl.when((i >= plan["own"]) & (i < plan["own"] + rows // tk))
        def _():
            own_tile(i - plan["own"])

        pl.when(i == plan["early"] - 1)(grad_out)

        @pl.when((i >= plan["early"]) & (i - plan["early"] < blk * (rows // tk)))
        def _():
            earlier(i - plan["early"])

        pl.when(i == plan["queries"] - 1)(kv_start)
        pl.when(i == plan["queries"])(project_queries)
        pl.when(i == plan["queries"] + 1)(project)
        pl.when(i == plan["queries"] + 2)(finish)

    early_turn = min(plan["early"] - 1, n_ffn)
    gap = max(0, plan["queries"] + 2 - n_ffn - n_small + 1)
    n = n_ffn + n_small + gap
    depth = max(st.stages for st in streams)

    def chunk_of(t):
        late = jnp.where(t <= n_ffn, t - 1, t - gap)
        return jnp.where(t < early_turn, t, jnp.where(t == early_turn, n_ffn, late))

    def slot(i, _):
        compute(i)
        for st in streams:
            for s in reversed(range(st.stages)):
                t = i - s
                real = (t >= 0) & (t < n)
                if gap:
                    real = real & ((t <= n_ffn) | (t > n_ffn + gap))

                @pl.when(real)
                def _(st=st, s=s, t=t):
                    st.stage(s, t, chunk_of(t))

        return 0

    lax.fori_loop(0, n + depth - 1, slot, 0)
    pltpu.make_async_copy(part_o, layer_out_ref, out_sem.at[0]).wait()
    pltpu.make_async_copy(din_own, input_grad_ref, out_sem.at[1]).wait()


def slots_of(n_ffn, tiles, nb):
    pairs = -(-n_ffn // 2)
    singles = pairs
    before = singles + -(-(pairs - singles) // 2)
    own = before + 1
    early = own + tiles
    return dict(
        singles=singles, before=before, own=own, early=early, queries=early + (nb - 1) * tiles
    )


def backward(values, heads, plane, line, nb):
    rows, width = values["cot"].shape
    half = rows // 2
    keys = values["kv"].shape[0]
    n_ffn = values["w_gate"].shape[1] // PART
    n_small = -(-(2 * heads * HEAD + 2 * SLOT) // CHUNK)
    streams = make_streams(width, plane, line)
    hbm = pl.BlockSpec(memory_space=pl.ANY)
    dma = pltpu.SemaphoreType.DMA
    vm = pltpu.VMEM
    assert half == 4 * PART and heads * SLOT == width
    scratch = [vm(values[name].shape, values[name].dtype) for name in LOADS]
    scratch += [
        dma((len(LOADS) + 4,)),
        vm((heads * HEAD + SLOT, width), bf16),
        vm((rows, HEAD), f32),
        vm((width, rows), bf16),
        vm((width, rows), bf16),
        vm((rows, width), bf16),
        vm((rows, 2 * CHUNK), bf16),
        vm((rows, width), f32),
        vm((rows, width), f32),
        vm((2, width, 2 * PART), bf16),
        vm((2, width, 2 * PART), bf16),
        vm((4 * PART, width), bf16),
        vm((2, 2, width, CHUNK), bf16),
        dma((3, 2)),
        dma((2,)),
        vm((rows, width), bf16),
        vm((half, width), bf16),
        vm((rows, width), bf16),
        vm((8, rows), f32),
        vm((keys, SLOT), bf16),
        vm((nb - 1, rows, SLOT), bf16),
        vm((keys, SLOT), bf16),
        vm((n_small, width, CHUNK), bf16),
        vm((half, width), bf16),
        vm((8, heads * HEAD + SLOT), f32),
        dma((4,)),
        dma((4,)),
        dma((nb - 1,)),
        dma((nb - 1,)),
        dma((2,)),
        vm((8, width), f32),
        vm((8, width), f32),
        vm((heads, HEAD, rows), f32),
        vm((HEAD, keys), bf16),
        vm((1, width), f32),
        vm((1, width), f32),
    ]
    for st in streams:
        scratch += st.scratch()
    return pl.pallas_call(
        functools.partial(backward_kernel, heads, streams, n_ffn, n_small),
        out_shape=(
            jax.ShapeDtypeStruct((n_ffn + n_small, width, CHUNK), bf16),
            jax.ShapeDtypeStruct((half, width), bf16),
            jax.ShapeDtypeStruct((half, width), bf16),
            jax.ShapeDtypeStruct((n_ffn + n_ffn % 2, width, CHUNK), bf16),
        ),
        in_specs=[hbm] * (len(LOADS) + len(STREAMED)),
        out_specs=(hbm, hbm, hbm, hbm),
        scratch_shapes=scratch,
        compiler_params=pltpu.CompilerParams(
            collective_id=0, has_side_effects=True, vmem_limit_bytes=60 * 2**20
        ),
        name="backward",
    )(*[values[name] for name in LOADS + STREAMED])


def unpack_kernel(heads, n_small, chunk_ref, *refs):
    small = refs[:n_small]
    down, gate, up, g_out, g_q, g_k, g_v, gain1, gain2, bias = refs[n_small:]
    step = pl.program_id(0)
    for c in range(2):
        value, at = chunk_ref[c], slice(c * PART, (c + 1) * PART)
        down[at, :] = jnp.transpose(value[:, :PART].astype(f32))
        gate[:, at] = value[:, PART : 2 * PART].astype(f32)
        up[:, at] = value[:, 2 * PART :].astype(f32)

    def take(first, count):
        done = 0
        while done < count:
            c, lane = divmod(first + done, CHUNK)
            n = min(count - done, SLOT - lane % SLOT)
            yield done, n, small[c][0, :, lane : lane + n].astype(f32)
            done += n

    @pl.when(step == 0)
    def _():
        nq = heads * HEAD
        for done, n, piece in take(0, nq):
            g_out[done : done + n, :] = jnp.transpose(piece)
        for done, n, piece in take(nq, nq):
            g_q[done : done + n, :] = jnp.transpose(piece)
        for done, n, piece in take(2 * nq, HEAD):
            g_k[...] = jnp.transpose(piece)
        for done, n, piece in take(2 * nq + HEAD, HEAD):
            g_v[...] = jnp.transpose(piece)
        for done, n, piece in take(2 * nq + 2 * HEAD, SLOT):
            vec = jnp.transpose(piece)
            for row, to in ((0, gain1), (1, gain2), (2, bias)):
                for i in range(to.shape[0]):
                    to[i : i + 1, :] = vec[row : row + 1, i * 128 : (i + 1) * 128]


def unpack(sums, n_ffn, heads):
    n, width, _ = sums.shape
    n_small = n - n_ffn
    shape = lambda *dims: jax.ShapeDtypeStruct(dims, f32)
    nq = heads * HEAD
    lanes = [(width // 128, 128), (width // 128, 128), (-(-(nq + SLOT) // 128), 128)]
    whole = [(nq, width), (nq, width), (HEAD, width), (HEAD, width)] + lanes
    return pl.pallas_call(
        functools.partial(unpack_kernel, heads, n_small),
        grid=(-(-n_ffn // 2),),
        out_shape=[
            shape(n_ffn * PART, width), shape(width, n_ffn * PART), shape(width, n_ffn * PART)
        ] + [shape(*dims) for dims in whole],
        in_specs=[pl.BlockSpec((2, width, CHUNK), lambda j: (j, 0, 0))]
        + [
            pl.BlockSpec((1, width, CHUNK), lambda j, c=c: (n_ffn + c, 0, 0))
            for c in range(n_small)
        ],
        out_specs=[
            pl.BlockSpec((2 * PART, width), lambda j: (j, 0)),
            pl.BlockSpec((width, 2 * PART), lambda j: (0, j)),
            pl.BlockSpec((width, 2 * PART), lambda j: (0, j)),
        ] + [pl.BlockSpec(dims, lambda j: (0, 0)) for dims in whole],
        compiler_params=pltpu.CompilerParams(
            vmem_limit_bytes=48 * 2**20, dimension_semantics=("arbitrary",)
        ),
        name="unpack",
    )(*[sums] * (1 + n_small))


def shards(
    layer_in, cotangent, lengths, attn_gain, w_query, query_bias, w_key, key_bias, w_value,
    value_bias, w_out, mlp_gain, w_gate, w_up, w_down,
):
    half, width = layer_in.shape
    rows = half * lax.axis_size("tensor")
    nb = lax.axis_size("blk")
    heads = w_query.shape[1] // HEAD
    biases = jnp.concatenate([query_bias, key_bias, value_bias]).astype(f32)
    biases = jnp.pad(biases, (0, -biases.shape[0] % 128)).reshape(-1, 128)
    values = dict(
        own_in=layer_in, own_cot=cotangent, wq=w_query.T, wk=w_key.T, wv=w_value.T, w_out=w_out,
        gain1=attn_gain.reshape(-1, 128), gain2=mlp_gain.reshape(-1, 128), bias=biases,
        table=jnp.asarray(rotary_table(rows * nb)), w_gate=w_gate, w_up=w_up, w_down=w_down,
    )
    values |= front(lengths, values, heads, nb)
    sums, layer_out, input_grad, _ = backward(
        values, heads, bits_of("blk"), bits_of("batch"), nb
    )
    g_down, g_gate, g_up, g_out, g_query, g_key, g_value, g_gain1, g_gain2, g_bias = unpack(
        sums, w_gate.shape[1] // PART, heads
    )
    nq = heads * HEAD
    g_bias = g_bias.reshape(-1)
    return (
        layer_out, input_grad, g_gain1.reshape(-1), g_query.T, g_bias[:nq], g_key.T,
        g_bias[nq : nq + HEAD], g_value.T, g_bias[nq + HEAD : nq + 2 * HEAD], g_out,
        g_gain2.reshape(-1), g_gate, g_up, g_down,
    )


def solution(mesh):
    rows = P(("batch", "blk", "tensor"), None)
    cols, part, split = P(None, "tensor"), P("tensor"), P("tensor", None)
    return jax.shard_map(
        shards,
        mesh=mesh,
        in_specs=(
            rows, rows, P("batch", None), P(), cols, part, cols, part, cols, part, split, P(),
            cols, cols, split,
        ),
        out_specs=(
            rows, rows, P(), cols, part, cols, part, cols, part, split, P(), cols, cols, split,
        ),
        check_vma=False,
    )
```

```python
import functools
import math

import jax
import jax.numpy as jnp
import numpy as np
from jax import lax
from jax.experimental import pallas as pl
from jax.experimental.pallas import tpu as pltpu
from jax.sharding import PartitionSpec as P

HEAD = 64
SLOT = 128

rope_base = 1000000.0
norm_eps = 1e-06
masked_value = -1e30
bf16 = jnp.bfloat16
f32 = jnp.float32


def dot(left, right, dims, kind=f32):
    return lax.dot_general(left, right, (dims, ((), ())), preferred_element_type=kind)


NN = ((1,), (0,))
NT = ((1,), (1,))
TN = ((0,), (0,))


def bits_of(mesh_axis):
    return [(mesh_axis, bit) for bit in range(int(math.log2(lax.axis_size(mesh_axis))))]


def rotary_table(count):
    half = HEAD // 2
    freq = np.float32(rope_base) ** (-(np.arange(half, dtype=np.float32) * np.float32(2.0)) / np.float32(HEAD))
    phase = np.arange(count, dtype=np.float32)[:, None] * freq[None, :].astype(np.float32)
    phase = phase.astype(np.float64)
    return np.concatenate([np.cos(phase), np.sin(phase)], 1).astype(np.float32)


def spread_table(table):
    n = table.shape[0]
    wide = jnp.concatenate([table, jnp.zeros_like(table)], 1)
    lane = lax.broadcasted_iota(jnp.int32, (n, SLOT), 1)
    cosine = jnp.where(lane < 32, wide, jnp.where(lane < HEAD, pltpu.roll(wide, 32, 1), 1.0))
    sine_a = jnp.where(lane < 32, pltpu.roll(wide, SLOT - 32, 1), 0.0)
    sine_b = jnp.where((lane >= 32) & (lane < HEAD), wide, 0.0)
    return cosine, sine_a, sine_b


def turn(v, table, sign):
    cosine, sine_a, sine_b = table
    return v * cosine + sign * (
        pltpu.roll(v, 32, 1) * sine_b - pltpu.roll(v, SLOT - 32, 1) * sine_a
    )


def meet(peers):
    barrier = pltpu.get_barrier_semaphore()
    for peer in peers:
        pl.semaphore_signal(barrier, 1, device_id=peer, device_id_type=pl.DeviceIdType.MESH)
    pl.semaphore_wait(barrier, len(peers))


def remote(src, dst, send, recv, peer):
    return pltpu.make_async_remote_copy(
        src_ref=src, dst_ref=dst, send_sem=send, recv_sem=recv,
        device_id=peer, device_id_type=pl.DeviceIdType.MESH,
    )


ONES = 72
FRONT_IN = ("own_in", "own_cot", "wq", "wk", "wv", "w_out", "gain1", "bias", "table")
FRONT_OUT = ("cot", "normed", "q", "kv", "ctx", "lse", "resid")


def row_of(ref, count):
    parts = [ref[i : i + 1, :] for i in range(-(-count // 128))]
    return jnp.concatenate(parts, 1)[:, :count]


def weight_copies(hbm, dst, sems, first, blk):
    rows = dst["table"].shape[0]
    nq = hbm["wq"].shape[0]
    nk = hbm["wk"].shape[0]
    parts = [
        (hbm["wq"], dst["w_qkv"].at[0:nq, :]),
        (hbm["wk"], dst["w_qkv"].at[nq : nq + nk, :]),
        (hbm["wv"], dst["w_qkv"].at[nq + nk : nq + 2 * nk, :]),
        (hbm["table"].at[pl.ds(pl.multiple_of(blk * rows, rows), rows), :], dst["table"]),
    ]
    return [
        pltpu.make_async_copy(src, to, sems.at[first + i]) for i, (src, to) in enumerate(parts)
    ]


def front_kernel(heads, length_ref, *refs):
    ni, no = len(FRONT_IN), len(FRONT_OUT)
    hbm = dict(zip(FRONT_IN, refs[:ni]))
    out = dict(zip(FRONT_OUT, refs[ni : ni + no]))
    m = dict(zip(FRONT_OUT, refs[ni + no : ni + 2 * no]))
    (
        x, ctx_o, w_qkv, w_out, w_out_o, gain, bias, gain_rows, bias_rows, table, q1, k1, vt1, m_s, acc_s,
        load_sem, out_sem, pair_send, pair_recv, kv_send, kv_recv,
    ) = refs[ni + 2 * no :]
    rows, width = m["cot"].shape
    half = rows // 2
    blk, nb = lax.axis_index("blk"), lax.axis_size("blk")
    core = lax.axis_index("tensor")
    other = {"tensor": 1 - core}
    ours = pl.multiple_of(core * half, 16)
    theirs = pl.multiple_of((1 - core) * half, 16)
    start = blk * rows
    length = length_ref[0, 0]
    tile, tk = 256, 512

    loads = [
        pltpu.make_async_copy(hbm["own_in"], x.at[pl.ds(ours, half), :], load_sem.at[0]),
        pltpu.make_async_copy(hbm["own_cot"], m["cot"].at[pl.ds(ours, half), :], load_sem.at[1]),
        pltpu.make_async_copy(hbm["w_out"], w_out, load_sem.at[2]),
        pltpu.make_async_copy(hbm["gain1"], gain_rows, load_sem.at[3]),
        pltpu.make_async_copy(hbm["bias"], bias_rows, load_sem.at[4]),
    ] + weight_copies(hbm, dict(w_qkv=w_qkv, table=table), load_sem, 5, blk)
    for copy in loads:
        copy.start()
    meet([other] + [{"blk": lax.rem(blk + d, nb)} for d in range(1, nb)])

    def swap(k, src, dst):
        return remote(src, dst, pair_send.at[k], pair_recv.at[k], other)

    def x_swap():
        return swap(0, hbm["own_in"], x.at[pl.ds(ours, half), :])

    def cot_swap():
        return swap(1, hbm["own_cot"], m["cot"].at[pl.ds(ours, half), :])

    def ctx_swap():
        return swap(2, m["ctx"], ctx_o)

    def out_swap():
        return swap(3, hbm["w_out"], w_out_o)

    def save(name):
        i = FRONT_OUT.index(name)
        return pltpu.make_async_copy(m[name], out[name], out_sem.at[i])

    x_swap().start()
    cot_swap().start()
    out_swap().start()
    loads[0].wait()
    for copy in loads[2:]:
        copy.wait()
    nq = heads * HEAD
    gain[...] = row_of(gain_rows, width)
    bias[...] = row_of(bias_rows, nq + SLOT)
    lane = lax.broadcasted_iota(jnp.int32, (tile, SLOT), 1)

    def rows_in(first):
        def step(r, _):
            at = pl.ds(pl.multiple_of(first + r * tile, tile), tile)
            own = x[at, :].astype(f32)
            rho = lax.rsqrt(jnp.mean(own * own, axis=1, keepdims=True) + norm_eps)
            normed = (own * rho * gain[...]).astype(bf16)
            m["normed"][at, :] = normed
            factors = spread_table(table[at, :])
            proj = dot(normed, w_qkv[...], NT) + bias[...]
            zero = jnp.zeros((tile, HEAD), f32)
            for h in range(heads):
                cols = slice(h * SLOT, (h + 1) * SLOT)
                v = jnp.concatenate([proj[:, h * HEAD : (h + 1) * HEAD], zero], 1)
                v = turn(v, factors, 1.0).astype(bf16).astype(f32) * HEAD**-0.5
                m["q"][at, cols] = v.astype(bf16)
                q1[at, cols] = jnp.where(lane == HEAD, 1.0, v).astype(bf16)
            at_b = pl.ds(pl.multiple_of(start + first + r * tile, tile), tile)
            m["kv"][at_b, :] = turn(proj[:, nq:], factors, 1.0).astype(bf16)
            return 0

        lax.fori_loop(0, half // tile, step, 0)

    rows_in(ours)
    x_swap().wait()
    rows_in(theirs)

    def kv_copy(d):
        at = pl.ds(pl.multiple_of(blk * rows, rows), rows)
        return remote(
            m["kv"].at[at, :], m["kv"].at[at, :], kv_send.at[d - 1], kv_recv.at[d - 1],
            {"blk": lax.rem(blk + d, nb)},
        )

    for d in range(1, nb):
        @pl.when(blk + d < nb)
        def _(d=d):
            kv_copy(d).start()

    save("normed").start()
    save("q").start()
    wide_lane = lax.broadcasted_iota(jnp.int32, (tk, SLOT), 1)
    wide_row = lax.broadcasted_iota(jnp.int32, (tk, SLOT), 0)

    def prepare(first):
        at = pl.ds(pl.multiple_of(first, tk), tk)
        kv = m["kv"][at, :].astype(f32)
        dead = jnp.where(wide_row + first < length, 0.0, masked_value)
        k1[at, :] = jnp.where(
            wide_lane < HEAD, kv, jnp.where(wide_lane == HEAD, dead, 0.0)
        ).astype(bf16)
        vt1[0:HEAD, at] = jnp.transpose(kv)[HEAD:, :].astype(bf16)
        vt1[HEAD:, at] = jnp.ones((ONES - HEAD, tk), bf16)
        return at

    def attend(first, q0, diagonal):
        at = prepare(first)
        kt, vt = k1[at, :], vt1[:, at]
        n = rows - q0
        qs = slice(q0, rows)

        def score(h):
            s = dot(kt, q1[qs, h * SLOT : (h + 1) * SLOT], NT)
            if diagonal:
                ki = lax.broadcasted_iota(jnp.int32, (tk, n), 0)
                qi = lax.broadcasted_iota(jnp.int32, (tk, n), 1)
                s = jnp.where(ki <= qi, s, masked_value)
            return s

        def add(h, p, alpha):
            acc_s[h, :, qs] = acc_s[h, :, qs] * alpha + dot(vt, p, NN)

        ahead, behind = score(0), None
        for h in range(heads):
            s = ahead
            if h + 1 < heads:
                ahead = score(h + 1)
            m_prev = m_s[h : h + 1, qs]
            m_new = jnp.maximum(m_prev, jnp.max(s, axis=0, keepdims=True))
            alpha = jnp.exp(m_prev - m_new)
            p = jnp.exp(s - m_new).astype(bf16)
            m_s[h : h + 1, qs] = m_new
            if behind is not None:
                add(*behind)
            behind = (h, p, alpha)
        add(*behind)

    m_s[...] = jnp.full(m_s.shape, masked_value, f32)
    acc_s[...] = jnp.zeros(acc_s.shape, f32)
    for e in range(rows // tk):
        attend(start + e * tk, e * tk, True)

    def block(d, _):
        src = blk - d
        at = pl.ds(pl.multiple_of(src * rows, rows), rows)
        remote(
            m["kv"].at[at, :], m["kv"].at[at, :], kv_send.at[d - 1], kv_recv.at[d - 1],
            {"blk": src},
        ).wait_recv()

        def key_tile(i, _):
            attend(src * rows + i * tk, 0, False)
            return 0

        lax.fori_loop(0, rows // tk, key_tile, 0)
        return 0

    lax.fori_loop(1, blk + 1, block, 0)
    pos = lax.broadcasted_iota(jnp.int32, (1, rows), 1) + start
    zero = jnp.zeros((HEAD, rows), f32)
    for h in range(heads):
        acc = acc_s[h]
        total = acc[HEAD : HEAD + 1, :]
        ctx = jnp.transpose(jnp.concatenate([acc[:HEAD] / total, zero], 0))
        m["ctx"][:, h * HEAD : (h + 1) * HEAD] = ctx[:, :HEAD].astype(bf16)
        m["lse"][h : h + 1, :] = jnp.where(
            pos < length, m_s[h : h + 1, :] + jnp.log(total), -masked_value
        )
    m["lse"][heads:, :] = jnp.zeros((8 - heads, rows), f32)
    ctx_swap().start()
    save("ctx").start()
    save("lse").start()

    def kv_save(b):
        at = pl.ds(pl.multiple_of(b * rows, rows), rows)
        return pltpu.make_async_copy(
            m["kv"].at[at, :], out["kv"].at[at, :], out_sem.at[FRONT_OUT.index("kv")]
        )

    def keep_kv(b, _):
        kv_save(b).start()
        kv_save(b).wait()
        return 0

    loads[1].wait()
    cot_swap().wait()

    def mask(r, _):
        at = pl.ds(pl.multiple_of(r * tile, tile), tile)
        row = lax.broadcasted_iota(jnp.int32, (tile, width), 0) + start + r * tile
        m["cot"][at, :] = jnp.where(row < length, m["cot"][at, :].astype(f32), 0.0).astype(bf16)
        return 0

    lax.fori_loop(0, rows // tile, mask, 0)
    save("cot").start()
    lax.fori_loop(0, blk + 1, keep_kv, 0)
    for d in range(1, nb):
        @pl.when(blk + d < nb)
        def _(d=d):
            kv_copy(d).wait_send()

    out_swap().wait()
    ctx_swap().wait()

    def out_rows(r, _):
        at = pl.ds(pl.multiple_of(r * tile, tile), tile)
        m["resid"][at, :] = (
            x[at, :].astype(f32)
            + dot(m["ctx"][at, :], w_out[...], NN)
            + dot(ctx_o[at, :], w_out_o[...], NN)
        )
        pltpu.make_async_copy(
            m["resid"].at[at, :], out["resid"].at[at, :], out_sem.at[FRONT_OUT.index("resid")]
        ).start()
        return 0

    lax.fori_loop(0, rows // tile, out_rows, 0)
    for name in FRONT_OUT:
        if name != "kv":
            save(name).wait()


def front(length, values, heads, nb):
    half, width = values["own_in"].shape
    rows = 2 * half
    keys = rows * nb
    shape = jax.ShapeDtypeStruct
    outs = dict(
        cot=shape((rows, width), bf16),
        normed=shape((rows, width), bf16),
        q=shape((rows, heads * SLOT), bf16),
        kv=shape((keys, SLOT), bf16),
        ctx=shape((rows, heads * HEAD), bf16),
        lse=shape((8, rows), f32),
        resid=shape((rows, width), f32),
    )
    hbm = pl.BlockSpec(memory_space=pl.ANY)
    dma = pltpu.SemaphoreType.DMA
    vm = lambda a: pltpu.VMEM(a.shape, a.dtype)
    results = pl.pallas_call(
        functools.partial(front_kernel, heads),
        out_shape=[outs[name] for name in FRONT_OUT],
        in_specs=[pl.BlockSpec(memory_space=pltpu.SMEM)] + [hbm] * len(FRONT_IN),
        out_specs=[hbm] * len(FRONT_OUT),
        scratch_shapes=[vm(outs[name]) for name in FRONT_OUT]
        + [
            pltpu.VMEM((rows, width), bf16),
            pltpu.VMEM((rows, heads * HEAD), bf16),
            pltpu.VMEM((heads * HEAD + SLOT, width), bf16),
            vm(values["w_out"]),
            vm(values["w_out"]),
            pltpu.VMEM((1, width), f32),
            pltpu.VMEM((1, heads * HEAD + SLOT), f32),
            vm(values["gain1"]),
            vm(values["bias"]),
            pltpu.VMEM((rows, HEAD), f32),
            pltpu.VMEM((rows, heads * SLOT), bf16),
            pltpu.VMEM((keys, SLOT), bf16),
            pltpu.VMEM((ONES, keys), bf16),
            pltpu.VMEM((8, rows), f32),
            pltpu.VMEM((heads, ONES, rows), f32),
            dma((9,)),
            dma((len(FRONT_OUT),)),
            dma((4,)),
            dma((4,)),
            dma((nb - 1,)),
            dma((nb - 1,)),
        ],
        compiler_params=pltpu.CompilerParams(
            collective_id=1, has_side_effects=True, vmem_limit_bytes=58 * 2**20
        ),
        name="front",
    )(length, *[values[name] for name in FRONT_IN])
    return dict(zip(FRONT_OUT, results))


PART = 128
RING = 4
CHUNK = 3 * PART


class Stream:
    def __init__(self, first, count, axes):
        self.first, self.count = first, count
        self.reduce, self.sizes = [], []
        size = count
        for axis, bit in axes:
            if bit == "line":
                kinds = [("up", axis, 0), ("middle", axis, None), ("down", axis, 0)]
            elif size % 32 == 0 and size >= 64:
                kinds = [("half", axis, bit)]
                size //= 2
            else:
                kinds = [("full", axis, bit)]
            self.reduce += kinds
            self.sizes += [size] * len(kinds)
        self.gather = [(axis, bit) for kind, axis, bit in reversed(self.reduce) if kind == "half"]
        self.stages = len(self.reduce) + len(self.gather) + 1

    def scratch(self):
        copies = len(self.reduce) + len(self.gather)
        return [pltpu.VMEM((RING, self.sizes[0], CHUNK), bf16)] + [
            pltpu.VMEM((RING, size, CHUNK), bf16) for size in self.sizes
        ] + [
            pltpu.SemaphoreType.DMA((copies, RING)),
            pltpu.SemaphoreType.DMA((copies, RING)),
            pltpu.SemaphoreType.DMA((2, RING)),
        ]

    def bind(self, refs, sources, out):
        n = len(self.reduce)
        self.keep, self.got = refs[0], refs[1 : n + 1]
        self.send, self.recv, self.local = refs[n + 1 :]
        self.sources, self.out = sources, out
        self.peer, self.mine, offset = [], [], self.first
        self.sends, self.gets = [], []
        self.offsets = []
        for (kind, axis, bit), size in zip(self.reduce, self.sizes):
            at = lax.axis_index(axis)
            if kind == "middle":
                self.peer.append({axis: 3 - at})
            else:
                one = lax.rem(at // (1 << bit), 2)
                self.peer.append({axis: at + (1 - 2 * one) * (1 << bit)})
            middle = (at + 1) // 2 == 1
            self.middle = middle
            sends = {"up": jnp.logical_not(middle), "middle": middle, "down": middle}
            gets = {"up": middle, "middle": middle, "down": jnp.logical_not(middle)}
            self.sends.append(sends.get(kind))
            self.gets.append(gets.get(kind))
            self.mine.append(one if kind == "half" else 0)
            offset = offset + one * size if kind == "half" else offset
            self.offsets.append(offset)
        self.whole = []
        offset, size = self.offsets[-1], self.sizes[-1]
        self.gather_peer = []
        for k in reversed(range(n)):
            if self.reduce[k][0] == "half":
                self.whole.append((offset, size))
                self.gather_peer.append(self.peer[k])
                offset, size = offset - self.mine[k] * size, 2 * size

    def copy(self, k, ring, src, dst, peer):
        return pltpu.make_async_remote_copy(
            src_ref=src,
            dst_ref=dst,
            send_sem=self.send.at[k, ring],
            recv_sem=self.recv.at[k, ring],
            device_id=peer,
            device_id_type=pl.DeviceIdType.MESH,
        )

    def start_first(self, ring, source):
        size, one = self.sizes[0], self.mine[0]
        theirs = pl.multiple_of(self.first + (1 - one) * size, 16)
        own = pl.multiple_of(self.first + one * size, 16)
        self.copy(
            0, ring, source.at[pl.ds(theirs, size), :], self.got[0].at[ring], self.peer[0]
        ).start()
        pltpu.make_async_copy(
            source.at[pl.ds(own, size), :], self.keep.at[ring], self.local.at[0, ring]
        ).start()

    def reduce_copy(self, k, ring):
        if k == 0:
            src = self.keep.at[ring]
        elif self.reduce[k][0] == "half":
            size = self.sizes[k]
            theirs = pl.multiple_of((1 - self.mine[k]) * size, 16)
            src = self.got[k - 1].at[ring, pl.ds(theirs, size), :]
        else:
            src = self.got[k - 1].at[ring]
        return self.copy(k, ring, src, self.got[k].at[ring], self.peer[k])

    def gather_copy(self, t, ring, chunk):
        offset, size = self.whole[t]
        rows = pl.ds(pl.multiple_of(offset, 16), size)
        place = self.out.at[chunk, rows, :]
        src = self.got[-1].at[ring] if t == 0 else place
        return self.copy(len(self.reduce) + t, ring, src, place, self.gather_peer[t])

    def own_copy(self, ring, chunk):
        offset, size = self.whole[0]
        rows = pl.ds(pl.multiple_of(offset, 16), size)
        return pltpu.make_async_copy(
            self.got[-1].at[ring], self.out.at[chunk, rows, :], self.local.at[1, ring]
        )

    def stage(self, s, turn, chunk):
        ring = lax.rem(turn, RING)
        n = len(self.reduce)
        if s == 0:
            base = 0
            for count, place in self.sources:
                @pl.when((chunk >= base) & (chunk < base + count))
                def _(base=base, place=place):
                    self.start_first(ring, place(chunk - base))

                base += count
            return
        if s <= n:
            k = s - 1
            if k == 0:
                pltpu.make_async_copy(
                    self.got[0].at[ring], self.keep.at[ring], self.local.at[0, ring]
                ).wait()
            kind, size = self.reduce[k][0], self.sizes[k]
            copy = self.reduce_copy(k, ring)
            if kind in ("half", "full"):
                copy.wait()
                if k == 0:
                    own = self.keep[ring]
                elif kind == "half":
                    rows = pl.ds(pl.multiple_of(self.mine[k] * size, 16), size)
                    own = self.got[k - 1][ring, rows, :]
                else:
                    own = self.got[k - 1][ring]
                total = own.astype(f32) + self.got[k][ring].astype(f32)
                self.got[k][ring] = total.astype(bf16)
            else:
                pl.when(self.sends[k])(copy.wait_send)
                pl.when(self.gets[k])(copy.wait_recv)

                @pl.when(self.middle)
                def _():
                    if kind == "down":
                        self.got[k][ring] = self.got[k - 1][ring]
                    else:
                        total = self.got[k - 1][ring].astype(f32) + self.got[k][ring].astype(f32)
                        self.got[k][ring] = total.astype(bf16)

            if s < n:
                follow = self.reduce_copy(s, ring)
                if self.sends[s] is None:
                    follow.start()
                else:
                    pl.when(self.sends[s])(follow.start)
            else:
                self.own_copy(ring, chunk).start()
                self.gather_copy(0, ring, chunk).start()
            return
        t = s - n - 1
        self.gather_copy(t, ring, chunk).wait()
        if t == 0:
            self.own_copy(ring, chunk).wait()
        if t + 1 < len(self.gather):
            self.gather_copy(t + 1, ring, chunk).start()


def make_streams(width, plane, line):
    unit = width // 14
    short = [(line[0][0], "line")] if len(line) == 2 else line
    return [
        Stream(0, 5 * unit, plane + short),
        Stream(5 * unit, 5 * unit, plane[::-1] + short),
        Stream(10 * unit, 4 * unit, line + plane),
    ]


LOADS = ("resid", "cot", "gain1", "gain2", "w_out", "ctx", "q", "kv", "lse", "normed", "own_in")
FIRST = ("resid", "cot", "gain1", "gain2")
STREAMED = ("wq", "wk", "wv", "table", "w_gate", "w_up", "w_down")


def backward_kernel(heads, streams, n_ffn, n_small, *refs):
    nl, ns = len(LOADS), len(STREAMED)
    hbm = dict(zip(LOADS + STREAMED, refs[: nl + ns]))
    sums_ref, layer_out_ref, input_grad_ref, grads_ref = refs[nl + ns : nl + ns + 4]
    refs = list(refs[nl + ns + 4 :])
    m = dict(zip(LOADS, refs[:nl]))
    refs = refs[nl:]
    (
        load_sem, w_qkv, table_s, up_t, cot_t, wide, trio, acc, out_s, wgu, wd, made,
        w_sem, made_sem, dmid_o, part_o, dlow, delta, dkv, dkv_o, k0, small,
        din_o, rowsum, pair_send, pair_recv, kv_send, kv_recv, out_sem,
        gain_own, gain_o, dq_t, k_t, gain1, gain2,
    ) = refs[:35]
    refs = refs[35:]
    mlp = do = wide
    dmid_s = acc
    dproj = trio
    vec = acc.at[0:SLOT, :]
    din_own = dmid_o.at[0 : dmid_o.shape[0] // 2, :]
    to_send = wd
    rows, width = m["cot"].shape
    half = rows // 2
    blk, nb = lax.axis_index("blk"), lax.axis_size("blk")
    core = lax.axis_index("tensor")
    nz = lax.axis_size("batch")
    other = {"tensor": 1 - core}
    tile = 256
    nq = heads * HEAD
    qkv = nq + SLOT

    pos = 0
    for st in streams:
        cnt = len(st.scratch())
        st.bind(
            refs[pos : pos + cnt],
            [(n_ffn, lambda c: grads_ref.at[c]), (n_small, lambda c: small.at[c])],
            sums_ref,
        )
        pos += cnt

    loads = {
        name: pltpu.make_async_copy(hbm[name], m[name], load_sem.at[i])
        for i, name in enumerate(LOADS)
    }
    late = weight_copies(hbm, dict(w_qkv=w_qkv, table=table_s), load_sem, nl, blk)

    n_pairs = -(-n_ffn // 2)
    odd = n_ffn % 2 == 1
    wide2 = 2 * PART

    def weights(p, count):
        slot = lax.rem(p, 2)
        cols = pl.ds(pl.multiple_of(p * wide2, wide2), count)
        return [
            pltpu.make_async_copy(
                hbm["w_gate"].at[:, cols], wgu.at[slot, :, 0:count], w_sem.at[0, slot]
            ),
            pltpu.make_async_copy(
                hbm["w_up"].at[:, cols], wgu.at[slot, :, wide2 : wide2 + count], w_sem.at[1, slot]
            ),
            pltpu.make_async_copy(
                hbm["w_down"].at[cols, :],
                wd.at[pl.ds(pl.multiple_of(slot * wide2, wide2), count), :],
                w_sem.at[2, slot],
            ),
        ]

    def for_weights(p, act):
        last = n_pairs - 1 if odd else n_pairs

        @pl.when(p < last)
        def _():
            for copy in weights(p, wide2):
                act(copy)

        if odd:
            @pl.when(p == last)
            def _():
                for copy in weights(p, PART):
                    act(copy)

    for name in FIRST:
        loads[name].start()
    for_weights(0, lambda copy: copy.start())
    for_weights(1, lambda copy: copy.start())
    for name in LOADS:
        if name not in FIRST:
            loads[name].start()
    for copy in late:
        copy.start()

    batch = lax.axis_index("batch")
    meet(
        [other]
        + [{"blk": lax.rem(blk + d, nb)} for d in range(1, nb)]
        + [
            {"batch": batch + (1 - 2 * lax.rem(batch // (1 << b), 2)) * (1 << b)}
            for b in range(int(math.log2(nz)))
        ]
        + ([{"batch": 3 - batch}] if nz == 4 else [])
    )

    def swap(k, src, dst):
        return remote(src, dst, pair_send.at[k], pair_recv.at[k], other)

    def dmid_swap():
        return swap(0, dlow, dmid_o)

    theirs = pl.multiple_of((1 - core) * half, 16)
    ours = pl.multiple_of(core * half, 16)

    def part_swap():
        return swap(1, to_send, part_o)

    def din_swap():
        return swap(2, to_send, din_o)

    def gain_swap():
        return swap(3, gain_own, gain_o)

    def put(first, at, value):
        done, n = 0, value.shape[1]
        while done < n:
            c, lane = divmod(first + done, CHUNK)
            take = min(n - done, CHUNK - lane)
            small[c, at, lane : lane + take] = value[:, done : done + take].astype(bf16)
            done += take

    tq, tk = 256, 512

    def begin():
        for name in FIRST:
            loads[name].wait()
        gain1[...] = row_of(m["gain1"], width)
        gain2[...] = row_of(m["gain2"], width)

        def step(r, _):
            at = pl.ds(pl.multiple_of(r * tile, tile), tile)
            resid = m["resid"][at, :]
            rho = lax.rsqrt(jnp.mean(resid * resid, axis=1, keepdims=True) + norm_eps)
            normed = resid * rho * gain2[...]
            mlp[at, :] = normed.astype(bf16)
            up_t[:, at] = jnp.transpose(normed).astype(bf16)
            cot_t[:, at] = jnp.transpose(m["cot"][at, :].astype(f32)).astype(bf16)
            return 0

        lax.fori_loop(0, rows // tile, step, 0)
        dmid_s[...] = jnp.zeros(dmid_s.shape, f32)
        out_s[...] = jnp.zeros(out_s.shape, f32)

    def made_copy(p):
        slot = lax.rem(p, 2)
        return pltpu.make_async_copy(
            made.at[slot], grads_ref.at[pl.ds(p * 2, 2)], made_sem.at[slot]
        )

    def feed_forward(p):
        slot = lax.rem(p, 2)

        @pl.when(p >= 2)
        def _():
            made_copy(p - 1).wait()

        for_weights(p, lambda copy: copy.wait())
        if odd:
            @pl.when(p == n_pairs - 1)
            def _():
                wgu[slot, :, PART:wide2] = jnp.zeros((width, PART), bf16)
                wgu[slot, :, wide2 + PART :] = jnp.zeros((width, PART), bf16)
                rest = pl.ds(pl.multiple_of(slot * wide2 + PART, PART), PART)
                wd[rest, :] = jnp.zeros((PART, width), bf16)

        w_gu = wgu[slot]
        w_d = wd[pl.ds(pl.multiple_of(slot * wide2, wide2), wide2), :]
        for r in range(rows // tile):
            at = slice(r * tile, (r + 1) * tile)
            both = dot(mlp[at, :], w_gu, NN)
            gate, upper = both[:, :wide2], both[:, wide2:]
            d_hidden = dot(m["cot"][at, :], w_d, NT)
            sigma = 1.0 / (1.0 + jnp.exp(-gate))
            activ = gate * sigma
            hidden = (activ * upper).astype(bf16)
            d_gate = (d_hidden * upper * sigma * (1.0 + gate * (1.0 - sigma))).astype(bf16)
            d_up = (d_hidden * activ).astype(bf16)
            d_pair = jnp.concatenate([d_gate, d_up], 1)
            trio[at, :wide2] = hidden
            trio[at, wide2:] = d_pair
            out_s[at, :] += dot(hidden, w_d, NN)
            dmid_s[at, :] += dot(d_pair, w_gu, NT)
        for r in range(2):
            at = slice(r * width // 2, (r + 1) * width // 2)
            down = dot(cot_t[at, :], trio[:, :wide2], NN).astype(bf16)
            pairs = dot(up_t[at, :], trio[:, wide2:], NN).astype(bf16)
            for c in range(2):
                cols = slice(c * PART, (c + 1) * PART)
                made[slot, c, at, :PART] = down[:, cols]
                made[slot, c, at, PART : 2 * PART] = pairs[:, cols]
                made[slot, c, at, 2 * PART :] = pairs[:, wide2 + c * PART : wide2 + (c + 1) * PART]
        made_copy(p).start()
        for_weights(p + 2, lambda copy: copy.start())

        @pl.when(p == 0)
        def _():
            made_copy(p).wait()

    def hand_over():
        made_copy(n_pairs - 1).wait()

        def step(r, _):
            at = pl.ds(pl.multiple_of(r * tile, tile), tile)
            dlow[at, :] = dmid_s[at, :].astype(bf16)
            return 0

        lax.fori_loop(0, rows // tile, step, 0)
        dmid_swap().start()

        def step_part(r, _):
            at = pl.ds(pl.multiple_of(r * tile, tile), tile)
            src = pl.ds(pl.multiple_of(theirs + r * tile, tile), tile)
            to_send[at, :] = out_s[src, :].astype(bf16)
            return 0

        lax.fori_loop(0, half // tile, step_part, 0)
        part_swap().start()

    def before():
        for name in LOADS:
            if name not in FIRST + ("kv",):
                loads[name].wait()
        for copy in late:
            copy.wait()
        dmid_swap().wait()
        part_swap().wait()
        vec[...] = jnp.zeros(vec.shape, f32)

        def out_rows(r, _):
            at = pl.ds(pl.multiple_of(r * tile, tile), tile)
            mine = pl.ds(pl.multiple_of(ours + r * tile, tile), tile)
            part_o[at, :] = (
                m["resid"][mine, :] + out_s[mine, :] + part_o[at, :].astype(f32)
            ).astype(bf16)
            return 0

        lax.fori_loop(0, half // tile, out_rows, 0)
        pltpu.make_async_copy(part_o, layer_out_ref, out_sem.at[0]).start()

        head = lax.broadcasted_iota(jnp.int32, (8, nq), 0)
        column = lax.broadcasted_iota(jnp.int32, (8, nq), 1)
        inside = (column >= head * HEAD) & (column < (head + 1) * HEAD)
        of_head = jnp.where(inside, 1.0, 0.0).astype(bf16)

        def norm(r, _):
            at = pl.ds(pl.multiple_of(r * tile, tile), tile)
            dmid = dlow[at, :].astype(f32) + dmid_o[at, :].astype(f32)
            resid = m["resid"][at, :]
            rho = lax.rsqrt(jnp.mean(resid * resid, axis=1, keepdims=True) + norm_eps)
            n2 = resid * rho
            vec[1:2, :] += jnp.sum(dmid * n2, axis=0, keepdims=True)
            weighted = dmid * gain2[...]
            d_resid = m["cot"][at, :].astype(f32) + rho * (
                weighted - n2 * jnp.mean(weighted * n2, axis=1, keepdims=True)
            )
            m["resid"][at, :] = d_resid
            low = d_resid.astype(bf16)
            dlow[at, :] = low
            d_ctx = dot(low, m["w_out"][...], NT).astype(bf16).astype(f32)
            zero = jnp.zeros((tile, HEAD), f32)
            for h in range(heads):
                own = d_ctx[:, h * HEAD : (h + 1) * HEAD]
                do[at, h * SLOT : (h + 1) * SLOT] = jnp.concatenate([zero, own], 1).astype(bf16)
            rest = d_ctx * m["ctx"][at, :].astype(f32)
            total = jnp.zeros((8, tile), f32)
            for _ in range(3):
                term = rest.astype(bf16)
                total = total + dot(of_head, term, NT)
                rest = rest - term.astype(f32)
            delta[:, at] = total
            return 0

        lax.fori_loop(0, rows // tile, norm, 0)

    def keys_first():
        loads["kv"].wait()
        lane = lax.broadcasted_iota(jnp.int32, (tk, SLOT), 1)

        def keys(i, _):
            at = pl.ds(pl.multiple_of(i * tk, tk), tk)
            kv = m["kv"][at, :].astype(f32)
            k0[at, :] = jnp.where(lane < HEAD, kv, 0.0).astype(bf16)
            k_t[:, at] = jnp.transpose(kv)[:HEAD, :].astype(bf16)
            return 0

        lax.fori_loop(0, (blk + 1) * (rows // tk), keys, 0)
        dq_t[...] = jnp.zeros(dq_t.shape, f32)

    def grad_out():
        def step(k, _):
            at = pl.ds(pl.multiple_of(k * 128, 128), 128)
            put(0, at, dot(dlow[:, at], m["ctx"][...], TN))
            return 0

        lax.fori_loop(0, width // 128, step, 0)

    def pair(kt, kvt, kt_t, qt, masked):
        at = pl.ds(pl.multiple_of(qt * tq, tq), tq)

        def score(h):
            cols = slice(h * SLOT, (h + 1) * SLOT)
            return dot(kt, m["q"][at, cols], NT), dot(kvt, do[at, cols], NT)

        def add(h, p, ds):
            cols = slice(h * SLOT, (h + 1) * SLOT)
            dq_t[h, :, at] += dot(kt_t, ds, NN)
            return dot(ds, m["q"][at, cols], NN) + dot(p, do[at, cols], NN)

        grad, ahead, behind = None, score(0), None
        for h in range(heads):
            s, dp = ahead
            if h + 1 < heads:
                ahead = score(h + 1)
            p = jnp.exp(s - m["lse"][h : h + 1, at])
            if masked is not None:
                p = jnp.where(masked, p, 0.0)
            ds = (p * (dp - delta[h : h + 1, at])).astype(bf16)
            if behind is not None:
                part = add(*behind)
                grad = part if grad is None else grad + part
            behind = (h, p.astype(bf16), ds)
        return grad + add(*behind)

    def own_tile(e):
        ki = lax.broadcasted_iota(jnp.int32, (tk, tq), 0)
        qi = lax.broadcasted_iota(jnp.int32, (tk, tq), 1)
        at_k = pl.ds(pl.multiple_of(blk * rows + e * tk, tk), tk)
        kt, kvt, kt_t = k0[at_k, :], m["kv"][at_k, :], k_t[:, at_k]
        first = e * (tk // tq)

        def near(j, grad):
            return grad + pair(kt, kvt, kt_t, first + j, ki <= qi + j * tq)

        def far(qt, grad):
            return grad + pair(kt, kvt, kt_t, qt, None)

        grad = lax.fori_loop(0, tk // tq, near, jnp.zeros((tk, SLOT), f32))
        grad = lax.fori_loop(first + tk // tq, rows // tq, far, grad)
        dkv[at_k, :] = grad.astype(bf16)

    def earlier(i):
        at_k = pl.ds(pl.multiple_of(i * tk, tk), tk)
        kt, kvt, kt_t = k0[at_k, :], m["kv"][at_k, :], k_t[:, at_k]

        def step(qt, grad):
            return grad + pair(kt, kvt, kt_t, qt, None)

        grad = lax.fori_loop(0, rows // tq, step, jnp.zeros((tk, SLOT), f32))
        dkv[at_k, :] = grad.astype(bf16)

    def kv_copy(d):
        to = lax.rem(blk + d, nb)
        at = pl.ds(pl.multiple_of(to * rows, rows), rows)
        return remote(
            dkv.at[at, :], dkv_o.at[d - 1], kv_send.at[d - 1], kv_recv.at[d - 1], {"blk": to}
        )

    def kv_start():
        for d in range(1, nb):
            @pl.when(lax.rem(blk + d, nb) < blk)
            def _(d=d):
                kv_copy(d).start()

    def project_queries():
        def step(r, _):
            at = pl.ds(pl.multiple_of(r * tile, tile), tile)
            table = spread_table(table_s[at, :])
            zero = jnp.zeros((HEAD, tile), f32)
            for h in range(heads):
                v = jnp.transpose(jnp.concatenate([dq_t[h, :, at], zero], 0))
                v = turn(v * HEAD**-0.5, table, -1.0)
                dproj[at, h * HEAD : (h + 1) * HEAD] = v[:, :HEAD].astype(bf16)
            return 0

        lax.fori_loop(0, rows // tile, step, 0)

    def project():
        for d in range(1, nb):
            @pl.when(lax.rem(blk + d, nb) < blk)
            def _(d=d):
                kv_copy(d).wait_send()

            @pl.when(lax.rem(blk + nb - d, nb) > blk)
            def _(d=d):
                kv_copy(d).wait_recv()
                for r in range(rows // tile):
                    at = pl.ds(pl.multiple_of(blk * rows + r * tile, tile), tile)
                    total = dkv[at, :].astype(f32) + dkv_o[d - 1, r * tile : (r + 1) * tile].astype(f32)
                    dkv[at, :] = total.astype(bf16)

        rowsum[...] = jnp.zeros(rowsum.shape, f32)

        def unrotate(r, _):
            at = pl.ds(pl.multiple_of(r * tile, tile), tile)
            at_b = pl.ds(pl.multiple_of(blk * rows + r * tile, tile), tile)
            table = spread_table(table_s[at, :])
            dproj[at, nq:qkv] = turn(dkv[at_b, :].astype(f32), table, -1.0).astype(bf16)
            rowsum[0:1, :] += jnp.sum(dproj[at, :qkv].astype(f32), axis=0, keepdims=True)
            return 0

        lax.fori_loop(0, rows // tile, unrotate, 0)

        def d_in(to, first):
            def step(r, _):
                src = pl.ds(pl.multiple_of(first + r * tile, tile), tile)
                at = pl.ds(pl.multiple_of(r * tile, tile), tile)
                to[at, :] = dot(dproj[src, :qkv], w_qkv[...], NN).astype(bf16)
                return 0

            lax.fori_loop(0, half // tile, step, 0)

        d_in(to_send, theirs)
        din_swap().start()
        d_in(din_own, ours)

        def grads(k, _):
            at = pl.ds(pl.multiple_of(k * 128, 128), 128)
            put(nq, at, dot(m["normed"][:, at], dproj[:, :qkv], TN))
            return 0

        lax.fori_loop(0, width // 128, grads, 0)

    def finish():
        din_swap().wait()

        def step(r, _):
            at = pl.ds(pl.multiple_of(r * tile, tile), tile)
            mine = pl.ds(pl.multiple_of(ours + r * tile, tile), tile)
            d_in = din_own[at, :].astype(f32) + din_o[at, :].astype(f32)
            x = m["own_in"][at, :].astype(f32)
            rho = lax.rsqrt(jnp.mean(x * x, axis=1, keepdims=True) + norm_eps)
            n1 = x * rho
            vec[0:1, :] += jnp.sum(d_in * n1, axis=0, keepdims=True)
            weighted = d_in * gain1[...]
            grad = m["resid"][mine, :] + rho * (
                weighted - n1 * jnp.mean(weighted * n1, axis=1, keepdims=True)
            )
            din_own[at, :] = grad.astype(bf16)
            return 0

        lax.fori_loop(0, half // tile, step, 0)
        pltpu.make_async_copy(din_own, input_grad_ref, out_sem.at[1]).start()
        gain_own[...] = vec[0:8, :]
        gain_swap().start()
        vec[2:3, : nq + SLOT] = rowsum[0:1, :]
        gain_swap().wait()
        vec[0:1, :] = gain_own[0:1, :] + gain_o[0:1, :]
        put(2 * nq + SLOT, slice(None), jnp.transpose(vec[...]))

    plan = slots_of(n_ffn, rows // tk, nb)

    def compute(i):
        pl.when(i == 0)(begin)
        few = plan["singles"]
        count = jnp.where(i < few, 1, jnp.where(i < plan["before"], 2, 0))
        first = jnp.where(i < few, i, 2 * i - few)
        count = jnp.minimum(count, jnp.maximum(n_pairs - first, 0))

        def step(c, _):
            feed_forward(first + c)
            return 0

        lax.fori_loop(0, count, step, 0)
        pl.when(i == max(plan["before"] - 3, 0))(keys_first)
        pl.when(i == plan["before"] - 1)(hand_over)
        pl.when(i == plan["before"])(before)

        @pl.when((i >= plan["own"]) & (i < plan["own"] + rows // tk))
        def _():
            own_tile(i - plan["own"])

        pl.when(i == plan["early"] - 1)(grad_out)

        @pl.when((i >= plan["early"]) & (i - plan["early"] < blk * (rows // tk)))
        def _():
            earlier(i - plan["early"])

        pl.when(i == plan["queries"] - 1)(kv_start)
        pl.when(i == plan["queries"])(project_queries)
        pl.when(i == plan["queries"] + 1)(project)
        pl.when(i == plan["queries"] + 2)(finish)

    early_turn = min(plan["early"] - 1, n_ffn)
    gap = max(0, plan["queries"] + 2 - n_ffn - n_small + 1)
    n = n_ffn + n_small + gap
    depth = max(st.stages for st in streams)

    def chunk_of(t):
        late = jnp.where(t <= n_ffn, t - 1, t - gap)
        return jnp.where(t < early_turn, t, jnp.where(t == early_turn, n_ffn, late))

    def slot(i, _):
        compute(i)
        for st in streams:
            for s in reversed(range(st.stages)):
                t = i - s
                real = (t >= 0) & (t < n)
                if gap:
                    real = real & ((t <= n_ffn) | (t > n_ffn + gap))

                @pl.when(real)
                def _(st=st, s=s, t=t):
                    st.stage(s, t, chunk_of(t))

        return 0

    lax.fori_loop(0, n + depth - 1, slot, 0)
    pltpu.make_async_copy(part_o, layer_out_ref, out_sem.at[0]).wait()
    pltpu.make_async_copy(din_own, input_grad_ref, out_sem.at[1]).wait()


def slots_of(n_ffn, tiles, nb):
    pairs = -(-n_ffn // 2)
    singles = pairs
    before = singles + -(-(pairs - singles) // 2)
    own = before + 1
    early = own + tiles
    return dict(
        singles=singles, before=before, own=own, early=early, queries=early + (nb - 1) * tiles
    )


def backward(values, heads, plane, line, nb):
    rows, width = values["cot"].shape
    half = rows // 2
    keys = values["kv"].shape[0]
    n_ffn = values["w_gate"].shape[1] // PART
    n_small = -(-(2 * heads * HEAD + 2 * SLOT) // CHUNK)
    streams = make_streams(width, plane, line)
    hbm = pl.BlockSpec(memory_space=pl.ANY)
    dma = pltpu.SemaphoreType.DMA
    vm = pltpu.VMEM
    assert half == 4 * PART and heads * SLOT == width
    scratch = [vm(values[name].shape, values[name].dtype) for name in LOADS]
    scratch += [
        dma((len(LOADS) + 4,)),
        vm((heads * HEAD + SLOT, width), bf16),
        vm((rows, HEAD), f32),
        vm((width, rows), bf16),
        vm((width, rows), bf16),
        vm((rows, width), bf16),
        vm((rows, 2 * CHUNK), bf16),
        vm((rows, width), f32),
        vm((rows, width), f32),
        vm((2, width, 4 * PART), bf16),
        vm((4 * PART, width), bf16),
        vm((2, 2, width, CHUNK), bf16),
        dma((3, 2)),
        dma((2,)),
        vm((rows, width), bf16),
        vm((half, width), bf16),
        vm((rows, width), bf16),
        vm((8, rows), f32),
        vm((keys, SLOT), bf16),
        vm((nb - 1, rows, SLOT), bf16),
        vm((keys, SLOT), bf16),
        vm((n_small, width, CHUNK), bf16),
        vm((half, width), bf16),
        vm((8, heads * HEAD + SLOT), f32),
        dma((4,)),
        dma((4,)),
        dma((nb - 1,)),
        dma((nb - 1,)),
        dma((2,)),
        vm((8, width), f32),
        vm((8, width), f32),
        vm((heads, HEAD, rows), f32),
        vm((HEAD, keys), bf16),
        vm((1, width), f32),
        vm((1, width), f32),
    ]
    for st in streams:
        scratch += st.scratch()
    return pl.pallas_call(
        functools.partial(backward_kernel, heads, streams, n_ffn, n_small),
        out_shape=(
            jax.ShapeDtypeStruct((n_ffn + n_small, width, CHUNK), bf16),
            jax.ShapeDtypeStruct((half, width), bf16),
            jax.ShapeDtypeStruct((half, width), bf16),
            jax.ShapeDtypeStruct((n_ffn + n_ffn % 2, width, CHUNK), bf16),
        ),
        in_specs=[hbm] * (len(LOADS) + len(STREAMED)),
        out_specs=(hbm, hbm, hbm, hbm),
        scratch_shapes=scratch,
        compiler_params=pltpu.CompilerParams(
            collective_id=0, has_side_effects=True, vmem_limit_bytes=60 * 2**20
        ),
        name="backward",
    )(*[values[name] for name in LOADS + STREAMED])


def unpack_kernel(heads, n_small, chunk_ref, *refs):
    small = refs[:n_small]
    down, gate, up, g_out, g_q, g_k, g_v, gain1, gain2, bias = refs[n_small:]
    step = pl.program_id(0)
    for c in range(2):
        value, at = chunk_ref[c], slice(c * PART, (c + 1) * PART)
        down[at, :] = jnp.transpose(value[:, :PART].astype(f32))
        gate[:, at] = value[:, PART : 2 * PART].astype(f32)
        up[:, at] = value[:, 2 * PART :].astype(f32)

    def take(first, count):
        done = 0
        while done < count:
            c, lane = divmod(first + done, CHUNK)
            n = min(count - done, SLOT - lane % SLOT)
            yield done, n, small[c][0, :, lane : lane + n].astype(f32)
            done += n

    @pl.when(step == 0)
    def _():
        nq = heads * HEAD
        for done, n, piece in take(0, nq):
            g_out[done : done + n, :] = jnp.transpose(piece)
        for done, n, piece in take(nq, nq):
            g_q[done : done + n, :] = jnp.transpose(piece)
        for done, n, piece in take(2 * nq, HEAD):
            g_k[...] = jnp.transpose(piece)
        for done, n, piece in take(2 * nq + HEAD, HEAD):
            g_v[...] = jnp.transpose(piece)
        for done, n, piece in take(2 * nq + 2 * HEAD, SLOT):
            vec = jnp.transpose(piece)
            for row, to in ((0, gain1), (1, gain2), (2, bias)):
                for i in range(to.shape[0]):
                    to[i : i + 1, :] = vec[row : row + 1, i * 128 : (i + 1) * 128]


def unpack(sums, n_ffn, heads):
    n, width, _ = sums.shape
    n_small = n - n_ffn
    shape = lambda *dims: jax.ShapeDtypeStruct(dims, f32)
    nq = heads * HEAD
    lanes = [(width // 128, 128), (width // 128, 128), (-(-(nq + SLOT) // 128), 128)]
    whole = [(nq, width), (nq, width), (HEAD, width), (HEAD, width)] + lanes
    return pl.pallas_call(
        functools.partial(unpack_kernel, heads, n_small),
        grid=(-(-n_ffn // 2),),
        out_shape=[
            shape(n_ffn * PART, width), shape(width, n_ffn * PART), shape(width, n_ffn * PART)
        ] + [shape(*dims) for dims in whole],
        in_specs=[pl.BlockSpec((2, width, CHUNK), lambda j: (j, 0, 0))]
        + [
            pl.BlockSpec((1, width, CHUNK), lambda j, c=c: (n_ffn + c, 0, 0))
            for c in range(n_small)
        ],
        out_specs=[
            pl.BlockSpec((2 * PART, width), lambda j: (j, 0)),
            pl.BlockSpec((width, 2 * PART), lambda j: (0, j)),
            pl.BlockSpec((width, 2 * PART), lambda j: (0, j)),
        ] + [pl.BlockSpec(dims, lambda j: (0, 0)) for dims in whole],
        compiler_params=pltpu.CompilerParams(
            vmem_limit_bytes=48 * 2**20, dimension_semantics=("arbitrary",)
        ),
        name="unpack",
    )(*[sums] * (1 + n_small))


def shards(
    layer_in, cotangent, lengths, attn_gain, w_query, query_bias, w_key, key_bias, w_value,
    value_bias, w_out, mlp_gain, w_gate, w_up, w_down,
):
    half, width = layer_in.shape
    rows = half * lax.axis_size("tensor")
    nb = lax.axis_size("blk")
    heads = w_query.shape[1] // HEAD
    biases = jnp.concatenate([query_bias, key_bias, value_bias]).astype(f32)
    biases = jnp.pad(biases, (0, -biases.shape[0] % 128)).reshape(-1, 128)
    values = dict(
        own_in=layer_in, own_cot=cotangent, wq=w_query.T, wk=w_key.T, wv=w_value.T, w_out=w_out,
        gain1=attn_gain.reshape(-1, 128), gain2=mlp_gain.reshape(-1, 128), bias=biases,
        table=jnp.asarray(rotary_table(rows * nb)), w_gate=w_gate, w_up=w_up, w_down=w_down,
    )
    values |= front(lengths, values, heads, nb)
    sums, layer_out, input_grad, _ = backward(
        values, heads, bits_of("blk"), bits_of("batch"), nb
    )
    g_down, g_gate, g_up, g_out, g_query, g_key, g_value, g_gain1, g_gain2, g_bias = unpack(
        sums, w_gate.shape[1] // PART, heads
    )
    nq = heads * HEAD
    g_bias = g_bias.reshape(-1)
    return (
        layer_out, input_grad, g_gain1.reshape(-1), g_query.T, g_bias[:nq], g_key.T,
        g_bias[nq : nq + HEAD], g_value.T, g_bias[nq + HEAD : nq + 2 * HEAD], g_out,
        g_gain2.reshape(-1), g_gate, g_up, g_down,
    )


def solution(mesh):
    rows = P(("batch", "blk", "tensor"), None)
    cols, part, split = P(None, "tensor"), P("tensor"), P("tensor", None)
    return jax.shard_map(
        shards,
        mesh=mesh,
        in_specs=(
            rows, rows, P("batch", None), P(), cols, part, cols, part, cols, part, split, P(),
            cols, cols, split,
        ),
        out_specs=(
            rows, rows, P(), cols, part, cols, part, cols, part, split, P(), cols, cols, split,
        ),
        check_vma=False,
    )
```

```python
import functools
import math

import jax
import jax.numpy as jnp
import numpy as np
from jax import lax
from jax.experimental import pallas as pl
from jax.experimental.pallas import tpu as pltpu
from jax.sharding import PartitionSpec as P

HEAD = 64
SLOT = 128

rope_base = 1000000.0
norm_eps = 1e-06
masked_value = -1e30
bf16 = jnp.bfloat16
f32 = jnp.float32


def dot(left, right, dims, kind=f32):
    return lax.dot_general(left, right, (dims, ((), ())), preferred_element_type=kind)


NN = ((1,), (0,))
NT = ((1,), (1,))
TN = ((0,), (0,))


def bits_of(mesh_axis):
    return [(mesh_axis, bit) for bit in range(int(math.log2(lax.axis_size(mesh_axis))))]


def rotary_table(count):
    half = HEAD // 2
    freq = np.float32(rope_base) ** (-(np.arange(half, dtype=np.float32) * np.float32(2.0)) / np.float32(HEAD))
    phase = np.arange(count, dtype=np.float32)[:, None] * freq[None, :].astype(np.float32)
    phase = phase.astype(np.float64)
    return np.concatenate([np.cos(phase), np.sin(phase)], 1).astype(np.float32)


def spread_table(table):
    n = table.shape[0]
    wide = jnp.concatenate([table, jnp.zeros_like(table)], 1)
    lane = lax.broadcasted_iota(jnp.int32, (n, SLOT), 1)
    cosine = jnp.where(lane < 32, wide, jnp.where(lane < HEAD, pltpu.roll(wide, 32, 1), 1.0))
    sine_a = jnp.where(lane < 32, pltpu.roll(wide, SLOT - 32, 1), 0.0)
    sine_b = jnp.where((lane >= 32) & (lane < HEAD), wide, 0.0)
    return cosine, sine_a, sine_b


def turn(v, table, sign):
    cosine, sine_a, sine_b = table
    return v * cosine + sign * (
        pltpu.roll(v, 32, 1) * sine_b - pltpu.roll(v, SLOT - 32, 1) * sine_a
    )


def meet(peers):
    barrier = pltpu.get_barrier_semaphore()
    for peer in peers:
        pl.semaphore_signal(barrier, 1, device_id=peer, device_id_type=pl.DeviceIdType.MESH)
    pl.semaphore_wait(barrier, len(peers))


def remote(src, dst, send, recv, peer):
    return pltpu.make_async_remote_copy(
        src_ref=src, dst_ref=dst, send_sem=send, recv_sem=recv,
        device_id=peer, device_id_type=pl.DeviceIdType.MESH,
    )


ONES = 72
FRONT_IN = ("own_in", "own_cot", "wq", "wk", "wv", "w_out", "gain1", "bias", "table")
FRONT_OUT = ("cot", "normed", "q", "kv", "ctx", "lse", "resid")


def row_of(ref, count):
    parts = [ref[i : i + 1, :] for i in range(-(-count // 128))]
    return jnp.concatenate(parts, 1)[:, :count]


def weight_copies(hbm, dst, sems, first, blk):
    rows = dst["table"].shape[0]
    nq = hbm["wq"].shape[0]
    nk = hbm["wk"].shape[0]
    parts = [
        (hbm["wq"], dst["w_qkv"].at[0:nq, :]),
        (hbm["wk"], dst["w_qkv"].at[nq : nq + nk, :]),
        (hbm["wv"], dst["w_qkv"].at[nq + nk : nq + 2 * nk, :]),
        (hbm["table"].at[pl.ds(pl.multiple_of(blk * rows, rows), rows), :], dst["table"]),
    ]
    return [
        pltpu.make_async_copy(src, to, sems.at[first + i]) for i, (src, to) in enumerate(parts)
    ]


def front_kernel(heads, length_ref, *refs):
    ni, no = len(FRONT_IN), len(FRONT_OUT)
    hbm = dict(zip(FRONT_IN, refs[:ni]))
    out = dict(zip(FRONT_OUT, refs[ni : ni + no]))
    m = dict(zip(FRONT_OUT, refs[ni + no : ni + 2 * no]))
    (
        x, ctx_o, w_qkv, w_out, w_out_o, gain, bias, gain_rows, bias_rows, table, q1, k1, vt1, m_s, acc_s,
        load_sem, out_sem, pair_send, pair_recv, kv_send, kv_recv,
    ) = refs[ni + 2 * no :]
    rows, width = m["cot"].shape
    half = rows // 2
    blk, nb = lax.axis_index("blk"), lax.axis_size("blk")
    core = lax.axis_index("tensor")
    other = {"tensor": 1 - core}
    ours = pl.multiple_of(core * half, 16)
    theirs = pl.multiple_of((1 - core) * half, 16)
    start = blk * rows
    length = length_ref[0, 0]
    tile, tk = 256, 512

    loads = [
        pltpu.make_async_copy(hbm["own_in"], x.at[pl.ds(ours, half), :], load_sem.at[0]),
        pltpu.make_async_copy(hbm["own_cot"], m["cot"].at[pl.ds(ours, half), :], load_sem.at[1]),
        pltpu.make_async_copy(hbm["w_out"], w_out, load_sem.at[2]),
        pltpu.make_async_copy(hbm["gain1"], gain_rows, load_sem.at[3]),
        pltpu.make_async_copy(hbm["bias"], bias_rows, load_sem.at[4]),
    ] + weight_copies(hbm, dict(w_qkv=w_qkv, table=table), load_sem, 5, blk)
    for copy in loads:
        copy.start()
    meet([other] + [{"blk": lax.rem(blk + d, nb)} for d in range(1, nb)])

    def swap(k, src, dst):
        return remote(src, dst, pair_send.at[k], pair_recv.at[k], other)

    def x_swap():
        return swap(0, hbm["own_in"], x.at[pl.ds(ours, half), :])

    def cot_swap():
        return swap(1, hbm["own_cot"], m["cot"].at[pl.ds(ours, half), :])

    def ctx_swap():
        return swap(2, m["ctx"], ctx_o)

    def out_swap():
        return swap(3, hbm["w_out"], w_out_o)

    def save(name):
        i = FRONT_OUT.index(name)
        return pltpu.make_async_copy(m[name], out[name], out_sem.at[i])

    x_swap().start()
    cot_swap().start()
    out_swap().start()
    loads[0].wait()
    for copy in loads[2:]:
        copy.wait()
    nq = heads * HEAD
    gain[...] = row_of(gain_rows, width)
    bias[...] = row_of(bias_rows, nq + SLOT)
    lane = lax.broadcasted_iota(jnp.int32, (tile, SLOT), 1)

    def rows_in(first):
        def step(r, _):
            at = pl.ds(pl.multiple_of(first + r * tile, tile), tile)
            own = x[at, :].astype(f32)
            rho = lax.rsqrt(jnp.mean(own * own, axis=1, keepdims=True) + norm_eps)
            normed = (own * rho * gain[...]).astype(bf16)
            m["normed"][at, :] = normed
            factors = spread_table(table[at, :])
            proj = dot(normed, w_qkv[...], NT) + bias[...]
            zero = jnp.zeros((tile, HEAD), f32)
            for h in range(heads):
                cols = slice(h * SLOT, (h + 1) * SLOT)
                v = jnp.concatenate([proj[:, h * HEAD : (h + 1) * HEAD], zero], 1)
                v = turn(v, factors, 1.0).astype(bf16).astype(f32) * HEAD**-0.5
                m["q"][at, cols] = v.astype(bf16)
                q1[at, cols] = jnp.where(lane == HEAD, 1.0, v).astype(bf16)
            at_b = pl.ds(pl.multiple_of(start + first + r * tile, tile), tile)
            m["kv"][at_b, :] = turn(proj[:, nq:], factors, 1.0).astype(bf16)
            return 0

        lax.fori_loop(0, half // tile, step, 0)

    rows_in(ours)
    x_swap().wait()
    rows_in(theirs)

    def kv_copy(d):
        at = pl.ds(pl.multiple_of(blk * rows, rows), rows)
        return remote(
            m["kv"].at[at, :], m["kv"].at[at, :], kv_send.at[d - 1], kv_recv.at[d - 1],
            {"blk": lax.rem(blk + d, nb)},
        )

    for d in range(1, nb):
        @pl.when(blk + d < nb)
        def _(d=d):
            kv_copy(d).start()

    save("normed").start()
    save("q").start()
    wide_lane = lax.broadcasted_iota(jnp.int32, (tk, SLOT), 1)
    wide_row = lax.broadcasted_iota(jnp.int32, (tk, SLOT), 0)

    def prepare(first):
        at = pl.ds(pl.multiple_of(first, tk), tk)
        kv = m["kv"][at, :].astype(f32)
        dead = jnp.where(wide_row + first < length, 0.0, masked_value)
        k1[at, :] = jnp.where(
            wide_lane < HEAD, kv, jnp.where(wide_lane == HEAD, dead, 0.0)
        ).astype(bf16)
        vt1[0:HEAD, at] = jnp.transpose(kv)[HEAD:, :].astype(bf16)
        vt1[HEAD:, at] = jnp.ones((ONES - HEAD, tk), bf16)
        return at

    def attend(first, q0, diagonal):
        at = prepare(first)
        kt, vt = k1[at, :], vt1[:, at]
        n = rows - q0
        qs = slice(q0, rows)

        def score(h):
            s = dot(kt, q1[qs, h * SLOT : (h + 1) * SLOT], NT)
            if diagonal:
                ki = lax.broadcasted_iota(jnp.int32, (tk, n), 0)
                qi = lax.broadcasted_iota(jnp.int32, (tk, n), 1)
                s = jnp.where(ki <= qi, s, masked_value)
            return s

        def add(h, p, alpha):
            acc_s[h, :, qs] = acc_s[h, :, qs] * alpha + dot(vt, p, NN)

        ahead, behind = score(0), None
        for h in range(heads):
            s = ahead
            if h + 1 < heads:
                ahead = score(h + 1)
            m_prev = m_s[h : h + 1, qs]
            m_new = jnp.maximum(m_prev, jnp.max(s, axis=0, keepdims=True))
            alpha = jnp.exp(m_prev - m_new)
            p = jnp.exp(s - m_new).astype(bf16)
            m_s[h : h + 1, qs] = m_new
            if behind is not None:
                add(*behind)
            behind = (h, p, alpha)
        add(*behind)

    m_s[...] = jnp.full(m_s.shape, masked_value, f32)
    acc_s[...] = jnp.zeros(acc_s.shape, f32)
    for e in range(rows // tk):
        attend(start + e * tk, e * tk, True)

    def block(d, _):
        src = blk - d
        at = pl.ds(pl.multiple_of(src * rows, rows), rows)
        remote(
            m["kv"].at[at, :], m["kv"].at[at, :], kv_send.at[d - 1], kv_recv.at[d - 1],
            {"blk": src},
        ).wait_recv()

        def key_tile(i, _):
            attend(src * rows + i * tk, 0, False)
            return 0

        lax.fori_loop(0, rows // tk, key_tile, 0)
        return 0

    lax.fori_loop(1, blk + 1, block, 0)
    pos = lax.broadcasted_iota(jnp.int32, (1, rows), 1) + start
    zero = jnp.zeros((HEAD, rows), f32)
    for h in range(heads):
        acc = acc_s[h]
        total = acc[HEAD : HEAD + 1, :]
        ctx = jnp.transpose(jnp.concatenate([acc[:HEAD] / total, zero], 0))
        m["ctx"][:, h * HEAD : (h + 1) * HEAD] = ctx[:, :HEAD].astype(bf16)
        m["lse"][h : h + 1, :] = jnp.where(
            pos < length, m_s[h : h + 1, :] + jnp.log(total), -masked_value
        )
    m["lse"][heads:, :] = jnp.zeros((8 - heads, rows), f32)
    ctx_swap().start()
    save("ctx").start()
    save("lse").start()

    def kv_save(b):
        at = pl.ds(pl.multiple_of(b * rows, rows), rows)
        return pltpu.make_async_copy(
            m["kv"].at[at, :], out["kv"].at[at, :], out_sem.at[FRONT_OUT.index("kv")]
        )

    def keep_kv(b, _):
        kv_save(b).start()
        kv_save(b).wait()
        return 0

    loads[1].wait()
    cot_swap().wait()

    def mask(r, _):
        at = pl.ds(pl.multiple_of(r * tile, tile), tile)
        row = lax.broadcasted_iota(jnp.int32, (tile, width), 0) + start + r * tile
        m["cot"][at, :] = jnp.where(row < length, m["cot"][at, :].astype(f32), 0.0).astype(bf16)
        return 0

    lax.fori_loop(0, rows // tile, mask, 0)
    save("cot").start()
    lax.fori_loop(0, blk + 1, keep_kv, 0)
    for d in range(1, nb):
        @pl.when(blk + d < nb)
        def _(d=d):
            kv_copy(d).wait_send()

    out_swap().wait()
    ctx_swap().wait()

    def out_rows(r, _):
        at = pl.ds(pl.multiple_of(r * tile, tile), tile)
        m["resid"][at, :] = (
            x[at, :].astype(f32)
            + dot(m["ctx"][at, :], w_out[...], NN)
            + dot(ctx_o[at, :], w_out_o[...], NN)
        )
        pltpu.make_async_copy(
            m["resid"].at[at, :], out["resid"].at[at, :], out_sem.at[FRONT_OUT.index("resid")]
        ).start()
        return 0

    lax.fori_loop(0, rows // tile, out_rows, 0)
    for name in FRONT_OUT:
        if name != "kv":
            save(name).wait()


def front(length, values, heads, nb):
    half, width = values["own_in"].shape
    rows = 2 * half
    keys = rows * nb
    shape = jax.ShapeDtypeStruct
    outs = dict(
        cot=shape((rows, width), bf16),
        normed=shape((rows, width), bf16),
        q=shape((rows, heads * SLOT), bf16),
        kv=shape((keys, SLOT), bf16),
        ctx=shape((rows, heads * HEAD), bf16),
        lse=shape((8, rows), f32),
        resid=shape((rows, width), f32),
    )
    hbm = pl.BlockSpec(memory_space=pl.ANY)
    dma = pltpu.SemaphoreType.DMA
    vm = lambda a: pltpu.VMEM(a.shape, a.dtype)
    results = pl.pallas_call(
        functools.partial(front_kernel, heads),
        out_shape=[outs[name] for name in FRONT_OUT],
        in_specs=[pl.BlockSpec(memory_space=pltpu.SMEM)] + [hbm] * len(FRONT_IN),
        out_specs=[hbm] * len(FRONT_OUT),
        scratch_shapes=[vm(outs[name]) for name in FRONT_OUT]
        + [
            pltpu.VMEM((rows, width), bf16),
            pltpu.VMEM((rows, heads * HEAD), bf16),
            pltpu.VMEM((heads * HEAD + SLOT, width), bf16),
            vm(values["w_out"]),
            vm(values["w_out"]),
            pltpu.VMEM((1, width), f32),
            pltpu.VMEM((1, heads * HEAD + SLOT), f32),
            vm(values["gain1"]),
            vm(values["bias"]),
            pltpu.VMEM((rows, HEAD), f32),
            pltpu.VMEM((rows, heads * SLOT), bf16),
            pltpu.VMEM((keys, SLOT), bf16),
            pltpu.VMEM((ONES, keys), bf16),
            pltpu.VMEM((8, rows), f32),
            pltpu.VMEM((heads, ONES, rows), f32),
            dma((9,)),
            dma((len(FRONT_OUT),)),
            dma((4,)),
            dma((4,)),
            dma((nb - 1,)),
            dma((nb - 1,)),
        ],
        compiler_params=pltpu.CompilerParams(
            collective_id=1, has_side_effects=True, vmem_limit_bytes=58 * 2**20
        ),
        name="front",
    )(length, *[values[name] for name in FRONT_IN])
    return dict(zip(FRONT_OUT, results))


PART = 128
RING = 4
CHUNK = 3 * PART


class Stream:
    def __init__(self, first, count, axes):
        self.first, self.count = first, count
        self.reduce, self.sizes = [], []
        size = count
        for axis, bit in axes:
            if bit == "line":
                kinds = [("up", axis, 0), ("middle", axis, None), ("down", axis, 0)]
            elif size % 32 == 0 and size >= 64:
                kinds = [("half", axis, bit)]
                size //= 2
            else:
                kinds = [("full", axis, bit)]
            self.reduce += kinds
            self.sizes += [size] * len(kinds)
        self.gather = [(axis, bit) for kind, axis, bit in reversed(self.reduce) if kind == "half"]
        self.stages = len(self.reduce) + len(self.gather) + 1

    def scratch(self):
        copies = len(self.reduce) + len(self.gather)
        return [pltpu.VMEM((RING, self.sizes[0], CHUNK), bf16)] + [
            pltpu.VMEM((RING, size, CHUNK), bf16) for size in self.sizes
        ] + [
            pltpu.SemaphoreType.DMA((copies, RING)),
            pltpu.SemaphoreType.DMA((copies, RING)),
            pltpu.SemaphoreType.DMA((2, RING)),
        ]

    def bind(self, refs, sources, out):
        n = len(self.reduce)
        self.keep, self.got = refs[0], refs[1 : n + 1]
        self.send, self.recv, self.local = refs[n + 1 :]
        self.sources, self.out = sources, out
        self.peer, self.mine, offset = [], [], self.first
        self.sends, self.gets = [], []
        self.offsets = []
        for (kind, axis, bit), size in zip(self.reduce, self.sizes):
            at = lax.axis_index(axis)
            if kind == "middle":
                self.peer.append({axis: 3 - at})
            else:
                one = lax.rem(at // (1 << bit), 2)
                self.peer.append({axis: at + (1 - 2 * one) * (1 << bit)})
            middle = (at + 1) // 2 == 1
            self.middle = middle
            sends = {"up": jnp.logical_not(middle), "middle": middle, "down": middle}
            gets = {"up": middle, "middle": middle, "down": jnp.logical_not(middle)}
            self.sends.append(sends.get(kind))
            self.gets.append(gets.get(kind))
            self.mine.append(one if kind == "half" else 0)
            offset = offset + one * size if kind == "half" else offset
            self.offsets.append(offset)
        self.whole = []
        offset, size = self.offsets[-1], self.sizes[-1]
        self.gather_peer = []
        for k in reversed(range(n)):
            if self.reduce[k][0] == "half":
                self.whole.append((offset, size))
                self.gather_peer.append(self.peer[k])
                offset, size = offset - self.mine[k] * size, 2 * size

    def copy(self, k, ring, src, dst, peer):
        return pltpu.make_async_remote_copy(
            src_ref=src,
            dst_ref=dst,
            send_sem=self.send.at[k, ring],
            recv_sem=self.recv.at[k, ring],
            device_id=peer,
            device_id_type=pl.DeviceIdType.MESH,
        )

    def start_first(self, ring, source):
        size, one = self.sizes[0], self.mine[0]
        theirs = pl.multiple_of(self.first + (1 - one) * size, 16)
        own = pl.multiple_of(self.first + one * size, 16)
        self.copy(
            0, ring, source.at[pl.ds(theirs, size), :], self.got[0].at[ring], self.peer[0]
        ).start()
        pltpu.make_async_copy(
            source.at[pl.ds(own, size), :], self.keep.at[ring], self.local.at[0, ring]
        ).start()

    def reduce_copy(self, k, ring):
        if k == 0:
            src = self.keep.at[ring]
        elif self.reduce[k][0] == "half":
            size = self.sizes[k]
            theirs = pl.multiple_of((1 - self.mine[k]) * size, 16)
            src = self.got[k - 1].at[ring, pl.ds(theirs, size), :]
        else:
            src = self.got[k - 1].at[ring]
        return self.copy(k, ring, src, self.got[k].at[ring], self.peer[k])

    def gather_copy(self, t, ring, chunk):
        offset, size = self.whole[t]
        rows = pl.ds(pl.multiple_of(offset, 16), size)
        place = self.out.at[chunk, rows, :]
        src = self.got[-1].at[ring] if t == 0 else place
        return self.copy(len(self.reduce) + t, ring, src, place, self.gather_peer[t])

    def own_copy(self, ring, chunk):
        offset, size = self.whole[0]
        rows = pl.ds(pl.multiple_of(offset, 16), size)
        return pltpu.make_async_copy(
            self.got[-1].at[ring], self.out.at[chunk, rows, :], self.local.at[1, ring]
        )

    def stage(self, s, turn, chunk):
        ring = lax.rem(turn, RING)
        n = len(self.reduce)
        if s == 0:
            base = 0
            for count, place in self.sources:
                @pl.when((chunk >= base) & (chunk < base + count))
                def _(base=base, place=place):
                    self.start_first(ring, place(chunk - base))

                base += count
            return
        if s <= n:
            k = s - 1
            if k == 0:
                pltpu.make_async_copy(
                    self.got[0].at[ring], self.keep.at[ring], self.local.at[0, ring]
                ).wait()
            kind, size = self.reduce[k][0], self.sizes[k]
            copy = self.reduce_copy(k, ring)
            if kind in ("half", "full"):
                copy.wait()
                if k == 0:
                    own = self.keep[ring]
                elif kind == "half":
                    rows = pl.ds(pl.multiple_of(self.mine[k] * size, 16), size)
                    own = self.got[k - 1][ring, rows, :]
                else:
                    own = self.got[k - 1][ring]
                total = own.astype(f32) + self.got[k][ring].astype(f32)
                self.got[k][ring] = total.astype(bf16)
            else:
                pl.when(self.sends[k])(copy.wait_send)
                pl.when(self.gets[k])(copy.wait_recv)

                @pl.when(self.middle)
                def _():
                    if kind == "down":
                        self.got[k][ring] = self.got[k - 1][ring]
                    else:
                        total = self.got[k - 1][ring].astype(f32) + self.got[k][ring].astype(f32)
                        self.got[k][ring] = total.astype(bf16)

            if s < n:
                follow = self.reduce_copy(s, ring)
                if self.sends[s] is None:
                    follow.start()
                else:
                    pl.when(self.sends[s])(follow.start)
            else:
                self.own_copy(ring, chunk).start()
                self.gather_copy(0, ring, chunk).start()
            return
        t = s - n - 1
        self.gather_copy(t, ring, chunk).wait()
        if t == 0:
            self.own_copy(ring, chunk).wait()
        if t + 1 < len(self.gather):
            self.gather_copy(t + 1, ring, chunk).start()


def make_streams(width, plane, line):
    unit = width // 14
    short = [(line[0][0], "line")] if len(line) == 2 else line
    return [
        Stream(0, 5 * unit, plane + short),
        Stream(5 * unit, 5 * unit, plane[::-1] + short),
        Stream(10 * unit, 4 * unit, line + plane),
    ]


LOADS = ("resid", "cot", "gain1", "gain2", "w_out", "ctx", "q", "kv", "lse", "normed", "own_in")
FIRST = ("resid", "cot", "gain1", "gain2")
STREAMED = ("wq", "wk", "wv", "table", "w_gate", "w_up", "w_down")


def backward_kernel(heads, streams, n_ffn, n_small, *refs):
    nl, ns = len(LOADS), len(STREAMED)
    hbm = dict(zip(LOADS + STREAMED, refs[: nl + ns]))
    sums_ref, layer_out_ref, input_grad_ref, grads_ref = refs[nl + ns : nl + ns + 4]
    refs = list(refs[nl + ns + 4 :])
    m = dict(zip(LOADS, refs[:nl]))
    refs = refs[nl:]
    (
        load_sem, w_qkv, table_s, up_t, cot_t, wide, trio, acc, out_s, wgu, wd, made,
        w_sem, made_sem, dmid_o, part_o, dlow, delta, dkv, dkv_o, k0, small,
        din_o, rowsum, pair_send, pair_recv, kv_send, kv_recv, out_sem,
        gain_own, gain_o, dq_t, k_t, gain1, gain2,
    ) = refs[:35]
    refs = refs[35:]
    mlp = do = wide
    dmid_s = acc
    dproj = trio
    vec = acc.at[0:SLOT, :]
    din_own = dmid_o.at[0 : dmid_o.shape[0] // 2, :]
    to_send = wd
    rows, width = m["cot"].shape
    half = rows // 2
    blk, nb = lax.axis_index("blk"), lax.axis_size("blk")
    core = lax.axis_index("tensor")
    nz = lax.axis_size("batch")
    other = {"tensor": 1 - core}
    tile = 256
    nq = heads * HEAD
    qkv = nq + SLOT

    pos = 0
    for st in streams:
        cnt = len(st.scratch())
        st.bind(
            refs[pos : pos + cnt],
            [(n_ffn, lambda c: grads_ref.at[c]), (n_small, lambda c: small.at[c])],
            sums_ref,
        )
        pos += cnt

    loads = {
        name: pltpu.make_async_copy(hbm[name], m[name], load_sem.at[i])
        for i, name in enumerate(LOADS)
    }
    late = weight_copies(hbm, dict(w_qkv=w_qkv, table=table_s), load_sem, nl, blk)

    n_pairs = -(-n_ffn // 2)
    odd = n_ffn % 2 == 1
    wide2 = 2 * PART

    def weights(p, count):
        slot = lax.rem(p, 2)
        cols = pl.ds(pl.multiple_of(p * wide2, wide2), count)
        return [
            pltpu.make_async_copy(
                hbm["w_gate"].at[:, cols], wgu.at[slot, :, 0:count], w_sem.at[0, slot]
            ),
            pltpu.make_async_copy(
                hbm["w_up"].at[:, cols], wgu.at[slot, :, wide2 : wide2 + count], w_sem.at[1, slot]
            ),
            pltpu.make_async_copy(
                hbm["w_down"].at[cols, :],
                wd.at[pl.ds(pl.multiple_of(slot * wide2, wide2), count), :],
                w_sem.at[2, slot],
            ),
        ]

    def for_weights(p, act):
        last = n_pairs - 1 if odd else n_pairs

        @pl.when(p < last)
        def _():
            for copy in weights(p, wide2):
                act(copy)

        if odd:
            @pl.when(p == last)
            def _():
                for copy in weights(p, PART):
                    act(copy)

    for name in FIRST:
        loads[name].start()
    for_weights(0, lambda copy: copy.start())
    for_weights(1, lambda copy: copy.start())
    for name in LOADS:
        if name not in FIRST:
            loads[name].start()
    for copy in late:
        copy.start()

    batch = lax.axis_index("batch")
    meet(
        [other]
        + [{"blk": lax.rem(blk + d, nb)} for d in range(1, nb)]
        + [
            {"batch": batch + (1 - 2 * lax.rem(batch // (1 << b), 2)) * (1 << b)}
            for b in range(int(math.log2(nz)))
        ]
        + ([{"batch": 3 - batch}] if nz == 4 else [])
    )

    def swap(k, src, dst):
        return remote(src, dst, pair_send.at[k], pair_recv.at[k], other)

    def dmid_swap():
        return swap(0, dlow, dmid_o)

    theirs = pl.multiple_of((1 - core) * half, 16)
    ours = pl.multiple_of(core * half, 16)

    def part_swap():
        return swap(1, to_send, part_o)

    def din_swap():
        return swap(2, to_send, din_o)

    def gain_swap():
        return swap(3, gain_own, gain_o)

    def put(first, at, value):
        done, n = 0, value.shape[1]
        while done < n:
            c, lane = divmod(first + done, CHUNK)
            take = min(n - done, CHUNK - lane)
            small[c, at, lane : lane + take] = value[:, done : done + take].astype(bf16)
            done += take

    tq, tk = 256, 512

    def begin():
        for name in FIRST:
            loads[name].wait()
        gain1[...] = row_of(m["gain1"], width)
        gain2[...] = row_of(m["gain2"], width)

        def step(r, _):
            at = pl.ds(pl.multiple_of(r * tile, tile), tile)
            resid = m["resid"][at, :]
            rho = lax.rsqrt(jnp.mean(resid * resid, axis=1, keepdims=True) + norm_eps)
            normed = resid * rho * gain2[...]
            mlp[at, :] = normed.astype(bf16)
            up_t[:, at] = jnp.transpose(normed).astype(bf16)
            cot_t[:, at] = jnp.transpose(m["cot"][at, :].astype(f32)).astype(bf16)
            return 0

        lax.fori_loop(0, rows // tile, step, 0)
        dmid_s[...] = jnp.zeros(dmid_s.shape, f32)
        out_s[...] = jnp.zeros(out_s.shape, f32)

    def made_copy(p):
        slot = lax.rem(p, 2)
        return pltpu.make_async_copy(
            made.at[slot], grads_ref.at[pl.ds(p * 2, 2)], made_sem.at[slot]
        )

    def feed_forward(p):
        slot = lax.rem(p, 2)

        @pl.when(p >= 2)
        def _():
            made_copy(p - 1).wait()

        for_weights(p, lambda copy: copy.wait())
        if odd:
            @pl.when(p == n_pairs - 1)
            def _():
                wgu[slot, :, PART:wide2] = jnp.zeros((width, PART), bf16)
                wgu[slot, :, wide2 + PART :] = jnp.zeros((width, PART), bf16)
                rest = pl.ds(pl.multiple_of(slot * wide2 + PART, PART), PART)
                wd[rest, :] = jnp.zeros((PART, width), bf16)

        w_gu = wgu[slot]
        w_d = wd[pl.ds(pl.multiple_of(slot * wide2, wide2), wide2), :]
        for r in range(rows // tile):
            at = slice(r * tile, (r + 1) * tile)
            both = dot(mlp[at, :], w_gu, NN)
            gate, upper = both[:, :wide2], both[:, wide2:]
            d_hidden = dot(m["cot"][at, :], w_d, NT)
            sigma = 1.0 / (1.0 + jnp.exp(-gate))
            activ = gate * sigma
            hidden = (activ * upper).astype(bf16)
            d_gate = (d_hidden * upper * sigma * (1.0 + gate * (1.0 - sigma))).astype(bf16)
            d_up = (d_hidden * activ).astype(bf16)
            d_pair = jnp.concatenate([d_gate, d_up], 1)
            trio[at, :wide2] = hidden
            trio[at, wide2:] = d_pair
            out_s[at, :] += dot(hidden, w_d, NN)
            dmid_s[at, :] += dot(d_pair, w_gu, NT)
        for r in range(2):
            at = slice(r * width // 2, (r + 1) * width // 2)
            down = dot(cot_t[at, :], trio[:, :wide2], NN).astype(bf16)
            pairs = dot(up_t[at, :], trio[:, wide2:], NN).astype(bf16)
            for c in range(2):
                cols = slice(c * PART, (c + 1) * PART)
                made[slot, c, at, :PART] = down[:, cols]
                made[slot, c, at, PART : 2 * PART] = pairs[:, cols]
                made[slot, c, at, 2 * PART :] = pairs[:, wide2 + c * PART : wide2 + (c + 1) * PART]
        made_copy(p).start()
        for_weights(p + 2, lambda copy: copy.start())

        @pl.when(p == 0)
        def _():
            made_copy(p).wait()

    def hand_over():
        made_copy(n_pairs - 1).wait()

        def step(r, _):
            at = pl.ds(pl.multiple_of(r * tile, tile), tile)
            dlow[at, :] = dmid_s[at, :].astype(bf16)
            return 0

        lax.fori_loop(0, rows // tile, step, 0)
        dmid_swap().start()

        def step_part(r, _):
            at = pl.ds(pl.multiple_of(r * tile, tile), tile)
            src = pl.ds(pl.multiple_of(theirs + r * tile, tile), tile)
            to_send[at, :] = out_s[src, :].astype(bf16)
            return 0

        lax.fori_loop(0, half // tile, step_part, 0)
        part_swap().start()

    def before():
        for name in LOADS:
            if name not in FIRST + ("kv",):
                loads[name].wait()
        for copy in late:
            copy.wait()
        dmid_swap().wait()
        part_swap().wait()
        vec[...] = jnp.zeros(vec.shape, f32)

        def out_rows(r, _):
            at = pl.ds(pl.multiple_of(r * tile, tile), tile)
            mine = pl.ds(pl.multiple_of(ours + r * tile, tile), tile)
            part_o[at, :] = (
                m["resid"][mine, :] + out_s[mine, :] + part_o[at, :].astype(f32)
            ).astype(bf16)
            return 0

        lax.fori_loop(0, half // tile, out_rows, 0)
        pltpu.make_async_copy(part_o, layer_out_ref, out_sem.at[0]).start()

        head = lax.broadcasted_iota(jnp.int32, (8, nq), 0)
        column = lax.broadcasted_iota(jnp.int32, (8, nq), 1)
        inside = (column >= head * HEAD) & (column < (head + 1) * HEAD)
        of_head = jnp.where(inside, 1.0, 0.0).astype(bf16)

        def norm(r, _):
            at = pl.ds(pl.multiple_of(r * tile, tile), tile)
            dmid = dlow[at, :].astype(f32) + dmid_o[at, :].astype(f32)
            resid = m["resid"][at, :]
            rho = lax.rsqrt(jnp.mean(resid * resid, axis=1, keepdims=True) + norm_eps)
            n2 = resid * rho
            vec[1:2, :] += jnp.sum(dmid * n2, axis=0, keepdims=True)
            weighted = dmid * gain2[...]
            d_resid = m["cot"][at, :].astype(f32) + rho * (
                weighted - n2 * jnp.mean(weighted * n2, axis=1, keepdims=True)
            )
            m["resid"][at, :] = d_resid
            low = d_resid.astype(bf16)
            dlow[at, :] = low
            d_ctx = dot(low, m["w_out"][...], NT).astype(bf16).astype(f32)
            zero = jnp.zeros((tile, HEAD), f32)
            for h in range(heads):
                own = d_ctx[:, h * HEAD : (h + 1) * HEAD]
                do[at, h * SLOT : (h + 1) * SLOT] = jnp.concatenate([zero, own], 1).astype(bf16)
            rest = d_ctx * m["ctx"][at, :].astype(f32)
            total = jnp.zeros((8, tile), f32)
            for _ in range(3):
                term = rest.astype(bf16)
                total = total + dot(of_head, term, NT)
                rest = rest - term.astype(f32)
            delta[:, at] = total
            return 0

        lax.fori_loop(0, rows // tile, norm, 0)

    def keys_first():
        loads["kv"].wait()
        lane = lax.broadcasted_iota(jnp.int32, (tk, SLOT), 1)

        def keys(i, _):
            at = pl.ds(pl.multiple_of(i * tk, tk), tk)
            kv = m["kv"][at, :].astype(f32)
            k0[at, :] = jnp.where(lane < HEAD, kv, 0.0).astype(bf16)
            k_t[:, at] = jnp.transpose(kv)[:HEAD, :].astype(bf16)
            return 0

        lax.fori_loop(0, (blk + 1) * (rows // tk), keys, 0)
        dq_t[...] = jnp.zeros(dq_t.shape, f32)

    def grad_out():
        def step(k, _):
            at = pl.ds(pl.multiple_of(k * 128, 128), 128)
            put(0, at, dot(dlow[:, at], m["ctx"][...], TN))
            return 0

        lax.fori_loop(0, width // 128, step, 0)

    def pair(kt, kvt, kt_t, qt, masked):
        at = pl.ds(pl.multiple_of(qt * tq, tq), tq)

        def score(h):
            cols = slice(h * SLOT, (h + 1) * SLOT)
            return dot(kt, m["q"][at, cols], NT), dot(kvt, do[at, cols], NT)

        def add(h, p, ds):
            cols = slice(h * SLOT, (h + 1) * SLOT)
            dq_t[h, :, at] += dot(kt_t, ds, NN)
            return dot(
                jnp.concatenate([ds, p], 1),
                jnp.concatenate([m["q"][at, cols], do[at, cols]], 0),
                NN,
            )

        grad, ahead, behind = None, score(0), None
        for h in range(heads):
            s, dp = ahead
            if h + 1 < heads:
                ahead = score(h + 1)
            p = jnp.exp(s - m["lse"][h : h + 1, at])
            if masked is not None:
                p = jnp.where(masked, p, 0.0)
            ds = (p * (dp - delta[h : h + 1, at])).astype(bf16)
            if behind is not None:
                part = add(*behind)
                grad = part if grad is None else grad + part
            behind = (h, p.astype(bf16), ds)
        return grad + add(*behind)

    def own_tile(e):
        ki = lax.broadcasted_iota(jnp.int32, (tk, tq), 0)
        qi = lax.broadcasted_iota(jnp.int32, (tk, tq), 1)
        at_k = pl.ds(pl.multiple_of(blk * rows + e * tk, tk), tk)
        kt, kvt, kt_t = k0[at_k, :], m["kv"][at_k, :], k_t[:, at_k]
        first = e * (tk // tq)

        def near(j, grad):
            return grad + pair(kt, kvt, kt_t, first + j, ki <= qi + j * tq)

        def far(qt, grad):
            return grad + pair(kt, kvt, kt_t, qt, None)

        grad = lax.fori_loop(0, tk // tq, near, jnp.zeros((tk, SLOT), f32))
        grad = lax.fori_loop(first + tk // tq, rows // tq, far, grad)
        dkv[at_k, :] = grad.astype(bf16)

    def earlier(i):
        at_k = pl.ds(pl.multiple_of(i * tk, tk), tk)
        kt, kvt, kt_t = k0[at_k, :], m["kv"][at_k, :], k_t[:, at_k]

        def step(qt, grad):
            return grad + pair(kt, kvt, kt_t, qt, None)

        grad = lax.fori_loop(0, rows // tq, step, jnp.zeros((tk, SLOT), f32))
        dkv[at_k, :] = grad.astype(bf16)

    def kv_copy(d):
        to = lax.rem(blk + d, nb)
        at = pl.ds(pl.multiple_of(to * rows, rows), rows)
        return remote(
            dkv.at[at, :], dkv_o.at[d - 1], kv_send.at[d - 1], kv_recv.at[d - 1], {"blk": to}
        )

    def kv_start():
        for d in range(1, nb):
            @pl.when(lax.rem(blk + d, nb) < blk)
            def _(d=d):
                kv_copy(d).start()

    def project_queries():
        def step(r, _):
            at = pl.ds(pl.multiple_of(r * tile, tile), tile)
            table = spread_table(table_s[at, :])
            zero = jnp.zeros((HEAD, tile), f32)
            for h in range(heads):
                v = jnp.transpose(jnp.concatenate([dq_t[h, :, at], zero], 0))
                v = turn(v * HEAD**-0.5, table, -1.0)
                dproj[at, h * HEAD : (h + 1) * HEAD] = v[:, :HEAD].astype(bf16)
            return 0

        lax.fori_loop(0, rows // tile, step, 0)

    def project():
        for d in range(1, nb):
            @pl.when(lax.rem(blk + d, nb) < blk)
            def _(d=d):
                kv_copy(d).wait_send()

            @pl.when(lax.rem(blk + nb - d, nb) > blk)
            def _(d=d):
                kv_copy(d).wait_recv()
                for r in range(rows // tile):
                    at = pl.ds(pl.multiple_of(blk * rows + r * tile, tile), tile)
                    total = dkv[at, :].astype(f32) + dkv_o[d - 1, r * tile : (r + 1) * tile].astype(f32)
                    dkv[at, :] = total.astype(bf16)

        rowsum[...] = jnp.zeros(rowsum.shape, f32)

        def unrotate(r, _):
            at = pl.ds(pl.multiple_of(r * tile, tile), tile)
            at_b = pl.ds(pl.multiple_of(blk * rows + r * tile, tile), tile)
            table = spread_table(table_s[at, :])
            dproj[at, nq:qkv] = turn(dkv[at_b, :].astype(f32), table, -1.0).astype(bf16)
            rowsum[0:1, :] += jnp.sum(dproj[at, :qkv].astype(f32), axis=0, keepdims=True)
            return 0

        lax.fori_loop(0, rows // tile, unrotate, 0)

        def d_in(to, first):
            def step(r, _):
                src = pl.ds(pl.multiple_of(first + r * tile, tile), tile)
                at = pl.ds(pl.multiple_of(r * tile, tile), tile)
                to[at, :] = dot(dproj[src, :qkv], w_qkv[...], NN).astype(bf16)
                return 0

            lax.fori_loop(0, half // tile, step, 0)

        d_in(to_send, theirs)
        din_swap().start()
        d_in(din_own, ours)

        def grads(k, _):
            at = pl.ds(pl.multiple_of(k * 128, 128), 128)
            put(nq, at, dot(m["normed"][:, at], dproj[:, :qkv], TN))
            return 0

        lax.fori_loop(0, width // 128, grads, 0)

    def finish():
        din_swap().wait()

        def step(r, _):
            at = pl.ds(pl.multiple_of(r * tile, tile), tile)
            mine = pl.ds(pl.multiple_of(ours + r * tile, tile), tile)
            d_in = din_own[at, :].astype(f32) + din_o[at, :].astype(f32)
            x = m["own_in"][at, :].astype(f32)
            rho = lax.rsqrt(jnp.mean(x * x, axis=1, keepdims=True) + norm_eps)
            n1 = x * rho
            vec[0:1, :] += jnp.sum(d_in * n1, axis=0, keepdims=True)
            weighted = d_in * gain1[...]
            grad = m["resid"][mine, :] + rho * (
                weighted - n1 * jnp.mean(weighted * n1, axis=1, keepdims=True)
            )
            din_own[at, :] = grad.astype(bf16)
            return 0

        lax.fori_loop(0, half // tile, step, 0)
        pltpu.make_async_copy(din_own, input_grad_ref, out_sem.at[1]).start()
        gain_own[...] = vec[0:8, :]
        gain_swap().start()
        vec[2:3, : nq + SLOT] = rowsum[0:1, :]
        gain_swap().wait()
        vec[0:1, :] = gain_own[0:1, :] + gain_o[0:1, :]
        put(2 * nq + SLOT, slice(None), jnp.transpose(vec[...]))

    plan = slots_of(n_ffn, rows // tk, nb)

    def compute(i):
        pl.when(i == 0)(begin)
        few = plan["singles"]
        count = jnp.where(i < few, 1, jnp.where(i < plan["before"], 2, 0))
        first = jnp.where(i < few, i, 2 * i - few)
        count = jnp.minimum(count, jnp.maximum(n_pairs - first, 0))

        def step(c, _):
            feed_forward(first + c)
            return 0

        lax.fori_loop(0, count, step, 0)
        pl.when(i == max(plan["before"] - 3, 0))(keys_first)
        pl.when(i == plan["before"] - 1)(hand_over)
        pl.when(i == plan["before"])(before)

        @pl.when((i >= plan["own"]) & (i < plan["own"] + rows // tk))
        def _():
            own_tile(i - plan["own"])

        pl.when(i == plan["early"] - 1)(grad_out)

        @pl.when((i >= plan["early"]) & (i - plan["early"] < blk * (rows // tk)))
        def _():
            earlier(i - plan["early"])

        pl.when(i == plan["queries"] - 1)(kv_start)
        pl.when(i == plan["queries"])(project_queries)
        pl.when(i == plan["queries"] + 1)(project)
        pl.when(i == plan["queries"] + 2)(finish)

    early_turn = min(plan["early"] - 1, n_ffn)
    gap = max(0, plan["queries"] + 2 - n_ffn - n_small + 1)
    n = n_ffn + n_small + gap
    depth = max(st.stages for st in streams)

    def chunk_of(t):
        late = jnp.where(t <= n_ffn, t - 1, t - gap)
        return jnp.where(t < early_turn, t, jnp.where(t == early_turn, n_ffn, late))

    def slot(i, _):
        compute(i)
        for st in streams[::-1]:
            for s in reversed(range(st.stages)):
                t = i - s
                real = (t >= 0) & (t < n)
                if gap:
                    real = real & ((t <= n_ffn) | (t > n_ffn + gap))

                @pl.when(real)
                def _(st=st, s=s, t=t):
                    st.stage(s, t, chunk_of(t))

        return 0

    lax.fori_loop(0, n + depth - 1, slot, 0)
    pltpu.make_async_copy(part_o, layer_out_ref, out_sem.at[0]).wait()
    pltpu.make_async_copy(din_own, input_grad_ref, out_sem.at[1]).wait()


def slots_of(n_ffn, tiles, nb):
    pairs = -(-n_ffn // 2)
    singles = pairs
    before = singles + -(-(pairs - singles) // 2)
    own = before + 1
    early = own + tiles
    return dict(
        singles=singles, before=before, own=own, early=early, queries=early + (nb - 1) * tiles
    )


def backward(values, heads, plane, line, nb):
    rows, width = values["cot"].shape
    half = rows // 2
    keys = values["kv"].shape[0]
    n_ffn = values["w_gate"].shape[1] // PART
    n_small = -(-(2 * heads * HEAD + 2 * SLOT) // CHUNK)
    streams = make_streams(width, plane, line)
    hbm = pl.BlockSpec(memory_space=pl.ANY)
    dma = pltpu.SemaphoreType.DMA
    vm = pltpu.VMEM
    assert half == 4 * PART and heads * SLOT == width
    scratch = [vm(values[name].shape, values[name].dtype) for name in LOADS]
    scratch += [
        dma((len(LOADS) + 4,)),
        vm((heads * HEAD + SLOT, width), bf16),
        vm((rows, HEAD), f32),
        vm((width, rows), bf16),
        vm((width, rows), bf16),
        vm((rows, width), bf16),
        vm((rows, 2 * CHUNK), bf16),
        vm((rows, width), f32),
        vm((rows, width), f32),
        vm((2, width, 4 * PART), bf16),
        vm((4 * PART, width), bf16),
        vm((2, 2, width, CHUNK), bf16),
        dma((3, 2)),
        dma((2,)),
        vm((rows, width), bf16),
        vm((half, width), bf16),
        vm((rows, width), bf16),
        vm((8, rows), f32),
        vm((keys, SLOT), bf16),
        vm((nb - 1, rows, SLOT), bf16),
        vm((keys, SLOT), bf16),
        vm((n_small, width, CHUNK), bf16),
        vm((half, width), bf16),
        vm((8, heads * HEAD + SLOT), f32),
        dma((4,)),
        dma((4,)),
        dma((nb - 1,)),
        dma((nb - 1,)),
        dma((2,)),
        vm((8, width), f32),
        vm((8, width), f32),
        vm((heads, HEAD, rows), f32),
        vm((HEAD, keys), bf16),
        vm((1, width), f32),
        vm((1, width), f32),
    ]
    for st in streams:
        scratch += st.scratch()
    return pl.pallas_call(
        functools.partial(backward_kernel, heads, streams, n_ffn, n_small),
        out_shape=(
            jax.ShapeDtypeStruct((n_ffn + n_small, width, CHUNK), bf16),
            jax.ShapeDtypeStruct((half, width), bf16),
            jax.ShapeDtypeStruct((half, width), bf16),
            jax.ShapeDtypeStruct((n_ffn + n_ffn % 2, width, CHUNK), bf16),
        ),
        in_specs=[hbm] * (len(LOADS) + len(STREAMED)),
        out_specs=(hbm, hbm, hbm, hbm),
        scratch_shapes=scratch,
        compiler_params=pltpu.CompilerParams(
            collective_id=0, has_side_effects=True, vmem_limit_bytes=60 * 2**20
        ),
        name="backward",
    )(*[values[name] for name in LOADS + STREAMED])


def unpack_kernel(heads, n_small, chunk_ref, *refs):
    small = refs[:n_small]
    rows_in, refs = refs[n_small : n_small + 2], refs[n_small + 2 :]
    rows_out, refs = refs[-2:], refs[:-2]
    for src, dst in zip(rows_in, rows_out):
        dst[...] = src[...]
    down, gate, up, g_out, g_q, g_k, g_v, gain1, gain2, bias = refs
    step = pl.program_id(0)
    for c in range(2):
        value, at = chunk_ref[c], slice(c * PART, (c + 1) * PART)
        down[at, :] = jnp.transpose(value[:, :PART].astype(f32))
        gate[:, at] = value[:, PART : 2 * PART].astype(f32)
        up[:, at] = value[:, 2 * PART :].astype(f32)

    def take(first, count):
        done = 0
        while done < count:
            c, lane = divmod(first + done, CHUNK)
            n = min(count - done, SLOT - lane % SLOT)
            yield done, n, small[c][0, :, lane : lane + n].astype(f32)
            done += n

    @pl.when(step == 0)
    def _():
        nq = heads * HEAD
        for done, n, piece in take(0, nq):
            g_out[done : done + n, :] = jnp.transpose(piece)
        for done, n, piece in take(nq, nq):
            g_q[done : done + n, :] = jnp.transpose(piece)
        for done, n, piece in take(2 * nq, HEAD):
            g_k[...] = jnp.transpose(piece)
        for done, n, piece in take(2 * nq + HEAD, HEAD):
            g_v[...] = jnp.transpose(piece)
        for done, n, piece in take(2 * nq + 2 * HEAD, SLOT):
            vec = jnp.transpose(piece)
            for row, to in ((0, gain1), (1, gain2), (2, bias)):
                for i in range(to.shape[0]):
                    to[i : i + 1, :] = vec[row : row + 1, i * 128 : (i + 1) * 128]


def unpack(sums, layer_out, input_grad, n_ffn, heads):
    n, width, _ = sums.shape
    n_small = n - n_ffn
    shape = lambda *dims: jax.ShapeDtypeStruct(dims, f32)
    nq = heads * HEAD
    lanes = [(width // 128, 128), (width // 128, 128), (-(-(nq + SLOT) // 128), 128)]
    whole = [(nq, width), (nq, width), (HEAD, width), (HEAD, width)] + lanes
    half = layer_out.shape[0]
    steps = -(-n_ffn // 2)
    cut = max(c for c in (1, 2, 4, 8) if c <= steps)
    rows = pl.BlockSpec((half // cut, width), lambda j: (jnp.minimum(j, cut - 1), 0))
    return pl.pallas_call(
        functools.partial(unpack_kernel, heads, n_small),
        grid=(-(-n_ffn // 2),),
        out_shape=[
            shape(n_ffn * PART, width), shape(width, n_ffn * PART), shape(width, n_ffn * PART)
        ] + [shape(*dims) for dims in whole] + [
            jax.ShapeDtypeStruct((half, width), bf16)
        ] * 2,
        in_specs=[pl.BlockSpec((2, width, CHUNK), lambda j: (j, 0, 0))]
        + [
            pl.BlockSpec((1, width, CHUNK), lambda j, c=c: (n_ffn + c, 0, 0))
            for c in range(n_small)
        ] + [rows, rows],
        out_specs=[
            pl.BlockSpec((2 * PART, width), lambda j: (j, 0)),
            pl.BlockSpec((width, 2 * PART), lambda j: (0, j)),
            pl.BlockSpec((width, 2 * PART), lambda j: (0, j)),
        ] + [pl.BlockSpec(dims, lambda j: (0, 0)) for dims in whole] + [rows, rows],
        compiler_params=pltpu.CompilerParams(
            vmem_limit_bytes=48 * 2**20, dimension_semantics=("arbitrary",)
        ),
        name="unpack",
    )(*[sums] * (1 + n_small), layer_out, input_grad)


def shards(
    layer_in, cotangent, lengths, attn_gain, w_query, query_bias, w_key, key_bias, w_value,
    value_bias, w_out, mlp_gain, w_gate, w_up, w_down,
):
    half, width = layer_in.shape
    rows = half * lax.axis_size("tensor")
    nb = lax.axis_size("blk")
    heads = w_query.shape[1] // HEAD
    biases = jnp.concatenate([query_bias, key_bias, value_bias]).astype(f32)
    biases = jnp.pad(biases, (0, -biases.shape[0] % 128)).reshape(-1, 128)
    values = dict(
        own_in=layer_in, own_cot=cotangent, wq=w_query.T, wk=w_key.T, wv=w_value.T, w_out=w_out,
        gain1=attn_gain.reshape(-1, 128), gain2=mlp_gain.reshape(-1, 128), bias=biases,
        table=jnp.asarray(rotary_table(rows * nb)), w_gate=w_gate, w_up=w_up, w_down=w_down,
    )
    values |= front(lengths, values, heads, nb)
    sums, layer_out, input_grad, _ = backward(
        values, heads, bits_of("blk"), bits_of("batch"), nb
    )
    (
        g_down, g_gate, g_up, g_out, g_query, g_key, g_value, g_gain1, g_gain2, g_bias,
        layer_out, input_grad,
    ) = unpack(sums, layer_out, input_grad, w_gate.shape[1] // PART, heads)
    nq = heads * HEAD
    g_bias = g_bias.reshape(-1)
    return (
        layer_out, input_grad, g_gain1.reshape(-1), g_query.T, g_bias[:nq], g_key.T,
        g_bias[nq : nq + HEAD], g_value.T, g_bias[nq + HEAD : nq + 2 * HEAD], g_out,
        g_gain2.reshape(-1), g_gate, g_up, g_down,
    )


def solution(mesh):
    rows = P(("batch", "blk", "tensor"), None)
    cols, part, split = P(None, "tensor"), P("tensor"), P("tensor", None)
    return jax.shard_map(
        shards,
        mesh=mesh,
        in_specs=(
            rows, rows, P("batch", None), P(), cols, part, cols, part, cols, part, split, P(),
            cols, cols, split,
        ),
        out_specs=(
            rows, rows, P(), cols, part, cols, part, cols, part, split, P(), cols, cols, split,
        ),
        check_vma=False,
    )
```

```python
import functools
import math

import jax
import jax.numpy as jnp
import numpy as np
from jax import lax
from jax.experimental import pallas as pl
from jax.experimental.pallas import tpu as pltpu
from jax.sharding import PartitionSpec as P

HEAD = 64
SLOT = 128

rope_base = 1000000.0
norm_eps = 1e-06
masked_value = -1e30
bf16 = jnp.bfloat16
f32 = jnp.float32


def dot(left, right, dims, kind=f32):
    return lax.dot_general(left, right, (dims, ((), ())), preferred_element_type=kind)


NN = ((1,), (0,))
NT = ((1,), (1,))
TN = ((0,), (0,))


def bits_of(mesh_axis):
    return [(mesh_axis, bit) for bit in range(int(math.log2(lax.axis_size(mesh_axis))))]


def rotary_table(count):
    half = HEAD // 2
    freq = np.float32(rope_base) ** (-(np.arange(half, dtype=np.float32) * np.float32(2.0)) / np.float32(HEAD))
    phase = np.arange(count, dtype=np.float32)[:, None] * freq[None, :].astype(np.float32)
    phase = phase.astype(np.float64)
    return np.concatenate([np.cos(phase), np.sin(phase)], 1).astype(np.float32)


def spread_table(table):
    n = table.shape[0]
    wide = jnp.concatenate([table, jnp.zeros_like(table)], 1)
    lane = lax.broadcasted_iota(jnp.int32, (n, SLOT), 1)
    cosine = jnp.where(lane < 32, wide, jnp.where(lane < HEAD, pltpu.roll(wide, 32, 1), 1.0))
    sine_a = jnp.where(lane < 32, pltpu.roll(wide, SLOT - 32, 1), 0.0)
    sine_b = jnp.where((lane >= 32) & (lane < HEAD), wide, 0.0)
    return cosine, sine_a, sine_b


def turn(v, table, sign):
    cosine, sine_a, sine_b = table
    return v * cosine + sign * (
        pltpu.roll(v, 32, 1) * sine_b - pltpu.roll(v, SLOT - 32, 1) * sine_a
    )


def meet(peers):
    barrier = pltpu.get_barrier_semaphore()
    for peer in peers:
        pl.semaphore_signal(barrier, 1, device_id=peer, device_id_type=pl.DeviceIdType.MESH)
    pl.semaphore_wait(barrier, len(peers))


def remote(src, dst, send, recv, peer):
    return pltpu.make_async_remote_copy(
        src_ref=src, dst_ref=dst, send_sem=send, recv_sem=recv,
        device_id=peer, device_id_type=pl.DeviceIdType.MESH,
    )


ONES = 72
FRONT_IN = ("own_in", "own_cot", "wq", "wk", "wv", "w_out", "gain1", "bias", "table")
FRONT_OUT = ("cot", "normed", "q", "kv", "ctx", "lse", "resid")


def row_of(ref, count):
    parts = [ref[i : i + 1, :] for i in range(-(-count // 128))]
    return jnp.concatenate(parts, 1)[:, :count]


def weight_copies(hbm, dst, sems, first, blk):
    rows = dst["table"].shape[0]
    nq = hbm["wq"].shape[0]
    nk = hbm["wk"].shape[0]
    parts = [
        (hbm["wq"], dst["w_qkv"].at[0:nq, :]),
        (hbm["wk"], dst["w_qkv"].at[nq : nq + nk, :]),
        (hbm["wv"], dst["w_qkv"].at[nq + nk : nq + 2 * nk, :]),
        (hbm["table"].at[pl.ds(pl.multiple_of(blk * rows, rows), rows), :], dst["table"]),
    ]
    return [
        pltpu.make_async_copy(src, to, sems.at[first + i]) for i, (src, to) in enumerate(parts)
    ]


def front_kernel(heads, length_ref, *refs):
    ni, no = len(FRONT_IN), len(FRONT_OUT)
    hbm = dict(zip(FRONT_IN, refs[:ni]))
    out = dict(zip(FRONT_OUT, refs[ni : ni + no]))
    m = dict(zip(FRONT_OUT, refs[ni + no : ni + 2 * no]))
    (
        x, ctx_o, w_qkv, w_out, w_out_o, gain, bias, gain_rows, bias_rows, table, q1, k1, vt1, m_s, acc_s,
        load_sem, out_sem, pair_send, pair_recv, kv_send, kv_recv,
    ) = refs[ni + 2 * no :]
    rows, width = m["cot"].shape
    half = rows // 2
    blk, nb = lax.axis_index("blk"), lax.axis_size("blk")
    core = lax.axis_index("tensor")
    other = {"tensor": 1 - core}
    ours = pl.multiple_of(core * half, 16)
    theirs = pl.multiple_of((1 - core) * half, 16)
    start = blk * rows
    length = length_ref[0, 0]
    tile, tk = 256, 512

    loads = [
        pltpu.make_async_copy(hbm["own_in"], x.at[pl.ds(ours, half), :], load_sem.at[0]),
        pltpu.make_async_copy(hbm["own_cot"], m["cot"].at[pl.ds(ours, half), :], load_sem.at[1]),
        pltpu.make_async_copy(hbm["w_out"], w_out, load_sem.at[2]),
        pltpu.make_async_copy(hbm["gain1"], gain_rows, load_sem.at[3]),
        pltpu.make_async_copy(hbm["bias"], bias_rows, load_sem.at[4]),
    ] + weight_copies(hbm, dict(w_qkv=w_qkv, table=table), load_sem, 5, blk)
    for copy in loads:
        copy.start()
    meet([other] + [{"blk": lax.rem(blk + d, nb)} for d in range(1, nb)])

    def swap(k, src, dst):
        return remote(src, dst, pair_send.at[k], pair_recv.at[k], other)

    def x_swap():
        return swap(0, hbm["own_in"], x.at[pl.ds(ours, half), :])

    def cot_swap():
        return swap(1, hbm["own_cot"], m["cot"].at[pl.ds(ours, half), :])

    def ctx_swap():
        return swap(2, m["ctx"], ctx_o)

    def out_swap():
        return swap(3, hbm["w_out"], w_out_o)

    def save(name):
        i = FRONT_OUT.index(name)
        return pltpu.make_async_copy(m[name], out[name], out_sem.at[i])

    x_swap().start()
    cot_swap().start()
    out_swap().start()
    loads[0].wait()
    for copy in loads[2:]:
        copy.wait()
    nq = heads * HEAD
    gain[...] = row_of(gain_rows, width)
    bias[...] = row_of(bias_rows, nq + SLOT)
    lane = lax.broadcasted_iota(jnp.int32, (tile, SLOT), 1)

    def rows_in(first):
        def step(r, _):
            at = pl.ds(pl.multiple_of(first + r * tile, tile), tile)
            own = x[at, :].astype(f32)
            rho = lax.rsqrt(jnp.mean(own * own, axis=1, keepdims=True) + norm_eps)
            normed = (own * rho * gain[...]).astype(bf16)
            m["normed"][at, :] = normed
            factors = spread_table(table[at, :])
            proj = dot(normed, w_qkv[...], NT) + bias[...]
            zero = jnp.zeros((tile, HEAD), f32)
            for h in range(heads):
                cols = slice(h * SLOT, (h + 1) * SLOT)
                v = jnp.concatenate([proj[:, h * HEAD : (h + 1) * HEAD], zero], 1)
                v = turn(v, factors, 1.0).astype(bf16).astype(f32) * HEAD**-0.5
                m["q"][at, cols] = v.astype(bf16)
                q1[at, cols] = jnp.where(lane == HEAD, 1.0, v).astype(bf16)
            at_b = pl.ds(pl.multiple_of(start + first + r * tile, tile), tile)
            m["kv"][at_b, :] = turn(proj[:, nq:], factors, 1.0).astype(bf16)
            return 0

        lax.fori_loop(0, half // tile, step, 0)

    rows_in(ours)
    x_swap().wait()
    rows_in(theirs)

    def kv_copy(d):
        at = pl.ds(pl.multiple_of(blk * rows, rows), rows)
        return remote(
            m["kv"].at[at, :], m["kv"].at[at, :], kv_send.at[d - 1], kv_recv.at[d - 1],
            {"blk": lax.rem(blk + d, nb)},
        )

    for d in range(1, nb):
        @pl.when(blk + d < nb)
        def _(d=d):
            kv_copy(d).start()

    save("normed").start()
    save("q").start()
    wide_lane = lax.broadcasted_iota(jnp.int32, (tk, SLOT), 1)
    wide_row = lax.broadcasted_iota(jnp.int32, (tk, SLOT), 0)

    def prepare(first):
        at = pl.ds(pl.multiple_of(first, tk), tk)
        kv = m["kv"][at, :].astype(f32)
        dead = jnp.where(wide_row + first < length, 0.0, masked_value)
        k1[at, :] = jnp.where(
            wide_lane < HEAD, kv, jnp.where(wide_lane == HEAD, dead, 0.0)
        ).astype(bf16)
        vt1[0:HEAD, at] = jnp.transpose(kv)[HEAD:, :].astype(bf16)
        vt1[HEAD:, at] = jnp.ones((ONES - HEAD, tk), bf16)
        return at

    def attend(first, q0, diagonal):
        at = prepare(first)
        kt, vt = k1[at, :], vt1[:, at]
        n = rows - q0
        qs = slice(q0, rows)

        def score(h):
            s = dot(kt, q1[qs, h * SLOT : (h + 1) * SLOT], NT)
            if diagonal:
                ki = lax.broadcasted_iota(jnp.int32, (tk, n), 0)
                qi = lax.broadcasted_iota(jnp.int32, (tk, n), 1)
                s = jnp.where(ki <= qi, s, masked_value)
            return s

        def add(h, p, alpha):
            acc_s[h, :, qs] = acc_s[h, :, qs] * alpha + dot(vt, p, NN)

        ahead, behind = score(0), None
        for h in range(heads):
            s = ahead
            if h + 1 < heads:
                ahead = score(h + 1)
            m_prev = m_s[h : h + 1, qs]
            m_new = jnp.maximum(m_prev, jnp.max(s, axis=0, keepdims=True))
            alpha = jnp.exp(m_prev - m_new)
            p = jnp.exp(s - m_new).astype(bf16)
            m_s[h : h + 1, qs] = m_new
            if behind is not None:
                add(*behind)
            behind = (h, p, alpha)
        add(*behind)

    m_s[...] = jnp.full(m_s.shape, masked_value, f32)
    acc_s[...] = jnp.zeros(acc_s.shape, f32)
    for e in range(rows // tk):
        attend(start + e * tk, e * tk, True)

    def block(d, _):
        src = blk - d
        at = pl.ds(pl.multiple_of(src * rows, rows), rows)
        remote(
            m["kv"].at[at, :], m["kv"].at[at, :], kv_send.at[d - 1], kv_recv.at[d - 1],
            {"blk": src},
        ).wait_recv()

        def key_tile(i, _):
            attend(src * rows + i * tk, 0, False)
            return 0

        lax.fori_loop(0, rows // tk, key_tile, 0)
        return 0

    lax.fori_loop(1, blk + 1, block, 0)
    pos = lax.broadcasted_iota(jnp.int32, (1, rows), 1) + start
    zero = jnp.zeros((HEAD, rows), f32)
    for h in range(heads):
        acc = acc_s[h]
        total = acc[HEAD : HEAD + 1, :]
        ctx = jnp.transpose(jnp.concatenate([acc[:HEAD] / total, zero], 0))
        m["ctx"][:, h * HEAD : (h + 1) * HEAD] = ctx[:, :HEAD].astype(bf16)
        m["lse"][h : h + 1, :] = jnp.where(
            pos < length, m_s[h : h + 1, :] + jnp.log(total), -masked_value
        )
    m["lse"][heads:, :] = jnp.zeros((8 - heads, rows), f32)
    ctx_swap().start()
    save("ctx").start()
    save("lse").start()

    def kv_save(b):
        at = pl.ds(pl.multiple_of(b * rows, rows), rows)
        return pltpu.make_async_copy(
            m["kv"].at[at, :], out["kv"].at[at, :], out_sem.at[FRONT_OUT.index("kv")]
        )

    def keep_kv(b, _):
        kv_save(b).start()
        kv_save(b).wait()
        return 0

    loads[1].wait()
    cot_swap().wait()

    def mask(r, _):
        at = pl.ds(pl.multiple_of(r * tile, tile), tile)
        row = lax.broadcasted_iota(jnp.int32, (tile, width), 0) + start + r * tile
        m["cot"][at, :] = jnp.where(row < length, m["cot"][at, :].astype(f32), 0.0).astype(bf16)
        return 0

    lax.fori_loop(0, rows // tile, mask, 0)
    save("cot").start()
    lax.fori_loop(0, blk + 1, keep_kv, 0)
    for d in range(1, nb):
        @pl.when(blk + d < nb)
        def _(d=d):
            kv_copy(d).wait_send()

    out_swap().wait()
    ctx_swap().wait()

    def out_rows(r, _):
        at = pl.ds(pl.multiple_of(r * tile, tile), tile)
        m["resid"][at, :] = (
            x[at, :].astype(f32)
            + dot(m["ctx"][at, :], w_out[...], NN)
            + dot(ctx_o[at, :], w_out_o[...], NN)
        )
        pltpu.make_async_copy(
            m["resid"].at[at, :], out["resid"].at[at, :], out_sem.at[FRONT_OUT.index("resid")]
        ).start()
        return 0

    lax.fori_loop(0, rows // tile, out_rows, 0)
    for name in FRONT_OUT:
        if name != "kv":
            save(name).wait()


def front(length, values, heads, nb):
    half, width = values["own_in"].shape
    rows = 2 * half
    keys = rows * nb
    shape = jax.ShapeDtypeStruct
    outs = dict(
        cot=shape((rows, width), bf16),
        normed=shape((rows, width), bf16),
        q=shape((rows, heads * SLOT), bf16),
        kv=shape((keys, SLOT), bf16),
        ctx=shape((rows, heads * HEAD), bf16),
        lse=shape((8, rows), f32),
        resid=shape((rows, width), f32),
    )
    hbm = pl.BlockSpec(memory_space=pl.ANY)
    dma = pltpu.SemaphoreType.DMA
    vm = lambda a: pltpu.VMEM(a.shape, a.dtype)
    results = pl.pallas_call(
        functools.partial(front_kernel, heads),
        out_shape=[outs[name] for name in FRONT_OUT],
        in_specs=[pl.BlockSpec(memory_space=pltpu.SMEM)] + [hbm] * len(FRONT_IN),
        out_specs=[hbm] * len(FRONT_OUT),
        scratch_shapes=[vm(outs[name]) for name in FRONT_OUT]
        + [
            pltpu.VMEM((rows, width), bf16),
            pltpu.VMEM((rows, heads * HEAD), bf16),
            pltpu.VMEM((heads * HEAD + SLOT, width), bf16),
            vm(values["w_out"]),
            vm(values["w_out"]),
            pltpu.VMEM((1, width), f32),
            pltpu.VMEM((1, heads * HEAD + SLOT), f32),
            vm(values["gain1"]),
            vm(values["bias"]),
            pltpu.VMEM((rows, HEAD), f32),
            pltpu.VMEM((rows, heads * SLOT), bf16),
            pltpu.VMEM((keys, SLOT), bf16),
            pltpu.VMEM((ONES, keys), bf16),
            pltpu.VMEM((8, rows), f32),
            pltpu.VMEM((heads, ONES, rows), f32),
            dma((9,)),
            dma((len(FRONT_OUT),)),
            dma((4,)),
            dma((4,)),
            dma((nb - 1,)),
            dma((nb - 1,)),
        ],
        compiler_params=pltpu.CompilerParams(
            collective_id=1, has_side_effects=True, vmem_limit_bytes=58 * 2**20
        ),
        name="front",
    )(length, *[values[name] for name in FRONT_IN])
    return dict(zip(FRONT_OUT, results))


PART = 128
RING = 4
CHUNK = 3 * PART


class Stream:
    def __init__(self, first, count, axes):
        self.first, self.count = first, count
        self.reduce, self.sizes = [], []
        size = count
        for axis, bit in axes:
            if bit == "line":
                kinds = [("up", axis, 0), ("middle", axis, None), ("down", axis, 0)]
            elif size % 32 == 0 and size >= 64:
                kinds = [("half", axis, bit)]
                size //= 2
            else:
                kinds = [("full", axis, bit)]
            self.reduce += kinds
            self.sizes += [size] * len(kinds)
        self.gather = [(axis, bit) for kind, axis, bit in reversed(self.reduce) if kind == "half"]
        self.stages = len(self.reduce) + len(self.gather) + 1

    def scratch(self):
        copies = len(self.reduce) + len(self.gather)
        return [pltpu.VMEM((RING, self.sizes[0], CHUNK), bf16)] + [
            pltpu.VMEM((RING, size, CHUNK), bf16) for size in self.sizes
        ] + [
            pltpu.SemaphoreType.DMA((copies, RING)),
            pltpu.SemaphoreType.DMA((copies, RING)),
            pltpu.SemaphoreType.DMA((2, RING)),
        ]

    def bind(self, refs, sources, out):
        n = len(self.reduce)
        self.keep, self.got = refs[0], refs[1 : n + 1]
        self.send, self.recv, self.local = refs[n + 1 :]
        self.sources, self.out = sources, out
        self.peer, self.mine, offset = [], [], self.first
        self.sends, self.gets = [], []
        self.offsets = []
        for (kind, axis, bit), size in zip(self.reduce, self.sizes):
            at = lax.axis_index(axis)
            if kind == "middle":
                self.peer.append({axis: 3 - at})
            else:
                one = lax.rem(at // (1 << bit), 2)
                self.peer.append({axis: at + (1 - 2 * one) * (1 << bit)})
            middle = (at + 1) // 2 == 1
            self.middle = middle
            sends = {"up": jnp.logical_not(middle), "middle": middle, "down": middle}
            gets = {"up": middle, "middle": middle, "down": jnp.logical_not(middle)}
            self.sends.append(sends.get(kind))
            self.gets.append(gets.get(kind))
            self.mine.append(one if kind == "half" else 0)
            offset = offset + one * size if kind == "half" else offset
            self.offsets.append(offset)
        self.whole = []
        offset, size = self.offsets[-1], self.sizes[-1]
        self.gather_peer = []
        for k in reversed(range(n)):
            if self.reduce[k][0] == "half":
                self.whole.append((offset, size))
                self.gather_peer.append(self.peer[k])
                offset, size = offset - self.mine[k] * size, 2 * size

    def copy(self, k, ring, src, dst, peer):
        return pltpu.make_async_remote_copy(
            src_ref=src,
            dst_ref=dst,
            send_sem=self.send.at[k, ring],
            recv_sem=self.recv.at[k, ring],
            device_id=peer,
            device_id_type=pl.DeviceIdType.MESH,
        )

    def start_first(self, ring, source):
        size, one = self.sizes[0], self.mine[0]
        theirs = pl.multiple_of(self.first + (1 - one) * size, 16)
        own = pl.multiple_of(self.first + one * size, 16)
        self.copy(
            0, ring, source.at[pl.ds(theirs, size), :], self.got[0].at[ring], self.peer[0]
        ).start()
        pltpu.make_async_copy(
            source.at[pl.ds(own, size), :], self.keep.at[ring], self.local.at[0, ring]
        ).start()

    def reduce_copy(self, k, ring):
        if k == 0:
            src = self.keep.at[ring]
        elif self.reduce[k][0] == "half":
            size = self.sizes[k]
            theirs = pl.multiple_of((1 - self.mine[k]) * size, 16)
            src = self.got[k - 1].at[ring, pl.ds(theirs, size), :]
        else:
            src = self.got[k - 1].at[ring]
        return self.copy(k, ring, src, self.got[k].at[ring], self.peer[k])

    def gather_copy(self, t, ring, chunk):
        offset, size = self.whole[t]
        rows = pl.ds(pl.multiple_of(offset, 16), size)
        place = self.out.at[chunk, rows, :]
        src = self.got[-1].at[ring] if t == 0 else place
        return self.copy(len(self.reduce) + t, ring, src, place, self.gather_peer[t])

    def own_copy(self, ring, chunk):
        offset, size = self.whole[0]
        rows = pl.ds(pl.multiple_of(offset, 16), size)
        return pltpu.make_async_copy(
            self.got[-1].at[ring], self.out.at[chunk, rows, :], self.local.at[1, ring]
        )

    def stage(self, s, turn, chunk):
        ring = lax.rem(turn, RING)
        n = len(self.reduce)
        if s == 0:
            base = 0
            for count, place in self.sources:
                @pl.when((chunk >= base) & (chunk < base + count))
                def _(base=base, place=place):
                    self.start_first(ring, place(chunk - base))

                base += count
            return
        if s <= n:
            k = s - 1
            if k == 0:
                pltpu.make_async_copy(
                    self.got[0].at[ring], self.keep.at[ring], self.local.at[0, ring]
                ).wait()
            kind, size = self.reduce[k][0], self.sizes[k]
            copy = self.reduce_copy(k, ring)
            if kind in ("half", "full"):
                copy.wait()
                if k == 0:
                    own = self.keep[ring]
                elif kind == "half":
                    rows = pl.ds(pl.multiple_of(self.mine[k] * size, 16), size)
                    own = self.got[k - 1][ring, rows, :]
                else:
                    own = self.got[k - 1][ring]
                total = own.astype(f32) + self.got[k][ring].astype(f32)
                self.got[k][ring] = total.astype(bf16)
            else:
                pl.when(self.sends[k])(copy.wait_send)
                pl.when(self.gets[k])(copy.wait_recv)

                @pl.when(self.middle)
                def _():
                    if kind == "down":
                        self.got[k][ring] = self.got[k - 1][ring]
                    else:
                        total = self.got[k - 1][ring].astype(f32) + self.got[k][ring].astype(f32)
                        self.got[k][ring] = total.astype(bf16)

            if s < n:
                follow = self.reduce_copy(s, ring)
                if self.sends[s] is None:
                    follow.start()
                else:
                    pl.when(self.sends[s])(follow.start)
            else:
                self.own_copy(ring, chunk).start()
                self.gather_copy(0, ring, chunk).start()
            return
        t = s - n - 1
        self.gather_copy(t, ring, chunk).wait()
        if t == 0:
            self.own_copy(ring, chunk).wait()
        if t + 1 < len(self.gather):
            self.gather_copy(t + 1, ring, chunk).start()


def make_streams(width, plane, line):
    unit = width // 14
    short = [(line[0][0], "line")] if len(line) == 2 else line
    return [
        Stream(0, 5 * unit, plane + short),
        Stream(5 * unit, 5 * unit, plane[::-1] + short),
        Stream(10 * unit, 4 * unit, line + plane),
    ]


LOADS = ("resid", "cot", "gain1", "gain2", "w_out", "ctx", "q", "kv", "lse", "normed", "own_in")
FIRST = ("resid", "cot", "gain1", "gain2")
STREAMED = ("wq", "wk", "wv", "table", "w_gate", "w_up", "w_down")


def backward_kernel(heads, streams, n_ffn, n_small, *refs):
    nl, ns = len(LOADS), len(STREAMED)
    hbm = dict(zip(LOADS + STREAMED, refs[: nl + ns]))
    sums_ref, layer_out_ref, input_grad_ref, grads_ref = refs[nl + ns : nl + ns + 4]
    refs = list(refs[nl + ns + 4 :])
    m = dict(zip(LOADS, refs[:nl]))
    refs = refs[nl:]
    (
        load_sem, w_qkv, table_s, up_t, cot_t, wide, trio, acc, out_s, wgu, wd, made,
        w_sem, made_sem, dmid_o, part_o, dlow, delta, dkv, dkv_o, k0, small,
        din_o, rowsum, pair_send, pair_recv, kv_send, kv_recv, out_sem,
        gain_own, gain_o, dq_t, k_t, gain1, gain2,
    ) = refs[:35]
    refs = refs[35:]
    mlp = do = wide
    dmid_s = acc
    dproj = trio
    vec = acc.at[0:SLOT, :]
    din_own = dmid_o.at[0 : dmid_o.shape[0] // 2, :]
    to_send = wd
    rows, width = m["cot"].shape
    half = rows // 2
    blk, nb = lax.axis_index("blk"), lax.axis_size("blk")
    core = lax.axis_index("tensor")
    nz = lax.axis_size("batch")
    other = {"tensor": 1 - core}
    tile = 256
    nq = heads * HEAD
    qkv = nq + SLOT

    pos = 0
    for st in streams:
        cnt = len(st.scratch())
        st.bind(
            refs[pos : pos + cnt],
            [
                (1, lambda c: made.at[0, 0]),
                (n_ffn - 1, lambda c: grads_ref.at[1 + c]),
                (n_small, lambda c: small.at[c]),
            ],
            sums_ref,
        )
        pos += cnt

    loads = {
        name: pltpu.make_async_copy(hbm[name], m[name], load_sem.at[i])
        for i, name in enumerate(LOADS)
    }
    late = weight_copies(hbm, dict(w_qkv=w_qkv, table=table_s), load_sem, nl, blk)

    n_pairs = -(-n_ffn // 2)
    odd = n_ffn % 2 == 1
    wide2 = 2 * PART

    def weights(p, count):
        slot = lax.rem(p, 2)
        cols = pl.ds(pl.multiple_of(p * wide2, wide2), count)
        return [
            pltpu.make_async_copy(
                hbm["w_gate"].at[:, cols], wgu.at[slot, :, 0:count], w_sem.at[0, slot]
            ),
            pltpu.make_async_copy(
                hbm["w_up"].at[:, cols], wgu.at[slot, :, wide2 : wide2 + count], w_sem.at[1, slot]
            ),
            pltpu.make_async_copy(
                hbm["w_down"].at[cols, :],
                wd.at[pl.ds(pl.multiple_of(slot * wide2, wide2), count), :],
                w_sem.at[2, slot],
            ),
        ]

    def for_weights(p, act):
        last = n_pairs - 1 if odd else n_pairs

        @pl.when(p < last)
        def _():
            for copy in weights(p, wide2):
                act(copy)

        if odd:
            @pl.when(p == last)
            def _():
                for copy in weights(p, PART):
                    act(copy)

    for name in FIRST:
        loads[name].start()
    for_weights(0, lambda copy: copy.start())
    for_weights(1, lambda copy: copy.start())
    for name in LOADS:
        if name not in FIRST:
            loads[name].start()
    for copy in late:
        copy.start()

    batch = lax.axis_index("batch")
    meet(
        [other]
        + [{"blk": lax.rem(blk + d, nb)} for d in range(1, nb)]
        + [
            {"batch": batch + (1 - 2 * lax.rem(batch // (1 << b), 2)) * (1 << b)}
            for b in range(int(math.log2(nz)))
        ]
        + ([{"batch": 3 - batch}] if nz == 4 else [])
    )

    def swap(k, src, dst):
        return remote(src, dst, pair_send.at[k], pair_recv.at[k], other)

    def dmid_swap():
        return swap(0, dlow, dmid_o)

    theirs = pl.multiple_of((1 - core) * half, 16)
    ours = pl.multiple_of(core * half, 16)

    def part_swap():
        return swap(1, to_send, part_o)

    def din_swap():
        return swap(2, to_send, din_o)

    def gain_swap():
        return swap(3, gain_own, gain_o)

    def put(first, at, value):
        done, n = 0, value.shape[1]
        while done < n:
            c, lane = divmod(first + done, CHUNK)
            take = min(n - done, CHUNK - lane)
            small[c, at, lane : lane + take] = value[:, done : done + take].astype(bf16)
            done += take

    tq, tk = 256, 512

    def begin():
        for name in FIRST:
            loads[name].wait()
        gain1[...] = row_of(m["gain1"], width)
        gain2[...] = row_of(m["gain2"], width)

        def step(r, _):
            at = pl.ds(pl.multiple_of(r * tile, tile), tile)
            resid = m["resid"][at, :]
            rho = lax.rsqrt(jnp.mean(resid * resid, axis=1, keepdims=True) + norm_eps)
            normed = resid * rho * gain2[...]
            mlp[at, :] = normed.astype(bf16)
            up_t[:, at] = jnp.transpose(normed).astype(bf16)
            cot_t[:, at] = jnp.transpose(m["cot"][at, :].astype(f32)).astype(bf16)
            return 0

        lax.fori_loop(0, rows // tile, step, 0)
        dmid_s[...] = jnp.zeros(dmid_s.shape, f32)
        out_s[...] = jnp.zeros(out_s.shape, f32)

    def made_copy(p):
        slot = lax.rem(p, 2)
        return pltpu.make_async_copy(
            made.at[slot], grads_ref.at[pl.ds(p * 2, 2)], made_sem.at[slot]
        )

    def feed_forward(p):
        slot = lax.rem(p, 2)

        @pl.when(p >= 1)
        def _():
            made_copy(p - 1).wait()

        for_weights(p, lambda copy: copy.wait())
        if odd:
            @pl.when(p == n_pairs - 1)
            def _():
                wgu[slot, :, PART:wide2] = jnp.zeros((width, PART), bf16)
                wgu[slot, :, wide2 + PART :] = jnp.zeros((width, PART), bf16)
                rest = pl.ds(pl.multiple_of(slot * wide2 + PART, PART), PART)
                wd[rest, :] = jnp.zeros((PART, width), bf16)

        w_gu = wgu[slot]
        w_d = wd[pl.ds(pl.multiple_of(slot * wide2, wide2), wide2), :]
        for r in range(rows // tile):
            at = slice(r * tile, (r + 1) * tile)
            both = dot(mlp[at, :], w_gu, NN)
            gate, upper = both[:, :wide2], both[:, wide2:]
            d_hidden = dot(m["cot"][at, :], w_d, NT)
            sigma = 1.0 / (1.0 + jnp.exp(-gate))
            activ = gate * sigma
            hidden = (activ * upper).astype(bf16)
            d_gate = (d_hidden * upper * sigma * (1.0 + gate * (1.0 - sigma))).astype(bf16)
            d_up = (d_hidden * activ).astype(bf16)
            d_pair = jnp.concatenate([d_gate, d_up], 1)
            trio[at, :wide2] = hidden
            trio[at, wide2:] = d_pair
            out_s[at, :] += dot(hidden, w_d, NN)
            dmid_s[at, :] += dot(d_pair, w_gu, NT)
        for r in range(2):
            at = slice(r * width // 2, (r + 1) * width // 2)
            down = dot(cot_t[at, :], trio[:, :wide2], NN).astype(bf16)
            pairs = dot(up_t[at, :], trio[:, wide2:], NN).astype(bf16)
            for c in range(2):
                cols = slice(c * PART, (c + 1) * PART)
                made[slot, c, at, :PART] = down[:, cols]
                made[slot, c, at, PART : 2 * PART] = pairs[:, cols]
                made[slot, c, at, 2 * PART :] = pairs[:, wide2 + c * PART : wide2 + (c + 1) * PART]
        made_copy(p).start()
        for_weights(p + 2, lambda copy: copy.start())

    def hand_over():
        made_copy(n_pairs - 1).wait()

        def step(r, _):
            at = pl.ds(pl.multiple_of(r * tile, tile), tile)
            dlow[at, :] = dmid_s[at, :].astype(bf16)
            return 0

        lax.fori_loop(0, rows // tile, step, 0)
        dmid_swap().start()

        def step_part(r, _):
            at = pl.ds(pl.multiple_of(r * tile, tile), tile)
            src = pl.ds(pl.multiple_of(theirs + r * tile, tile), tile)
            to_send[at, :] = out_s[src, :].astype(bf16)
            return 0

        lax.fori_loop(0, half // tile, step_part, 0)
        part_swap().start()

    def before():
        for name in LOADS:
            if name not in FIRST + ("kv",):
                loads[name].wait()
        for copy in late:
            copy.wait()
        dmid_swap().wait()
        part_swap().wait()
        vec[...] = jnp.zeros(vec.shape, f32)

        def out_rows(r, _):
            at = pl.ds(pl.multiple_of(r * tile, tile), tile)
            mine = pl.ds(pl.multiple_of(ours + r * tile, tile), tile)
            part_o[at, :] = (
                m["resid"][mine, :] + out_s[mine, :] + part_o[at, :].astype(f32)
            ).astype(bf16)
            return 0

        lax.fori_loop(0, half // tile, out_rows, 0)
        pltpu.make_async_copy(part_o, layer_out_ref, out_sem.at[0]).start()

        head = lax.broadcasted_iota(jnp.int32, (8, nq), 0)
        column = lax.broadcasted_iota(jnp.int32, (8, nq), 1)
        inside = (column >= head * HEAD) & (column < (head + 1) * HEAD)
        of_head = jnp.where(inside, 1.0, 0.0).astype(bf16)

        def norm(r, _):
            at = pl.ds(pl.multiple_of(r * tile, tile), tile)
            dmid = dlow[at, :].astype(f32) + dmid_o[at, :].astype(f32)
            resid = m["resid"][at, :]
            rho = lax.rsqrt(jnp.mean(resid * resid, axis=1, keepdims=True) + norm_eps)
            n2 = resid * rho
            vec[1:2, :] += jnp.sum(dmid * n2, axis=0, keepdims=True)
            weighted = dmid * gain2[...]
            d_resid = m["cot"][at, :].astype(f32) + rho * (
                weighted - n2 * jnp.mean(weighted * n2, axis=1, keepdims=True)
            )
            m["resid"][at, :] = d_resid
            low = d_resid.astype(bf16)
            dlow[at, :] = low
            d_ctx = dot(low, m["w_out"][...], NT).astype(bf16).astype(f32)
            zero = jnp.zeros((tile, HEAD), f32)
            for h in range(heads):
                own = d_ctx[:, h * HEAD : (h + 1) * HEAD]
                do[at, h * SLOT : (h + 1) * SLOT] = jnp.concatenate([zero, own], 1).astype(bf16)
            rest = d_ctx * m["ctx"][at, :].astype(f32)
            total = jnp.zeros((8, tile), f32)
            for _ in range(3):
                term = rest.astype(bf16)
                total = total + dot(of_head, term, NT)
                rest = rest - term.astype(f32)
            delta[:, at] = total
            return 0

        lax.fori_loop(0, rows // tile, norm, 0)

    def keys_first():
        loads["kv"].wait()
        lane = lax.broadcasted_iota(jnp.int32, (tk, SLOT), 1)

        def keys(i, _):
            at = pl.ds(pl.multiple_of(i * tk, tk), tk)
            kv = m["kv"][at, :].astype(f32)
            k0[at, :] = jnp.where(lane < HEAD, kv, 0.0).astype(bf16)
            k_t[:, at] = jnp.transpose(kv)[:HEAD, :].astype(bf16)
            return 0

        lax.fori_loop(0, (blk + 1) * (rows // tk), keys, 0)
        dq_t[...] = jnp.zeros(dq_t.shape, f32)

    def grad_out():
        def step(k, _):
            at = pl.ds(pl.multiple_of(k * 128, 128), 128)
            put(0, at, dot(dlow[:, at], m["ctx"][...], TN))
            return 0

        lax.fori_loop(0, width // 128, step, 0)

    def pair(kt, kvt, kt_t, qt, masked):
        at = pl.ds(pl.multiple_of(qt * tq, tq), tq)

        def score(h):
            cols = slice(h * SLOT, (h + 1) * SLOT)
            return dot(kt, m["q"][at, cols], NT), dot(kvt, do[at, cols], NT)

        def add(h, p, ds):
            cols = slice(h * SLOT, (h + 1) * SLOT)
            dq_t[h, :, at] += dot(kt_t, ds, NN)
            return dot(
                jnp.concatenate([ds, p], 1),
                jnp.concatenate([m["q"][at, cols], do[at, cols]], 0),
                NN,
            )

        grad, ahead, behind = None, score(0), None
        for h in range(heads):
            s, dp = ahead
            if h + 1 < heads:
                ahead = score(h + 1)
            p = jnp.exp(s - m["lse"][h : h + 1, at])
            if masked is not None:
                p = jnp.where(masked, p, 0.0)
            ds = (p * (dp - delta[h : h + 1, at])).astype(bf16)
            if behind is not None:
                part = add(*behind)
                grad = part if grad is None else grad + part
            behind = (h, p.astype(bf16), ds)
        return grad + add(*behind)

    def own_tile(e):
        ki = lax.broadcasted_iota(jnp.int32, (tk, tq), 0)
        qi = lax.broadcasted_iota(jnp.int32, (tk, tq), 1)
        at_k = pl.ds(pl.multiple_of(blk * rows + e * tk, tk), tk)
        kt, kvt, kt_t = k0[at_k, :], m["kv"][at_k, :], k_t[:, at_k]
        first = e * (tk // tq)

        def near(j, grad):
            return grad + pair(kt, kvt, kt_t, first + j, ki <= qi + j * tq)

        def far(qt, grad):
            return grad + pair(kt, kvt, kt_t, qt, None)

        grad = lax.fori_loop(0, tk // tq, near, jnp.zeros((tk, SLOT), f32))
        grad = lax.fori_loop(first + tk // tq, rows // tq, far, grad)
        dkv[at_k, :] = grad.astype(bf16)

    def earlier(i):
        at_k = pl.ds(pl.multiple_of(i * tk, tk), tk)
        kt, kvt, kt_t = k0[at_k, :], m["kv"][at_k, :], k_t[:, at_k]

        def step(qt, grad):
            return grad + pair(kt, kvt, kt_t, qt, None)

        grad = lax.fori_loop(0, rows // tq, step, jnp.zeros((tk, SLOT), f32))
        dkv[at_k, :] = grad.astype(bf16)

    def kv_copy(d):
        to = lax.rem(blk + d, nb)
        at = pl.ds(pl.multiple_of(to * rows, rows), rows)
        return remote(
            dkv.at[at, :], dkv_o.at[d - 1], kv_send.at[d - 1], kv_recv.at[d - 1], {"blk": to}
        )

    def kv_start():
        for d in range(1, nb):
            @pl.when(lax.rem(blk + d, nb) < blk)
            def _(d=d):
                kv_copy(d).start()

    def project_queries():
        def step(r, _):
            at = pl.ds(pl.multiple_of(r * tile, tile), tile)
            table = spread_table(table_s[at, :])
            zero = jnp.zeros((HEAD, tile), f32)
            for h in range(heads):
                v = jnp.transpose(jnp.concatenate([dq_t[h, :, at], zero], 0))
                v = turn(v * HEAD**-0.5, table, -1.0)
                dproj[at, h * HEAD : (h + 1) * HEAD] = v[:, :HEAD].astype(bf16)
            return 0

        lax.fori_loop(0, rows // tile, step, 0)

    def project():
        for d in range(1, nb):
            @pl.when(lax.rem(blk + d, nb) < blk)
            def _(d=d):
                kv_copy(d).wait_send()

            @pl.when(lax.rem(blk + nb - d, nb) > blk)
            def _(d=d):
                kv_copy(d).wait_recv()
                for r in range(rows // tile):
                    at = pl.ds(pl.multiple_of(blk * rows + r * tile, tile), tile)
                    total = dkv[at, :].astype(f32) + dkv_o[d - 1, r * tile : (r + 1) * tile].astype(f32)
                    dkv[at, :] = total.astype(bf16)

        rowsum[...] = jnp.zeros(rowsum.shape, f32)

        def unrotate(r, _):
            at = pl.ds(pl.multiple_of(r * tile, tile), tile)
            at_b = pl.ds(pl.multiple_of(blk * rows + r * tile, tile), tile)
            table = spread_table(table_s[at, :])
            dproj[at, nq:qkv] = turn(dkv[at_b, :].astype(f32), table, -1.0).astype(bf16)
            rowsum[0:1, :] += jnp.sum(dproj[at, :qkv].astype(f32), axis=0, keepdims=True)
            return 0

        lax.fori_loop(0, rows // tile, unrotate, 0)

        def d_in(to, first):
            def step(r, _):
                src = pl.ds(pl.multiple_of(first + r * tile, tile), tile)
                at = pl.ds(pl.multiple_of(r * tile, tile), tile)
                to[at, :] = dot(dproj[src, :qkv], w_qkv[...], NN).astype(bf16)
                return 0

            lax.fori_loop(0, half // tile, step, 0)

        d_in(to_send, theirs)
        din_swap().start()
        d_in(din_own, ours)

        def grads(k, _):
            at = pl.ds(pl.multiple_of(k * 128, 128), 128)
            put(nq, at, dot(m["normed"][:, at], dproj[:, :qkv], TN))
            return 0

        lax.fori_loop(0, width // 128, grads, 0)

    def finish():
        din_swap().wait()

        def step(r, _):
            at = pl.ds(pl.multiple_of(r * tile, tile), tile)
            mine = pl.ds(pl.multiple_of(ours + r * tile, tile), tile)
            d_in = din_own[at, :].astype(f32) + din_o[at, :].astype(f32)
            x = m["own_in"][at, :].astype(f32)
            rho = lax.rsqrt(jnp.mean(x * x, axis=1, keepdims=True) + norm_eps)
            n1 = x * rho
            vec[0:1, :] += jnp.sum(d_in * n1, axis=0, keepdims=True)
            weighted = d_in * gain1[...]
            grad = m["resid"][mine, :] + rho * (
                weighted - n1 * jnp.mean(weighted * n1, axis=1, keepdims=True)
            )
            din_own[at, :] = grad.astype(bf16)
            return 0

        lax.fori_loop(0, half // tile, step, 0)
        pltpu.make_async_copy(din_own, input_grad_ref, out_sem.at[1]).start()
        gain_own[...] = vec[0:8, :]
        gain_swap().start()
        vec[2:3, : nq + SLOT] = rowsum[0:1, :]
        gain_swap().wait()
        vec[0:1, :] = gain_own[0:1, :] + gain_o[0:1, :]
        put(2 * nq + SLOT, slice(None), jnp.transpose(vec[...]))

    plan = slots_of(n_ffn, rows // tk, nb)

    def compute(i):
        pl.when(i == 0)(begin)
        few = plan["singles"]
        count = jnp.where(i < few, 1, jnp.where(i < plan["before"], 2, 0))
        first = jnp.where(i < few, i, 2 * i - few)
        count = jnp.minimum(count, jnp.maximum(n_pairs - first, 0))

        def step(c, _):
            feed_forward(first + c)
            return 0

        lax.fori_loop(0, count, step, 0)
        pl.when(i == max(plan["before"] - 3, 0))(keys_first)
        pl.when(i == plan["before"] - 1)(hand_over)
        pl.when(i == plan["before"])(before)

        @pl.when((i >= plan["own"]) & (i < plan["own"] + rows // tk))
        def _():
            own_tile(i - plan["own"])

        pl.when(i == plan["early"] - 1)(grad_out)

        @pl.when((i >= plan["early"]) & (i - plan["early"] < blk * (rows // tk)))
        def _():
            earlier(i - plan["early"])

        pl.when(i == plan["queries"] - 1)(kv_start)
        pl.when(i == plan["queries"])(project_queries)
        pl.when(i == plan["queries"] + 1)(project)
        pl.when(i == plan["queries"] + 2)(finish)

    early_turn = min(plan["early"] - 1, n_ffn)
    gap = max(0, plan["queries"] + 2 - n_ffn - n_small + 1)
    n = n_ffn + n_small + gap
    depth = max(st.stages for st in streams)

    def chunk_of(t):
        late = jnp.where(t <= n_ffn, t - 1, t - gap)
        return jnp.where(t < early_turn, t, jnp.where(t == early_turn, n_ffn, late))

    def slot(i, _):
        compute(i)
        for st in streams[::-1]:
            for s in reversed(range(st.stages)):
                t = i - s
                real = (t >= 0) & (t < n)
                if gap:
                    real = real & ((t <= n_ffn) | (t > n_ffn + gap))

                @pl.when(real)
                def _(st=st, s=s, t=t):
                    st.stage(s, t, chunk_of(t))

        return 0

    lax.fori_loop(0, n + depth - 1, slot, 0)
    pltpu.make_async_copy(part_o, layer_out_ref, out_sem.at[0]).wait()
    pltpu.make_async_copy(din_own, input_grad_ref, out_sem.at[1]).wait()


def slots_of(n_ffn, tiles, nb):
    pairs = -(-n_ffn // 2)
    singles = pairs
    before = singles + -(-(pairs - singles) // 2)
    own = before + 1
    early = own + tiles
    return dict(
        singles=singles, before=before, own=own, early=early, queries=early + (nb - 1) * tiles
    )


def backward(values, heads, plane, line, nb):
    rows, width = values["cot"].shape
    half = rows // 2
    keys = values["kv"].shape[0]
    n_ffn = values["w_gate"].shape[1] // PART
    n_small = -(-(2 * heads * HEAD + 2 * SLOT) // CHUNK)
    streams = make_streams(width, plane, line)
    hbm = pl.BlockSpec(memory_space=pl.ANY)
    dma = pltpu.SemaphoreType.DMA
    vm = pltpu.VMEM
    assert half == 4 * PART and heads * SLOT == width
    scratch = [vm(values[name].shape, values[name].dtype) for name in LOADS]
    scratch += [
        dma((len(LOADS) + 4,)),
        vm((heads * HEAD + SLOT, width), bf16),
        vm((rows, HEAD), f32),
        vm((width, rows), bf16),
        vm((width, rows), bf16),
        vm((rows, width), bf16),
        vm((rows, 2 * CHUNK), bf16),
        vm((rows, width), f32),
        vm((rows, width), f32),
        vm((2, width, 4 * PART), bf16),
        vm((4 * PART, width), bf16),
        vm((2, 2, width, CHUNK), bf16),
        dma((3, 2)),
        dma((2,)),
        vm((rows, width), bf16),
        vm((half, width), bf16),
        vm((rows, width), bf16),
        vm((8, rows), f32),
        vm((keys, SLOT), bf16),
        vm((nb - 1, rows, SLOT), bf16),
        vm((keys, SLOT), bf16),
        vm((n_small, width, CHUNK), bf16),
        vm((half, width), bf16),
        vm((8, heads * HEAD + SLOT), f32),
        dma((4,)),
        dma((4,)),
        dma((nb - 1,)),
        dma((nb - 1,)),
        dma((2,)),
        vm((8, width), f32),
        vm((8, width), f32),
        vm((heads, HEAD, rows), f32),
        vm((HEAD, keys), bf16),
        vm((1, width), f32),
        vm((1, width), f32),
    ]
    for st in streams:
        scratch += st.scratch()
    return pl.pallas_call(
        functools.partial(backward_kernel, heads, streams, n_ffn, n_small),
        out_shape=(
            jax.ShapeDtypeStruct((n_ffn + n_small, width, CHUNK), bf16),
            jax.ShapeDtypeStruct((half, width), bf16),
            jax.ShapeDtypeStruct((half, width), bf16),
            jax.ShapeDtypeStruct((n_ffn + n_ffn % 2, width, CHUNK), bf16),
        ),
        in_specs=[hbm] * (len(LOADS) + len(STREAMED)),
        out_specs=(hbm, hbm, hbm, hbm),
        scratch_shapes=scratch,
        compiler_params=pltpu.CompilerParams(
            collective_id=0, has_side_effects=True, vmem_limit_bytes=60 * 2**20
        ),
        name="backward",
    )(*[values[name] for name in LOADS + STREAMED])


def unpack_kernel(heads, n_small, chunk_ref, *refs):
    small = refs[:n_small]
    rows_in, refs = refs[n_small : n_small + 2], refs[n_small + 2 :]
    rows_out, refs = refs[-2:], refs[:-2]
    for src, dst in zip(rows_in, rows_out):
        dst[...] = src[...]
    down, gate, up, g_out, g_q, g_k, g_v, gain1, gain2, bias = refs
    step = pl.program_id(0)
    for c in range(2):
        value, at = chunk_ref[c], slice(c * PART, (c + 1) * PART)
        down[at, :] = jnp.transpose(value[:, :PART].astype(f32))
        gate[:, at] = value[:, PART : 2 * PART].astype(f32)
        up[:, at] = value[:, 2 * PART :].astype(f32)

    def take(first, count):
        done = 0
        while done < count:
            c, lane = divmod(first + done, CHUNK)
            n = min(count - done, SLOT - lane % SLOT)
            yield done, n, small[c][0, :, lane : lane + n].astype(f32)
            done += n

    @pl.when(step == 0)
    def _():
        nq = heads * HEAD
        for done, n, piece in take(0, nq):
            g_out[done : done + n, :] = jnp.transpose(piece)
        for done, n, piece in take(nq, nq):
            g_q[done : done + n, :] = jnp.transpose(piece)
        for done, n, piece in take(2 * nq, HEAD):
            g_k[...] = jnp.transpose(piece)
        for done, n, piece in take(2 * nq + HEAD, HEAD):
            g_v[...] = jnp.transpose(piece)
        for done, n, piece in take(2 * nq + 2 * HEAD, SLOT):
            vec = jnp.transpose(piece)
            for row, to in ((0, gain1), (1, gain2), (2, bias)):
                for i in range(to.shape[0]):
                    to[i : i + 1, :] = vec[row : row + 1, i * 128 : (i + 1) * 128]


def unpack(sums, layer_out, input_grad, n_ffn, heads):
    n, width, _ = sums.shape
    n_small = n - n_ffn
    shape = lambda *dims: jax.ShapeDtypeStruct(dims, f32)
    nq = heads * HEAD
    lanes = [(width // 128, 128), (width // 128, 128), (-(-(nq + SLOT) // 128), 128)]
    whole = [(nq, width), (nq, width), (HEAD, width), (HEAD, width)] + lanes
    half = layer_out.shape[0]
    steps = -(-n_ffn // 2)
    cut = max(c for c in (1, 2, 4, 8) if c <= steps)
    rows = pl.BlockSpec((half // cut, width), lambda j: (jnp.minimum(j, cut - 1), 0))
    return pl.pallas_call(
        functools.partial(unpack_kernel, heads, n_small),
        grid=(-(-n_ffn // 2),),
        out_shape=[
            shape(n_ffn * PART, width), shape(width, n_ffn * PART), shape(width, n_ffn * PART)
        ] + [shape(*dims) for dims in whole] + [
            jax.ShapeDtypeStruct((half, width), bf16)
        ] * 2,
        in_specs=[pl.BlockSpec((2, width, CHUNK), lambda j: (j, 0, 0))]
        + [
            pl.BlockSpec((1, width, CHUNK), lambda j, c=c: (n_ffn + c, 0, 0))
            for c in range(n_small)
        ] + [rows, rows],
        out_specs=[
            pl.BlockSpec((2 * PART, width), lambda j: (j, 0)),
            pl.BlockSpec((width, 2 * PART), lambda j: (0, j)),
            pl.BlockSpec((width, 2 * PART), lambda j: (0, j)),
        ] + [pl.BlockSpec(dims, lambda j: (0, 0)) for dims in whole] + [rows, rows],
        compiler_params=pltpu.CompilerParams(
            vmem_limit_bytes=48 * 2**20, dimension_semantics=("arbitrary",)
        ),
        name="unpack",
    )(*[sums] * (1 + n_small), layer_out, input_grad)


def shards(
    layer_in, cotangent, lengths, attn_gain, w_query, query_bias, w_key, key_bias, w_value,
    value_bias, w_out, mlp_gain, w_gate, w_up, w_down,
):
    half, width = layer_in.shape
    rows = half * lax.axis_size("tensor")
    nb = lax.axis_size("blk")
    heads = w_query.shape[1] // HEAD
    biases = jnp.concatenate([query_bias, key_bias, value_bias]).astype(f32)
    biases = jnp.pad(biases, (0, -biases.shape[0] % 128)).reshape(-1, 128)
    values = dict(
        own_in=layer_in, own_cot=cotangent, wq=w_query.T, wk=w_key.T, wv=w_value.T, w_out=w_out,
        gain1=attn_gain.reshape(-1, 128), gain2=mlp_gain.reshape(-1, 128), bias=biases,
        table=jnp.asarray(rotary_table(rows * nb)), w_gate=w_gate, w_up=w_up, w_down=w_down,
    )
    values |= front(lengths, values, heads, nb)
    sums, layer_out, input_grad, _ = backward(
        values, heads, bits_of("blk"), bits_of("batch"), nb
    )
    (
        g_down, g_gate, g_up, g_out, g_query, g_key, g_value, g_gain1, g_gain2, g_bias,
        layer_out, input_grad,
    ) = unpack(sums, layer_out, input_grad, w_gate.shape[1] // PART, heads)
    nq = heads * HEAD
    g_bias = g_bias.reshape(-1)
    return (
        layer_out, input_grad, g_gain1.reshape(-1), g_query.T, g_bias[:nq], g_key.T,
        g_bias[nq : nq + HEAD], g_value.T, g_bias[nq + HEAD : nq + 2 * HEAD], g_out,
        g_gain2.reshape(-1), g_gate, g_up, g_down,
    )


def solution(mesh):
    rows = P(("batch", "blk", "tensor"), None)
    cols, part, split = P(None, "tensor"), P("tensor"), P("tensor", None)
    return jax.shard_map(
        shards,
        mesh=mesh,
        in_specs=(
            rows, rows, P("batch", None), P(), cols, part, cols, part, cols, part, split, P(),
            cols, cols, split,
        ),
        out_specs=(
            rows, rows, P(), cols, part, cols, part, cols, part, split, P(), cols, cols, split,
        ),
        check_vma=False,
    )
```
